128 devices in a mesh: pair: 32 (over x, z, y_hi), win: 4 (over y_lo, core).
Axes of the slice: x: 4, y: 4 (y_hi: 2, y_lo: 2; y = y_hi * 2 + y_lo), z: 4, core: 2. Of those that a mesh axis runs over, the one named last changes fastest.
Arguments:
- spectra: bfloat16 [32, 2, 384, 8192], P(None, None, 'win', 'pair'), may hold values from -6 to 6
- channel_order: int32 [32, 256], P('pair'), may hold values from 0 to 255, each once within a row
- partners: int32 [4, 32], replicated, may hold values from 0 to 31, as said below
Outputs:
- stacks: float32 [32, 256, 4, 16, 256], P('pair', 'win')
The draws below stay inside these ranges and needn't reach their ends.
Inputs may be any that keep to these rules, and one draw needn't show every extreme that they name: For every round r and block b, partners[r, b] differs from b and partners[r, partners[r, b]] = b; no two rounds match the same two blocks. `channel_order`: each row lists every slot once.
All inputs are finite; a program needn't handle non-finite values.
Results may differ from the reference program's by a relative error of at most 0.004.
Values may be sent and summed in bfloat16 or wider, within the bound.
No kernel may reach another device: no remote copies, remote signals or barrier semaphores. Data moves between devices by JAX's collectives and lax.ppermute only.
A program may use at most 128 MiB of HBM per device.

```python
import math
import jax
import jax.numpy as jnp
from jax import lax

CH = 256
NF = 32
LAGS = 16
ROUNDS = 4
BLOCKS = 32
WINDOWS = 384
CHANNELS = 8192


def draw_partners(key, part):
    key = jax.random.fold_in(key, 11)
    key_pick, key_label = jax.random.split(key)
    fixed_block = BLOCKS - 1
    chosen = jax.random.permutation(key_pick, fixed_block)[:ROUNDS].astype(jnp.int32)
    relabel = jax.random.permutation(key_label, BLOCKS).astype(jnp.int32)
    block_ids = jnp.arange(BLOCKS, dtype=jnp.int32)[None, :]
    chosen_col = chosen[:, None]
    circle_mate = jnp.where(block_ids == fixed_block, chosen_col, jnp.where(block_ids == chosen_col, fixed_block, (2 * chosen_col - block_ids) % fixed_block))
    result = jnp.zeros((ROUNDS, BLOCKS), jnp.int32)
    return result.at[:, relabel].set(relabel[circle_mate])


def steps_of(key, extent, pieces, least, top_value):
    factor_of = 1.0
    for dim, parts in pieces:
        heights = jax.random.uniform(jax.random.fold_in(jax.random.fold_in(key, 6), dim), (parts,), jnp.float32, least / len(pieces), top_value / len(pieces))
        factor_of = factor_of * jnp.repeat(jnp.exp(heights), extent[dim] // parts).reshape((-1,) + (1,) * (len(extent) - 1 - dim))
    return factor_of


def noise(stream_key, shape, spread, reach, cuts=(), held_as=jnp.bfloat16):
    array = jax.random.normal(stream_key, shape, jnp.float32) * spread
    if len(cuts) > 0:
        array = steps_of(stream_key, shape, cuts, -0.22, 0.18) * array
    return jnp.clip(array, min=-reach, max=reach).astype(held_as)


def setup_inputs(seed: int = 0) -> dict:
    keys = jax.random.split(jax.random.key(seed), 4)
    return {
        "spectra": noise(keys[0], (NF, 2, WINDOWS, CHANNELS), 1.0, 6.0, ((2, 4), (3, 32))),
        "channel_order": jax.vmap(lambda own: jax.random.permutation(own, CH))(jax.random.split(keys[1], BLOCKS)).reshape((BLOCKS, CH)).astype(jnp.int32),
        "partners": draw_partners(jax.random.fold_in(keys[3], 71), 0),
    }


def whiten(spectra):
    values = spectra.astype(jnp.float32)
    band_power = values[:, 0] * values[:, 0] + values[:, 1] * values[:, 1]
    num_bins = band_power.shape[0]
    padded = jnp.pad(band_power, ((2, 2), (0, 0), (0, 0)))
    band_total = padded[0:num_bins] + padded[1:num_bins + 1] + padded[2:num_bins + 2] + padded[3:num_bins + 3] + padded[4:num_bins + 4]
    bin_index = jnp.arange(num_bins, dtype=jnp.int32)
    counts = (jnp.minimum(bin_index + 2, num_bins - 1) - jnp.maximum(bin_index - 2, 0) + 1).astype(jnp.float32)
    band_mean = band_total / counts[:, None, None]
    inv_scale = 1.0 / jnp.maximum(jnp.sqrt(band_mean), 0.5)
    return (values * inv_scale[:, None]).astype(jnp.bfloat16)

def make_table(num_bins, num_lags, window_total):
    bin_freq = jnp.arange(num_bins, dtype=jnp.float32)[:, None]
    lag_index = (jnp.arange(num_lags, dtype=jnp.int32) - num_lags // 2).astype(jnp.float32)[None, :]
    phase_angle = math.pi * bin_freq * lag_index / num_bins
    norm_factor = 1.0 / math.sqrt(window_total * num_bins)
    return jnp.concatenate([jnp.cos(phase_angle), -jnp.sin(phase_angle)], 0) * norm_factor

def correlate(own_block, mate_block, lag_table):
    num_bins, _, num_windows, num_cols = own_block.shape
    left_rows = own_block.astype(jnp.float32).reshape(num_bins, 2 * num_windows, num_cols)
    mate_float = mate_block.astype(jnp.float32)
    right_real = mate_float.reshape(num_bins, 2 * num_windows, num_cols)
    right_turned = jnp.concatenate([mate_float[:, 1], -mate_float[:, 0]], axis=1)
    cross_real = jnp.einsum('fki,fkj->fij', left_rows, right_real, precision=lax.Precision.HIGHEST)
    cross_imag = jnp.einsum('fki,fkj->fij', left_rows, right_turned, precision=lax.Precision.HIGHEST)
    stacked = jnp.concatenate([cross_real, cross_imag], 0)
    return jnp.einsum('gl,gij->ilj', lag_table, stacked, precision=lax.Precision.HIGHEST)

def reference(spectra, channel_order, partners):
    whitened = whiten(spectra)
    blocks = whitened.reshape(NF, 2, WINDOWS, BLOCKS, CH)
    blocks = jnp.moveaxis(blocks, 3, 0)
    blocks = jax.vmap(lambda block_data, order_row: jnp.take(block_data, order_row, axis=3))(blocks, channel_order)
    lag_table = make_table(NF, LAGS, WINDOWS)

    def one_block(block_id):
        own_block = lax.dynamic_index_in_dim(blocks, block_id, 0, keepdims=False)
        results = []
        for turn_index in range(ROUNDS):
            mate_id = partners[turn_index, block_id].astype(jnp.int32)
            mate_block = lax.dynamic_index_in_dim(blocks, mate_id, 0, keepdims=False)
            results.append(correlate(own_block, mate_block, lag_table))
        return jnp.stack(results, 1)
    return lax.map(one_block, jnp.arange(BLOCKS, dtype=jnp.int32))
```

```python
import functools
import math

import jax
import jax.numpy as jnp
from jax import lax
from jax.experimental import pallas as pl
from jax.experimental.pallas import tpu as pltpu
from jax.sharding import PartitionSpec as P

LAGS = 16
ROUNDS = 4
VMEM_BYTES = 56 * 1024 * 1024
QUARTER_ORDER = (0, 2, 1, 3)
bf16 = jnp.bfloat16
f32 = jnp.float32


def params(**more):
    return pltpu.CompilerParams(vmem_limit_bytes=VMEM_BYTES, **more)


def whiten_kernel(order_ref, spectra_ref, out_ref):
    num_bins, _, rows, cols = spectra_ref.shape
    slots = lax.broadcasted_iota(jnp.int32, (cols, cols), 0)
    pick = (slots == order_ref[...]).astype(f32).astype(bf16)
    values = spectra_ref[...].astype(f32)
    power = values[:, 0] * values[:, 0] + values[:, 1] * values[:, 1]
    parts = []
    for f in range(num_bins):
        lo, hi = max(f - 2, 0), min(f + 2, num_bins - 1)
        total = power[lo]
        for g in range(lo + 1, hi + 1):
            total = total + power[g]
        inv_scale = jnp.minimum(lax.rsqrt(total * (1.0 / (hi - lo + 1))), 2.0)
        parts.append((values[f] * inv_scale[None]).astype(bf16).reshape(2 * rows, cols))
    flat = jnp.concatenate(parts, 0)
    ordered = jnp.dot(flat, pick, preferred_element_type=f32).astype(bf16)
    out_ref[...] = ordered.reshape(num_bins, 2, rows, cols)


def whiten(spectra, channel_order):
    num_bins, _, num_windows, cols = spectra.shape
    rows = 16
    return pl.pallas_call(
        whiten_kernel,
        grid=(num_windows // rows,),
        out_shape=jax.ShapeDtypeStruct(spectra.shape, bf16),
        in_specs=[
            pl.BlockSpec((1, cols), lambda s: (0, 0)),
            pl.BlockSpec((num_bins, 2, rows, cols), lambda s: (0, 0, s, 0)),
        ],
        out_specs=pl.BlockSpec((num_bins, 2, rows, cols), lambda s: (0, 0, s, 0)),
        compiler_params=params(),
        name="whiten",
    )(channel_order, spectra)


def turn_kernel(own_ref, out_ref):
    bins, depth, cols = own_ref.shape
    half = depth // 2
    quarter = cols // 4
    for f in range(bins):
        block = own_ref[f].astype(f32)
        plain = block.T.astype(bf16)
        turned = jnp.concatenate([-block[half:], block[:half]], 0).T.astype(bf16)
        for place, source in enumerate(QUARTER_ORDER):
            rows = slice(source * quarter, (source + 1) * quarter)
            out_ref[f, place * quarter : (place + 1) * quarter, :] = plain[rows]
            out_ref[f, cols + place * quarter : cols + (place + 1) * quarter, :] = turned[rows]


def turn(own_rows):
    num_bins, depth, cols = own_rows.shape
    bins = 4
    return pl.pallas_call(
        turn_kernel,
        grid=(num_bins // bins,),
        out_shape=jax.ShapeDtypeStruct((num_bins, 2 * cols, depth), bf16),
        in_specs=[pl.BlockSpec((bins, depth, cols), lambda s: (s, 0, 0))],
        out_specs=pl.BlockSpec((bins, 2 * cols, depth), lambda s: (s, 0, 0)),
        compiler_params=params(),
        cost_estimate=pl.CostEstimate(flops=0, bytes_accessed=12_000_000, transcendentals=0),
        name="turn",
    )(own_rows)


def gather_kernel(index_ref, source_ref, out_ref, sems):
    count = out_ref.shape[0]
    copies = []
    for place in range(count):
        copy = pltpu.make_async_copy(
            source_ref.at[index_ref[place]], out_ref.at[place], sems.at[place]
        )
        copy.start()
        copies.append(copy)
    for copy in copies:
        copy.wait()


def gather(source, index):
    return pl.pallas_call(
        gather_kernel,
        out_shape=jax.ShapeDtypeStruct((index.shape[0],) + source.shape[1:], source.dtype),
        in_specs=[pl.BlockSpec(memory_space=pltpu.SMEM), pl.BlockSpec(memory_space=pl.ANY)],
        out_specs=pl.BlockSpec(memory_space=pl.ANY),
        scratch_shapes=[pltpu.SemaphoreType.DMA((index.shape[0],))],
        compiler_params=pltpu.CompilerParams(),
        name="gather",
    )(index, source)


def weighted(terms):
    total = None
    for weight, value in terms:
        if abs(weight) < 1e-12:
            continue
        term = value * weight
        total = term if total is None else total + term
    return total


def lag_sums(real, imag, norm):
    cosine = lambda f, t: math.cos(math.pi * f * t / 32) * norm
    sine = lambda f, t: -math.sin(math.pi * f * t / 32) * norm
    even, odd = {}, {}
    low = {0: real(0), 16: real(16)}
    diff = {0: low[0]}
    for f in range(1, 16):
        a, b = real(f), real(32 - f)
        low[f], diff[f] = a + b, a - b
    for t in (1, 3, 5, 7):
        even[t] = weighted([(cosine(f, t), diff[f]) for f in range(16)])
    minus = {f: low[f] - low[16 - f] for f in range(8)}
    for t in (2, 6):
        even[t] = weighted([(cosine(f, t), minus[f]) for f in range(8)])
    plus = {f: low[f] + low[16 - f] for f in range(8)}
    plus[8] = low[8]
    even[4] = weighted([(cosine(f, 4), plus[f] - plus[8 - f]) for f in range(4)])
    sums = {f: plus[f] + plus[8 - f] for f in range(4)}
    sums[4] = plus[4]
    even[8] = weighted([(cosine(f, 8), sums[f]) for f in range(5)])
    total = sums[0]
    for f in range(1, 5):
        total = total + sums[f]
    even[0] = total * norm

    add = {16: imag(16)}
    sub = {}
    for f in range(1, 16):
        a, b = imag(f), imag(32 - f)
        add[f], sub[f] = a + b, a - b
    for t in (1, 3, 5, 7):
        odd[t] = weighted([(sine(f, t), add[f]) for f in range(1, 17)])
    sums = {f: sub[f] + sub[16 - f] for f in range(1, 8)}
    sums[8] = sub[8]
    for t in (2, 6):
        odd[t] = weighted([(sine(f, t), sums[f]) for f in range(1, 9)])
    minus = {f: sub[f] - sub[16 - f] for f in range(1, 8)}
    odd[4] = weighted(
        [(sine(f, 4), minus[f] + minus[8 - f]) for f in range(1, 4)] + [(sine(4, 4), minus[4])]
    )
    odd[8] = weighted([(sine(f, 8), minus[f] - minus[8 - f]) for f in range(1, 4)])
    return even, odd


def correlate_kernel(norm, core_ref, own_ref, mate_ref, keep_ref, send_ref, cross):
    step = pl.program_id(0)
    bins = own_ref.shape[0]
    for f in range(bins):
        cross[step * bins + f] = jnp.dot(own_ref[f], mate_ref[f], preferred_element_type=f32)

    @pl.when(step == pl.num_programs(0) - 1)
    def _():
        lags, half, cols = keep_ref.shape
        core = core_ref[0]
        rows, lanes = 16, 128

        def part(out_ref, base):
            def body(chunk, carry):
                row = pl.multiple_of(chunk * rows, rows)
                for lane in range(0, cols, lanes):
                    where = pl.ds(pl.multiple_of(base + row, rows), rows)
                    turned = pl.ds(pl.multiple_of(2 * half + base + row, rows), rows)
                    even, odd = lag_sums(
                        lambda f: cross[f, where, lane : lane + lanes],
                        lambda f: cross[f, turned, lane : lane + lanes],
                        norm,
                    )
                    for lag in range(lags):
                        t = lag - LAGS // 2
                        if t == 0:
                            value = even[0]
                        elif t > 0:
                            value = even[t] + odd[t]
                        else:
                            value = even[-t] - odd[-t]
                        out_ref[lag, pl.ds(row, rows), lane : lane + lanes] = value.astype(
                            out_ref.dtype
                        )
                return carry

            lax.fori_loop(0, half // rows, body, 0)

        part(keep_ref, core * half)
        part(send_ref, (1 - core) * half)


def correlate(own_turned, mate, core, norm, lags):
    num_bins, double, depth = own_turned.shape
    cols = mate.shape[2]
    bins = 8
    half = double // 4
    return pl.pallas_call(
        functools.partial(correlate_kernel, norm),
        grid=(num_bins // bins,),
        out_shape=[
            jax.ShapeDtypeStruct((lags, half, cols), f32),
            jax.ShapeDtypeStruct((lags, half, cols), bf16),
        ],
        in_specs=[
            pl.BlockSpec(memory_space=pltpu.SMEM),
            pl.BlockSpec((bins, double, depth), lambda s: (s, 0, 0)),
            pl.BlockSpec((bins, depth, cols), lambda s: (s, 0, 0)),
        ],
        out_specs=[
            pl.BlockSpec((lags, half, cols), lambda s: (0, 0, 0)),
            pl.BlockSpec((lags, half, cols), lambda s: (0, 0, 0)),
        ],
        scratch_shapes=[pltpu.VMEM((num_bins, double, cols), f32)],
        compiler_params=params(),
        cost_estimate=pl.CostEstimate(
            flops=2 * num_bins * double * depth * cols, bytes_accessed=20_000_000, transcendentals=0
        ),
        name="correlate",
    )(core, own_turned, mate)


def final_kernel(*refs):
    *in_refs, out_ref = refs
    rows = 8
    for turn_index in range(len(in_refs) // 2):
        mine, theirs = in_refs[2 * turn_index], in_refs[2 * turn_index + 1]

        def body(chunk, carry):
            where = pl.ds(pl.multiple_of(chunk * 2 * rows, 2 * rows), 2 * rows)
            value = mine[:, where, :] + theirs[:, where, :].astype(f32)
            out_ref[where, turn_index] = jnp.swapaxes(value, 0, 1)
            return carry

        lax.fori_loop(0, out_ref.shape[0] // (2 * rows), body, 0)


def final(pairs):
    lags, rows, cols = pairs[0][0].shape
    flat = [array for pair in pairs for array in pair]
    vmem = pl.BlockSpec(memory_space=pltpu.VMEM)
    return pl.pallas_call(
        final_kernel,
        out_shape=jax.ShapeDtypeStruct((rows, len(pairs), lags, cols), f32),
        in_specs=[vmem] * len(flat),
        out_specs=vmem,
        compiler_params=params(),
        name="final",
    )(*flat)


def local(spectra, channel_order, partners):
    num_bins, _, num_windows, cols = spectra.shape
    win_count = lax.axis_size("win")
    place = lax.axis_index("win")
    core = (place % 2).astype(jnp.int32)
    chip = (place // 2).astype(jnp.int32)
    other_core = [(i, i ^ 1) for i in range(win_count)]
    other_chip = [(i, i ^ 2) for i in range(win_count)]
    norm = 1.0 / math.sqrt(num_windows * win_count * num_bins)

    own = whiten(spectra, channel_order).reshape(num_bins, 2 * num_windows, cols)
    own_turned = turn(own)
    shares = lax.all_to_all(own, "pair", split_axis=0, concat_axis=0, tiled=True)
    pairs = []
    for turn_index in range(ROUNDS):
        arranged = gather(shares, partners[turn_index])
        mate = lax.all_to_all(arranged, "pair", split_axis=0, concat_axis=0, tiled=True)
        keep, send = correlate(own_turned, mate, core[None], norm, LAGS)
        total = keep + lax.ppermute(send, "win", other_core).astype(f32)
        quarter = cols // 4
        mine = lax.dynamic_slice_in_dim(total, chip * quarter, quarter, 1)
        others = lax.dynamic_slice_in_dim(total, (1 - chip) * quarter, quarter, 1).astype(bf16)
        pairs.append((mine, lax.ppermute(others, "win", other_chip)))
    return final(pairs)[None]


def solution(mesh):
    return jax.shard_map(
        local,
        mesh=mesh,
        in_specs=(P(None, None, "win", "pair"), P("pair", None), P()),
        out_specs=P("pair", "win", None, None, None),
        check_vma=False,
    )
```

```python
import functools
import math

import jax
import jax.numpy as jnp
from jax import lax
from jax.experimental import pallas as pl
from jax.experimental.pallas import tpu as pltpu
from jax.sharding import PartitionSpec as P

LAGS = 16
ROUNDS = 4
VMEM_BYTES = 56 * 1024 * 1024
QUARTER_ORDER = (0, 2, 1, 3)
bf16 = jnp.bfloat16
f32 = jnp.float32


def params(**more):
    return pltpu.CompilerParams(vmem_limit_bytes=VMEM_BYTES, **more)


def whiten_kernel(order_ref, spectra_ref, out_ref):
    num_bins, _, rows, cols = spectra_ref.shape
    slots = lax.broadcasted_iota(jnp.int32, (cols, cols), 0)
    pick = (slots == order_ref[...]).astype(f32).astype(bf16)
    values = spectra_ref[...].astype(f32)
    power = values[:, 0] * values[:, 0] + values[:, 1] * values[:, 1]
    parts = []
    for f in range(num_bins):
        lo, hi = max(f - 2, 0), min(f + 2, num_bins - 1)
        total = power[lo]
        for g in range(lo + 1, hi + 1):
            total = total + power[g]
        inv_scale = jnp.minimum(lax.rsqrt(total * (1.0 / (hi - lo + 1))), 2.0)
        parts.append((values[f] * inv_scale[None]).astype(bf16).reshape(2 * rows, cols))
    flat = jnp.concatenate(parts, 0)
    ordered = jnp.dot(flat, pick, preferred_element_type=f32).astype(bf16)
    out_ref[...] = ordered.reshape(num_bins, 2, rows, cols)


def whiten(spectra, channel_order):
    num_bins, _, num_windows, cols = spectra.shape
    rows = 16
    return pl.pallas_call(
        whiten_kernel,
        grid=(num_windows // rows,),
        out_shape=jax.ShapeDtypeStruct(spectra.shape, bf16),
        in_specs=[
            pl.BlockSpec((1, cols), lambda s: (0, 0)),
            pl.BlockSpec((num_bins, 2, rows, cols), lambda s: (0, 0, s, 0)),
        ],
        out_specs=pl.BlockSpec((num_bins, 2, rows, cols), lambda s: (0, 0, s, 0)),
        compiler_params=params(),
        name="whiten",
    )(channel_order, spectra)


def turn_kernel(own_ref, out_ref):
    bins, depth, cols = own_ref.shape
    half = depth // 2
    quarter = cols // 4
    for f in range(bins):
        block = own_ref[f].astype(f32)
        plain = block.T.astype(bf16)
        turned = jnp.concatenate([-block[half:], block[:half]], 0).T.astype(bf16)
        for place, source in enumerate(QUARTER_ORDER):
            rows = slice(source * quarter, (source + 1) * quarter)
            out_ref[f, place * quarter : (place + 1) * quarter, :] = plain[rows]
            out_ref[f, cols + place * quarter : cols + (place + 1) * quarter, :] = turned[rows]


def turn(own_rows):
    num_bins, depth, cols = own_rows.shape
    bins = 4
    return pl.pallas_call(
        turn_kernel,
        grid=(num_bins // bins,),
        out_shape=jax.ShapeDtypeStruct((num_bins, 2 * cols, depth), bf16),
        in_specs=[pl.BlockSpec((bins, depth, cols), lambda s: (s, 0, 0))],
        out_specs=pl.BlockSpec((bins, 2 * cols, depth), lambda s: (s, 0, 0)),
        compiler_params=params(),
        cost_estimate=pl.CostEstimate(flops=0, bytes_accessed=12_000_000, transcendentals=0),
        name="turn",
    )(own_rows)


def gather_kernel(index_ref, source_ref, *refs):
    *out_refs, sems = refs
    copies = []
    for group, out_ref in enumerate(out_refs):
        for place in range(out_ref.shape[0]):
            copy = pltpu.make_async_copy(
                source_ref.at[index_ref[group, place]], out_ref.at[place], sems.at[group, place]
            )
            copy.start()
            copies.append(copy)
    for copy in copies:
        copy.wait()


def gather(source, index):
    groups, places = index.shape
    return pl.pallas_call(
        gather_kernel,
        out_shape=[jax.ShapeDtypeStruct((places,) + source.shape[1:], source.dtype)] * groups,
        in_specs=[
            pl.BlockSpec(memory_space=pltpu.SMEM),
            pl.BlockSpec(memory_space=pltpu.VMEM),
        ],
        out_specs=[pl.BlockSpec(memory_space=pl.ANY)] * groups,
        scratch_shapes=[pltpu.SemaphoreType.DMA(index.shape)],
        compiler_params=params(),
        name="gather",
    )(index, source)


def weighted(terms):
    total = None
    for weight, value in terms:
        if abs(weight) < 1e-12:
            continue
        term = value * weight
        total = term if total is None else total + term
    return total


def lag_sums(real, imag, norm):
    cosine = lambda f, t: math.cos(math.pi * f * t / 32) * norm
    sine = lambda f, t: -math.sin(math.pi * f * t / 32) * norm
    even, odd = {}, {}
    low = {0: real(0), 16: real(16)}
    diff = {0: low[0]}
    for f in range(1, 16):
        a, b = real(f), real(32 - f)
        low[f], diff[f] = a + b, a - b
    for t in (1, 3, 5, 7):
        even[t] = weighted([(cosine(f, t), diff[f]) for f in range(16)])
    minus = {f: low[f] - low[16 - f] for f in range(8)}
    for t in (2, 6):
        even[t] = weighted([(cosine(f, t), minus[f]) for f in range(8)])
    plus = {f: low[f] + low[16 - f] for f in range(8)}
    plus[8] = low[8]
    even[4] = weighted([(cosine(f, 4), plus[f] - plus[8 - f]) for f in range(4)])
    sums = {f: plus[f] + plus[8 - f] for f in range(4)}
    sums[4] = plus[4]
    even[8] = weighted([(cosine(f, 8), sums[f]) for f in range(5)])
    total = sums[0]
    for f in range(1, 5):
        total = total + sums[f]
    even[0] = total * norm

    add = {16: imag(16)}
    sub = {}
    for f in range(1, 16):
        a, b = imag(f), imag(32 - f)
        add[f], sub[f] = a + b, a - b
    for t in (1, 3, 5, 7):
        odd[t] = weighted([(sine(f, t), add[f]) for f in range(1, 17)])
    sums = {f: sub[f] + sub[16 - f] for f in range(1, 8)}
    sums[8] = sub[8]
    for t in (2, 6):
        odd[t] = weighted([(sine(f, t), sums[f]) for f in range(1, 9)])
    minus = {f: sub[f] - sub[16 - f] for f in range(1, 8)}
    odd[4] = weighted(
        [(sine(f, 4), minus[f] + minus[8 - f]) for f in range(1, 4)] + [(sine(4, 4), minus[4])]
    )
    odd[8] = weighted([(sine(f, 8), minus[f] - minus[8 - f]) for f in range(1, 4)])
    return even, odd


def correlate_kernel(norm, core_ref, own_ref, mate_ref, keep_ref, send_ref, cross):
    step = pl.program_id(0)
    bins = own_ref.shape[0]
    for f in range(bins):
        cross[step * bins + f] = jnp.dot(own_ref[f], mate_ref[f], preferred_element_type=f32)

    @pl.when(step == pl.num_programs(0) - 1)
    def _():
        lags, half, cols = keep_ref.shape
        core = core_ref[0]
        rows, lanes = 16, 128

        def part(out_ref, base):
            def body(chunk, carry):
                row = pl.multiple_of(chunk * rows, rows)
                for lane in range(0, cols, lanes):
                    where = pl.ds(pl.multiple_of(base + row, rows), rows)
                    turned = pl.ds(pl.multiple_of(2 * half + base + row, rows), rows)
                    even, odd = lag_sums(
                        lambda f: cross[f, where, lane : lane + lanes],
                        lambda f: cross[f, turned, lane : lane + lanes],
                        norm,
                    )
                    for lag in range(lags):
                        t = lag - LAGS // 2
                        if t == 0:
                            value = even[0]
                        elif t > 0:
                            value = even[t] + odd[t]
                        else:
                            value = even[-t] - odd[-t]
                        out_ref[lag, pl.ds(row, rows), lane : lane + lanes] = value.astype(
                            out_ref.dtype
                        )
                return carry

            lax.fori_loop(0, half // rows, body, 0)

        part(keep_ref, core * half)
        part(send_ref, (1 - core) * half)


def correlate(own_turned, mate, core, norm, lags):
    num_bins, double, depth = own_turned.shape
    cols = mate.shape[2]
    bins = 8
    half = double // 4
    return pl.pallas_call(
        functools.partial(correlate_kernel, norm),
        grid=(num_bins // bins,),
        out_shape=[
            jax.ShapeDtypeStruct((lags, half, cols), f32),
            jax.ShapeDtypeStruct((lags, half, cols), bf16),
        ],
        in_specs=[
            pl.BlockSpec(memory_space=pltpu.SMEM),
            pl.BlockSpec((bins, double, depth), lambda s: (s, 0, 0)),
            pl.BlockSpec((bins, depth, cols), lambda s: (s, 0, 0)),
        ],
        out_specs=[
            pl.BlockSpec((lags, half, cols), lambda s: (0, 0, 0)),
            pl.BlockSpec((lags, half, cols), lambda s: (0, 0, 0)),
        ],
        scratch_shapes=[pltpu.VMEM((num_bins, double, cols), f32)],
        compiler_params=params(),
        cost_estimate=pl.CostEstimate(
            flops=2 * num_bins * double * depth * cols, bytes_accessed=20_000_000, transcendentals=0
        ),
        name="correlate",
    )(core, own_turned, mate)


def final_kernel(*refs):
    *in_refs, out_ref = refs
    rows = 8
    for turn_index in range(len(in_refs) // 2):
        mine, theirs = in_refs[2 * turn_index], in_refs[2 * turn_index + 1]

        def body(chunk, carry):
            where = pl.ds(pl.multiple_of(chunk * 2 * rows, 2 * rows), 2 * rows)
            value = mine[:, where, :] + theirs[:, where, :].astype(f32)
            out_ref[where, turn_index] = jnp.swapaxes(value, 0, 1)
            return carry

        lax.fori_loop(0, out_ref.shape[0] // (2 * rows), body, 0)


def final(pairs):
    lags, rows, cols = pairs[0][0].shape
    flat = [array for pair in pairs for array in pair]
    vmem = pl.BlockSpec(memory_space=pltpu.VMEM)
    return pl.pallas_call(
        final_kernel,
        out_shape=jax.ShapeDtypeStruct((rows, len(pairs), lags, cols), f32),
        in_specs=[vmem] * len(flat),
        out_specs=vmem,
        compiler_params=params(),
        name="final",
    )(*flat)


def local(spectra, channel_order, partners):
    num_bins, _, num_windows, cols = spectra.shape
    win_count = lax.axis_size("win")
    place = lax.axis_index("win")
    core = (place % 2).astype(jnp.int32)
    chip = (place // 2).astype(jnp.int32)
    other_core = [(i, i ^ 1) for i in range(win_count)]
    other_chip = [(i, i ^ 2) for i in range(win_count)]
    norm = 1.0 / math.sqrt(num_windows * win_count * num_bins)

    own = whiten(spectra, channel_order).reshape(num_bins, 2 * num_windows, cols)
    own_turned = turn(own)
    shares = lax.all_to_all(own, "pair", split_axis=0, concat_axis=0, tiled=True)
    arranged = gather(shares, partners)
    pairs = []
    kept = []
    for turn_index in range(ROUNDS):
        operand = arranged[turn_index]
        if turn_index >= 2:
            operand, kept[turn_index - 2] = lax.optimization_barrier((operand, kept[turn_index - 2]))
        mate = lax.all_to_all(operand, "pair", split_axis=0, concat_axis=0, tiled=True)
        kept.append(correlate(own_turned, mate, core[None], norm, LAGS))
    quarter = cols // 4
    for keep, send in kept:
        total = keep + lax.ppermute(send, "win", other_core).astype(f32)
        mine = lax.dynamic_slice_in_dim(total, chip * quarter, quarter, 1)
        others = lax.dynamic_slice_in_dim(total, (1 - chip) * quarter, quarter, 1).astype(bf16)
        pairs.append((mine, lax.ppermute(others, "win", other_chip)))
    return final(pairs)[None]


def solution(mesh):
    return jax.shard_map(
        local,
        mesh=mesh,
        in_specs=(P(None, None, "win", "pair"), P("pair", None), P()),
        out_specs=P("pair", "win", None, None, None),
        check_vma=False,
    )
```

```python
import functools
import math

import jax
import jax.numpy as jnp
from jax import lax
from jax.experimental import pallas as pl
from jax.experimental.pallas import tpu as pltpu
from jax.sharding import PartitionSpec as P

LAGS = 16
ROUNDS = 4
VMEM_BYTES = 56 * 1024 * 1024
QUARTER_ORDER = (0, 2, 1, 3)
bf16 = jnp.bfloat16
f32 = jnp.float32


def params(**more):
    return pltpu.CompilerParams(vmem_limit_bytes=VMEM_BYTES, **more)


def whiten_kernel(order_ref, spectra_ref, out_ref):
    num_bins, _, rows, cols = spectra_ref.shape
    slots = lax.broadcasted_iota(jnp.int32, (cols, cols), 0)
    pick = (slots == order_ref[...]).astype(f32).astype(bf16)
    values = spectra_ref[...].astype(f32)
    power = values[:, 0] * values[:, 0] + values[:, 1] * values[:, 1]
    parts = []
    for f in range(num_bins):
        lo, hi = max(f - 2, 0), min(f + 2, num_bins - 1)
        total = power[lo]
        for g in range(lo + 1, hi + 1):
            total = total + power[g]
        inv_scale = jnp.minimum(lax.rsqrt(total * (1.0 / (hi - lo + 1))), 2.0)
        parts.append((values[f] * inv_scale[None]).astype(bf16).reshape(2 * rows, cols))
    flat = jnp.concatenate(parts, 0)
    ordered = jnp.dot(flat, pick, preferred_element_type=f32).astype(bf16)
    out_ref[...] = ordered.reshape(num_bins, 2, rows, cols)


def whiten(spectra, channel_order):
    num_bins, _, num_windows, cols = spectra.shape
    rows = 16
    return pl.pallas_call(
        whiten_kernel,
        grid=(num_windows // rows,),
        out_shape=jax.ShapeDtypeStruct(spectra.shape, bf16),
        in_specs=[
            pl.BlockSpec((1, cols), lambda s: (0, 0)),
            pl.BlockSpec((num_bins, 2, rows, cols), lambda s: (0, 0, s, 0)),
        ],
        out_specs=pl.BlockSpec((num_bins, 2, rows, cols), lambda s: (0, 0, s, 0)),
        compiler_params=params(),
        name="whiten",
    )(channel_order, spectra)


def turn_kernel(own_ref, out_ref):
    bins, depth, cols = own_ref.shape
    half = depth // 2
    quarter = cols // 4
    for f in range(bins):
        block = own_ref[f].astype(f32)
        plain = block.T.astype(bf16)
        turned = jnp.concatenate([-block[half:], block[:half]], 0).T.astype(bf16)
        for place, source in enumerate(QUARTER_ORDER):
            rows = slice(source * quarter, (source + 1) * quarter)
            out_ref[f, place * quarter : (place + 1) * quarter, :] = plain[rows]
            out_ref[f, cols + place * quarter : cols + (place + 1) * quarter, :] = turned[rows]


def turn(own_rows):
    num_bins, depth, cols = own_rows.shape
    bins = 4
    return pl.pallas_call(
        turn_kernel,
        grid=(num_bins // bins,),
        out_shape=jax.ShapeDtypeStruct((num_bins, 2 * cols, depth), bf16),
        in_specs=[pl.BlockSpec((bins, depth, cols), lambda s: (s, 0, 0))],
        out_specs=pl.BlockSpec((bins, 2 * cols, depth), lambda s: (s, 0, 0)),
        compiler_params=params(),
        cost_estimate=pl.CostEstimate(flops=0, bytes_accessed=12_000_000, transcendentals=0),
        name="turn",
    )(own_rows)


def gather_kernel(index_ref, source_ref, *refs):
    *out_refs, sems = refs
    copies = []
    for group, out_ref in enumerate(out_refs):
        for place in range(out_ref.shape[0]):
            copy = pltpu.make_async_copy(
                source_ref.at[index_ref[group, place]], out_ref.at[place], sems.at[group, place]
            )
            copy.start()
            copies.append(copy)
    for copy in copies:
        copy.wait()


def gather(source, index):
    groups, places = index.shape
    return pl.pallas_call(
        gather_kernel,
        out_shape=[jax.ShapeDtypeStruct((places,) + source.shape[1:], source.dtype)] * groups,
        in_specs=[
            pl.BlockSpec(memory_space=pltpu.SMEM),
            pl.BlockSpec(memory_space=pltpu.VMEM),
        ],
        out_specs=[pl.BlockSpec(memory_space=pl.ANY)] * groups,
        scratch_shapes=[pltpu.SemaphoreType.DMA(index.shape)],
        compiler_params=params(),
        name="gather",
    )(index, source)


def weighted(terms):
    total = None
    for weight, value in terms:
        if abs(weight) < 1e-12:
            continue
        term = value * weight
        total = term if total is None else total + term
    return total


def lag_sums(real, imag, norm):
    cosine = lambda f, t: math.cos(math.pi * f * t / 32) * norm
    sine = lambda f, t: -math.sin(math.pi * f * t / 32) * norm
    even, odd = {}, {}
    low = {0: real(0), 16: real(16)}
    diff = {0: low[0]}
    for f in range(1, 16):
        a, b = real(f), real(32 - f)
        low[f], diff[f] = a + b, a - b
    for t in (1, 3, 5, 7):
        even[t] = weighted([(cosine(f, t), diff[f]) for f in range(16)])
    minus = {f: low[f] - low[16 - f] for f in range(8)}
    for t in (2, 6):
        even[t] = weighted([(cosine(f, t), minus[f]) for f in range(8)])
    plus = {f: low[f] + low[16 - f] for f in range(8)}
    plus[8] = low[8]
    even[4] = weighted([(cosine(f, 4), plus[f] - plus[8 - f]) for f in range(4)])
    sums = {f: plus[f] + plus[8 - f] for f in range(4)}
    sums[4] = plus[4]
    even[8] = weighted([(cosine(f, 8), sums[f]) for f in range(5)])
    total = sums[0]
    for f in range(1, 5):
        total = total + sums[f]
    even[0] = total * norm

    add = {16: imag(16)}
    sub = {}
    for f in range(1, 16):
        a, b = imag(f), imag(32 - f)
        add[f], sub[f] = a + b, a - b
    for t in (1, 3, 5, 7):
        odd[t] = weighted([(sine(f, t), add[f]) for f in range(1, 17)])
    sums = {f: sub[f] + sub[16 - f] for f in range(1, 8)}
    sums[8] = sub[8]
    for t in (2, 6):
        odd[t] = weighted([(sine(f, t), sums[f]) for f in range(1, 9)])
    minus = {f: sub[f] - sub[16 - f] for f in range(1, 8)}
    odd[4] = weighted(
        [(sine(f, 4), minus[f] + minus[8 - f]) for f in range(1, 4)] + [(sine(4, 4), minus[4])]
    )
    odd[8] = weighted([(sine(f, 8), minus[f] - minus[8 - f]) for f in range(1, 4)])
    return even, odd


def correlate_kernel(norm, core_ref, own_ref, mate_ref, keep_ref, send_ref, cross):
    step = pl.program_id(0)
    bins = own_ref.shape[0]
    for f in range(bins):
        cross[step * bins + f] = jnp.dot(own_ref[f], mate_ref[f], preferred_element_type=f32)

    @pl.when(step == pl.num_programs(0) - 1)
    def _():
        lags, half, cols = keep_ref.shape
        core = core_ref[0]
        rows, lanes = 16, 128

        def part(out_ref, base):
            def body(chunk, carry):
                row = pl.multiple_of(chunk * rows, rows)
                for lane in range(0, cols, lanes):
                    where = pl.ds(pl.multiple_of(base + row, rows), rows)
                    turned = pl.ds(pl.multiple_of(2 * half + base + row, rows), rows)
                    even, odd = lag_sums(
                        lambda f: cross[f, where, lane : lane + lanes],
                        lambda f: cross[f, turned, lane : lane + lanes],
                        norm,
                    )
                    for lag in range(lags):
                        t = lag - LAGS // 2
                        if t == 0:
                            value = even[0]
                        elif t > 0:
                            value = even[t] + odd[t]
                        else:
                            value = even[-t] - odd[-t]
                        out_ref[lag, pl.ds(row, rows), lane : lane + lanes] = value.astype(
                            out_ref.dtype
                        )
                return carry

            lax.fori_loop(0, half // rows, body, 0)

        part(keep_ref, core * half)
        part(send_ref, (1 - core) * half)


def correlate(own_turned, mate, core, norm, lags):
    num_bins, double, depth = own_turned.shape
    cols = mate.shape[2]
    bins = 8
    half = double // 4
    return pl.pallas_call(
        functools.partial(correlate_kernel, norm),
        grid=(num_bins // bins,),
        out_shape=[
            jax.ShapeDtypeStruct((lags, half, cols), f32),
            jax.ShapeDtypeStruct((lags, half, cols), bf16),
        ],
        in_specs=[
            pl.BlockSpec(memory_space=pltpu.SMEM),
            pl.BlockSpec((bins, double, depth), lambda s: (s, 0, 0)),
            pl.BlockSpec((bins, depth, cols), lambda s: (s, 0, 0)),
        ],
        out_specs=[
            pl.BlockSpec((lags, half, cols), lambda s: (0, 0, 0)),
            pl.BlockSpec((lags, half, cols), lambda s: (0, 0, 0)),
        ],
        scratch_shapes=[pltpu.VMEM((num_bins, double, cols), f32)],
        compiler_params=params(),
        cost_estimate=pl.CostEstimate(
            flops=2 * num_bins * double * depth * cols, bytes_accessed=20_000_000, transcendentals=0
        ),
        name="correlate",
    )(core, own_turned, mate)


def plan_kernel(partners_ref, mate_ref, back_ref, flip_ref):
    rounds, blocks = partners_ref.shape
    for task in range(rounds // 2):
        first, second = 2 * task, 2 * task + 1

        def clear(block, carry):
            flip_ref[task, block] = -1
            return carry

        def walk(block):
            partner = partners_ref[first, block]
            flip_ref[task, block] = 0
            flip_ref[task, partner] = 1
            mate_ref[task, block] = partner
            back_ref[task, partner] = block
            following = partners_ref[second, partner]
            mate_ref[task, partner] = following
            back_ref[task, following] = partner
            return following

        def start(block, carry):
            lax.while_loop(lambda block: flip_ref[task, block] < 0, walk, block)
            return carry

        lax.fori_loop(0, blocks, clear, 0)
        lax.fori_loop(0, blocks, start, 0)


def plan(partners):
    rounds, blocks = partners.shape
    smem = pl.BlockSpec(memory_space=pltpu.SMEM)
    table = jax.ShapeDtypeStruct((rounds // 2, blocks), jnp.int32)
    return pl.pallas_call(
        plan_kernel,
        out_shape=[table] * 3,
        in_specs=[smem],
        out_specs=[smem] * 3,
        compiler_params=params(),
        name="plan",
    )(partners)


def core_sum_kernel(place_ref, keep_ref, recv_ref, own_ref, other_ref, send_ref):
    chip = place_ref[1]
    lags, rows, cols = own_ref.shape
    half = cols // 2
    own_rows = pl.ds(pl.multiple_of(chip * rows, rows), rows)
    other_rows = pl.ds(pl.multiple_of((1 - chip) * rows, rows), rows)
    own_cols = pl.ds(pl.multiple_of(chip * half, half), half)
    other_cols = pl.ds(pl.multiple_of((1 - chip) * half, half), half)
    for lag in range(lags):
        own_ref[lag] = keep_ref[lag, own_rows, :] + recv_ref[lag, own_rows, :].astype(f32)
        send_ref[lag] = (
            keep_ref[lag, other_rows, :] + recv_ref[lag, other_rows, :].astype(f32)
        ).astype(bf16)
        if lag > 0:
            other_ref[lag - 1] = keep_ref[lag, other_rows, own_cols] + recv_ref[
                lag, other_rows, own_cols
            ].astype(f32)
            lane = (lag - 1) % 2 * half
            send_ref[lags + (lag - 1) // 2, :, lane : lane + half] = (
                keep_ref[lag, own_rows, other_cols]
                + recv_ref[lag, own_rows, other_cols].astype(f32)
            ).astype(bf16)


def core_sum(place, keep, recv):
    lags, rows, cols = keep.shape
    vmem = pl.BlockSpec(memory_space=pltpu.VMEM)
    return pl.pallas_call(
        core_sum_kernel,
        out_shape=[
            jax.ShapeDtypeStruct((lags, rows // 2, cols), f32),
            jax.ShapeDtypeStruct((lags - 1, rows // 2, cols // 2), f32),
            jax.ShapeDtypeStruct((lags + (lags - 1) // 2, rows // 2, cols), bf16),
        ],
        in_specs=[pl.BlockSpec(memory_space=pltpu.SMEM), vmem, vmem],
        out_specs=[vmem] * 3,
        compiler_params=params(),
        cost_estimate=pl.CostEstimate(flops=0, bytes_accessed=8_000_000, transcendentals=0),
        name="core_sum",
    )(place, keep, recv)


def chip_sum_kernel(place_ref, own_ref, other_ref, recv_ref, mine_ref, keep_ref, send_ref):
    core, chip = place_ref[0], place_ref[1]
    lags, rows, cols = own_ref.shape
    half = cols // 2
    own_cols = pl.ds(pl.multiple_of(chip * half, half), half)
    for lag in range(lags - 1):
        mine_ref[lag] = own_ref[lag] + recv_ref[lag].astype(f32)
    for back in range(lags - 1):
        lag = lags - 1 - back
        lane = (lag - 1) % 2 * half
        own = own_ref[lag, :, own_cols] + recv_ref[lag, :, own_cols].astype(f32)
        other = other_ref[lag - 1] + recv_ref[
            lags + (lag - 1) // 2, :, lane : lane + half
        ].astype(f32)
        low = jnp.where(chip == 0, own, other)
        high = jnp.where(chip == 0, other, own)
        turned = jnp.concatenate([low, high], 0).T
        keep_ref[back] = jnp.where(core == 0, turned[:rows], turned[rows:]).astype(bf16)
        send_ref[back] = jnp.where(core == 0, turned[rows:], turned[:rows]).astype(bf16)


def chip_sum(place, own, other, recv):
    lags, rows, cols = own.shape
    vmem = pl.BlockSpec(memory_space=pltpu.VMEM)
    back = jax.ShapeDtypeStruct((lags - 1, rows, 2 * rows), bf16)
    return pl.pallas_call(
        chip_sum_kernel,
        out_shape=[jax.ShapeDtypeStruct((lags - 1, rows, cols), f32), back, back],
        in_specs=[pl.BlockSpec(memory_space=pltpu.SMEM), vmem, vmem, vmem],
        out_specs=[vmem] * 3,
        compiler_params=params(),
        cost_estimate=pl.CostEstimate(flops=0, bytes_accessed=10_000_000, transcendentals=0),
        name="chip_sum",
    )(place, own, other, recv)


def final_kernel(tasks, place_ref, flip_ref, *refs):
    out_ref = refs[-1]
    core, block = place_ref[0], place_ref[2]
    for task in range(tasks):
        mine_ref, back_ref = refs[2 * task], refs[2 * task + 1]
        flip = flip_ref[task, block]
        lags = mine_ref.shape[0]
        out_ref[:, 2 * task + flip] = jnp.swapaxes(mine_ref[...], 0, 1)
        near = back_ref[:lags].astype(f32)
        far = back_ref[lags:].astype(f32)
        first = jnp.where(core == 0, near, far)
        second = jnp.where(core == 0, far, near)
        lanes = first.shape[2]
        lane = lax.broadcasted_iota(jnp.int32, first.shape, 2)
        quarter = lanes // 2
        low = jnp.where(lane < quarter, first, pltpu.roll(second, quarter, 2))
        high = jnp.where(lane < quarter, pltpu.roll(first, quarter, 2), second)
        out_ref[:, 2 * task + 1 - flip, :, :lanes] = jnp.swapaxes(low, 0, 1)
        out_ref[:, 2 * task + 1 - flip, :, lanes:] = jnp.swapaxes(high, 0, 1)


def final(place, flip, pairs):
    lags, rows, cols = pairs[0][0].shape
    flat = [array for pair in pairs for array in pair]
    smem = pl.BlockSpec(memory_space=pltpu.SMEM)
    step = 16
    specs = [pl.BlockSpec((array.shape[0], step, array.shape[2]), lambda s: (0, s, 0)) for array in flat]
    return pl.pallas_call(
        functools.partial(final_kernel, len(pairs)),
        grid=(rows // step,),
        out_shape=jax.ShapeDtypeStruct((rows, 2 * len(pairs), lags, cols), f32),
        in_specs=[smem, smem] + specs,
        out_specs=pl.BlockSpec((step, 2 * len(pairs), lags, cols), lambda s: (s, 0, 0, 0)),
        compiler_params=params(),
        name="final",
    )(place, flip, *flat)


def exchange(array):
    return lax.all_to_all(array, "pair", split_axis=0, concat_axis=0, tiled=True)


def local(spectra, channel_order, partners):
    num_bins, _, num_windows, cols = spectra.shape
    win_count = lax.axis_size("win")
    win = lax.axis_index("win")
    place = jnp.stack([win % 2, win // 2, lax.axis_index("pair")]).astype(jnp.int32)
    other_core = [(i, i ^ 1) for i in range(win_count)]
    other_chip = [(i, i ^ 2) for i in range(win_count)]
    norm = 1.0 / math.sqrt(num_windows * win_count * num_bins)
    tasks = ROUNDS // 2

    own = whiten(spectra, channel_order).reshape(num_bins, 2 * num_windows, cols)
    own_turned = turn(own)
    mate_of, back_of, flip = plan(partners)
    shares = exchange(own)
    arranged = list(gather(shares, mate_of))
    arranged[0], own_turned = lax.optimization_barrier((arranged[0], own_turned))
    mates = [exchange(arranged[task]) for task in range(tasks)]
    pairs = []
    for task in range(tasks):
        keep, send = correlate(own_turned, mates[task], place, norm, LAGS + 1)
        own_sum, other_sum, chip_send = core_sum(
            place, keep, lax.ppermute(send, "win", other_core)
        )
        if task + 1 < tasks:
            mates[task + 1], chip_send = lax.optimization_barrier((mates[task + 1], chip_send))
        mine, back_keep, back_send = chip_sum(
            place, own_sum, other_sum, lax.ppermute(chip_send, "win", other_chip)
        )
        back_recv = lax.ppermute(back_send, "win", other_core)
        spread = exchange(jnp.concatenate([back_keep, back_recv], 0))
        (returned,) = gather(spread, back_of[task : task + 1])
        pairs.append((mine, exchange(returned)))
    return final(place, flip, pairs)[None]


def solution(mesh):
    return jax.shard_map(
        local,
        mesh=mesh,
        in_specs=(P(None, None, "win", "pair"), P("pair", None), P()),
        out_specs=P("pair", "win", None, None, None),
        check_vma=False,
    )
```

```python
import functools
import math

import jax
import jax.numpy as jnp
from jax import lax
from jax.experimental import pallas as pl
from jax.experimental.pallas import tpu as pltpu
from jax.sharding import PartitionSpec as P

LAGS = 16
ROUNDS = 4
VMEM_BYTES = 56 * 1024 * 1024
QUARTER_ORDER = (0, 2, 1, 3)
bf16 = jnp.bfloat16
f32 = jnp.float32


def params(**more):
    return pltpu.CompilerParams(vmem_limit_bytes=VMEM_BYTES, **more)


def whiten_kernel(order_ref, spectra_ref, out_ref):
    num_bins, _, rows, cols = spectra_ref.shape
    slots = lax.broadcasted_iota(jnp.int32, (cols, cols), 0)
    pick = (slots == order_ref[...]).astype(f32).astype(bf16)
    values = spectra_ref[...].astype(f32)
    power = values[:, 0] * values[:, 0] + values[:, 1] * values[:, 1]
    parts = []
    for f in range(num_bins):
        lo, hi = max(f - 2, 0), min(f + 2, num_bins - 1)
        total = power[lo]
        for g in range(lo + 1, hi + 1):
            total = total + power[g]
        inv_scale = jnp.minimum(lax.rsqrt(total * (1.0 / (hi - lo + 1))), 2.0)
        parts.append((values[f] * inv_scale[None]).astype(bf16).reshape(2 * rows, cols))
    flat = jnp.concatenate(parts, 0)
    ordered = jnp.dot(flat, pick, preferred_element_type=f32).astype(bf16)
    out_ref[...] = ordered.reshape(num_bins, 2, rows, cols)


def whiten(spectra, channel_order):
    num_bins, _, num_windows, cols = spectra.shape
    rows = 16
    return pl.pallas_call(
        whiten_kernel,
        grid=(num_windows // rows,),
        out_shape=jax.ShapeDtypeStruct(spectra.shape, bf16),
        in_specs=[
            pl.BlockSpec((1, cols), lambda s: (0, 0)),
            pl.BlockSpec((num_bins, 2, rows, cols), lambda s: (0, 0, s, 0)),
        ],
        out_specs=pl.BlockSpec((num_bins, 2, rows, cols), lambda s: (0, 0, s, 0)),
        compiler_params=params(),
        name="whiten",
    )(channel_order, spectra)


def turn_kernel(own_ref, out_ref):
    bins, depth, cols = own_ref.shape
    half = depth // 2
    quarter = cols // 4
    for f in range(bins):
        block = own_ref[f].astype(f32)
        plain = block.T.astype(bf16)
        turned = jnp.concatenate([-block[half:], block[:half]], 0).T.astype(bf16)
        for place, source in enumerate(QUARTER_ORDER):
            rows = slice(source * quarter, (source + 1) * quarter)
            out_ref[f, place * quarter : (place + 1) * quarter, :] = plain[rows]
            out_ref[f, cols + place * quarter : cols + (place + 1) * quarter, :] = turned[rows]


def turn(own_rows):
    num_bins, depth, cols = own_rows.shape
    bins = 4
    return pl.pallas_call(
        turn_kernel,
        grid=(num_bins // bins,),
        out_shape=jax.ShapeDtypeStruct((num_bins, 2 * cols, depth), bf16),
        in_specs=[pl.BlockSpec((bins, depth, cols), lambda s: (s, 0, 0))],
        out_specs=pl.BlockSpec((bins, 2 * cols, depth), lambda s: (s, 0, 0)),
        compiler_params=params(),
        cost_estimate=pl.CostEstimate(flops=0, bytes_accessed=12_000_000, transcendentals=0),
        name="turn",
    )(own_rows)


def gather_kernel(index_ref, source_ref, *refs):
    *out_refs, sems = refs
    copies = []
    for group, out_ref in enumerate(out_refs):
        for place in range(out_ref.shape[0]):
            copy = pltpu.make_async_copy(
                source_ref.at[index_ref[group, place]], out_ref.at[place], sems.at[group, place]
            )
            copy.start()
            copies.append(copy)
    for copy in copies:
        copy.wait()


def gather(source, index):
    groups, places = index.shape
    return pl.pallas_call(
        gather_kernel,
        out_shape=[jax.ShapeDtypeStruct((places,) + source.shape[1:], source.dtype)] * groups,
        in_specs=[
            pl.BlockSpec(memory_space=pltpu.SMEM),
            pl.BlockSpec(memory_space=pltpu.VMEM),
        ],
        out_specs=[pl.BlockSpec(memory_space=pl.ANY)] * groups,
        scratch_shapes=[pltpu.SemaphoreType.DMA(index.shape)],
        compiler_params=params(),
        name="gather",
    )(index, source)


def weighted(terms):
    total = None
    for weight, value in terms:
        if abs(weight) < 1e-12:
            continue
        term = value * weight
        total = term if total is None else total + term
    return total


def lag_sums(real, imag, norm):
    cosine = lambda f, t: math.cos(math.pi * f * t / 32) * norm
    sine = lambda f, t: -math.sin(math.pi * f * t / 32) * norm
    even, odd = {}, {}
    low = {0: real(0), 16: real(16)}
    diff = {0: low[0]}
    for f in range(1, 16):
        a, b = real(f), real(32 - f)
        low[f], diff[f] = a + b, a - b
    for t in (1, 3, 5, 7):
        even[t] = weighted([(cosine(f, t), diff[f]) for f in range(16)])
    minus = {f: low[f] - low[16 - f] for f in range(8)}
    for t in (2, 6):
        even[t] = weighted([(cosine(f, t), minus[f]) for f in range(8)])
    plus = {f: low[f] + low[16 - f] for f in range(8)}
    plus[8] = low[8]
    even[4] = weighted([(cosine(f, 4), plus[f] - plus[8 - f]) for f in range(4)])
    sums = {f: plus[f] + plus[8 - f] for f in range(4)}
    sums[4] = plus[4]
    even[8] = weighted([(cosine(f, 8), sums[f]) for f in range(5)])
    total = sums[0]
    for f in range(1, 5):
        total = total + sums[f]
    even[0] = total * norm

    add = {16: imag(16)}
    sub = {}
    for f in range(1, 16):
        a, b = imag(f), imag(32 - f)
        add[f], sub[f] = a + b, a - b
    for t in (1, 3, 5, 7):
        odd[t] = weighted([(sine(f, t), add[f]) for f in range(1, 17)])
    sums = {f: sub[f] + sub[16 - f] for f in range(1, 8)}
    sums[8] = sub[8]
    for t in (2, 6):
        odd[t] = weighted([(sine(f, t), sums[f]) for f in range(1, 9)])
    minus = {f: sub[f] - sub[16 - f] for f in range(1, 8)}
    odd[4] = weighted(
        [(sine(f, 4), minus[f] + minus[8 - f]) for f in range(1, 4)] + [(sine(4, 4), minus[4])]
    )
    odd[8] = weighted([(sine(f, 8), minus[f] - minus[8 - f]) for f in range(1, 4)])
    return even, odd


def correlate_kernel(norm, core_ref, own_ref, mate_ref, keep_ref, send_ref, cross):
    step = pl.program_id(0)
    bins = own_ref.shape[0]
    for f in range(bins):
        cross[step * bins + f] = jnp.dot(own_ref[f], mate_ref[f], preferred_element_type=f32)

    @pl.when(step == pl.num_programs(0) - 1)
    def _():
        lags, half, cols = keep_ref.shape
        core = core_ref[0]
        rows, lanes = 16, 128

        def part(out_ref, base):
            def body(chunk, carry):
                row = pl.multiple_of(chunk * rows, rows)
                for lane in range(0, cols, lanes):
                    where = pl.ds(pl.multiple_of(base + row, rows), rows)
                    turned = pl.ds(pl.multiple_of(2 * half + base + row, rows), rows)
                    even, odd = lag_sums(
                        lambda f: cross[f, where, lane : lane + lanes],
                        lambda f: cross[f, turned, lane : lane + lanes],
                        norm,
                    )
                    for lag in range(lags):
                        t = lag - LAGS // 2
                        if t == 0:
                            value = even[0]
                        elif t > 0:
                            value = even[t] + odd[t]
                        else:
                            value = even[-t] - odd[-t]
                        out_ref[lag, pl.ds(row, rows), lane : lane + lanes] = value.astype(
                            out_ref.dtype
                        )
                return carry

            lax.fori_loop(0, half // rows, body, 0)

        part(keep_ref, core * half)
        part(send_ref, (1 - core) * half)


def correlate(own_turned, mate, core, norm, lags):
    num_bins, double, depth = own_turned.shape
    cols = mate.shape[2]
    bins = 8
    half = double // 4
    return pl.pallas_call(
        functools.partial(correlate_kernel, norm),
        grid=(num_bins // bins,),
        out_shape=[
            jax.ShapeDtypeStruct((lags, half, cols), f32),
            jax.ShapeDtypeStruct((lags, half, cols), bf16),
        ],
        in_specs=[
            pl.BlockSpec(memory_space=pltpu.SMEM),
            pl.BlockSpec((bins, double, depth), lambda s: (s, 0, 0)),
            pl.BlockSpec((bins, depth, cols), lambda s: (s, 0, 0)),
        ],
        out_specs=[
            pl.BlockSpec((lags, half, cols), lambda s: (0, 0, 0)),
            pl.BlockSpec((lags, half, cols), lambda s: (0, 0, 0)),
        ],
        scratch_shapes=[pltpu.VMEM((num_bins, double, cols), f32)],
        compiler_params=params(),
        cost_estimate=pl.CostEstimate(
            flops=2 * num_bins * double * depth * cols, bytes_accessed=20_000_000, transcendentals=0
        ),
        name="correlate",
    )(core, own_turned, mate)


def plan_kernel(partners_ref, mate_ref, back_ref, flip_ref):
    rounds, blocks = partners_ref.shape
    for task in range(rounds // 2):
        first, second = 2 * task, 2 * task + 1

        def clear(block, carry):
            flip_ref[task, block] = -1
            return carry

        def walk(block):
            partner = partners_ref[first, block]
            flip_ref[task, block] = 0
            flip_ref[task, partner] = 1
            mate_ref[task, block] = partner
            back_ref[task, partner] = block
            following = partners_ref[second, partner]
            mate_ref[task, partner] = following
            back_ref[task, following] = partner
            return following

        def start(block, carry):
            lax.while_loop(lambda block: flip_ref[task, block] < 0, walk, block)
            return carry

        lax.fori_loop(0, blocks, clear, 0)
        lax.fori_loop(0, blocks, start, 0)


def plan(partners):
    rounds, blocks = partners.shape
    smem = pl.BlockSpec(memory_space=pltpu.SMEM)
    table = jax.ShapeDtypeStruct((rounds // 2, blocks), jnp.int32)
    return pl.pallas_call(
        plan_kernel,
        out_shape=[table] * 3,
        in_specs=[smem],
        out_specs=[smem] * 3,
        compiler_params=params(),
        name="plan",
    )(partners)


def core_sum_kernel(place_ref, keep_ref, recv_ref, near_ref, far_ref, turn_ref, rest_ref):
    chip = place_ref[1]
    lags, rows, half = near_ref.shape
    count = rows // 2
    own_rows = pl.ds(pl.multiple_of(chip * count, count), count)
    other_rows = pl.ds(pl.multiple_of((1 - chip) * count, count), count)
    own_cols = pl.ds(pl.multiple_of(chip * half, half), half)
    other_cols = pl.ds(pl.multiple_of((1 - chip) * half, half), half)

    def total(lag, where, columns):
        return keep_ref[lag, where, columns] + recv_ref[lag, where, columns].astype(f32)

    everything = slice(None)
    rest_ref[lags - 1] = total(0, other_rows, other_cols).astype(bf16)
    for lag in range(lags):
        near_ref[lag] = total(lag, everything, own_cols)
        if lag > 0:
            turn_ref[lag - 1] = total(lag, everything, other_cols).astype(bf16)
        if lag < lags - 1:
            far_ref[lag] = total(lag, own_rows, other_cols)
            rest_ref[lag] = total(lag, other_rows, own_cols).astype(bf16)


def core_sum(place, keep, recv):
    lags, rows, cols = keep.shape
    vmem = pl.BlockSpec(memory_space=pltpu.VMEM)
    return pl.pallas_call(
        core_sum_kernel,
        out_shape=[
            jax.ShapeDtypeStruct((lags, rows, cols // 2), f32),
            jax.ShapeDtypeStruct((lags - 1, rows // 2, cols // 2), f32),
            jax.ShapeDtypeStruct((lags - 1, rows, cols // 2), bf16),
            jax.ShapeDtypeStruct((lags, rows // 2, cols // 2), bf16),
        ],
        in_specs=[pl.BlockSpec(memory_space=pltpu.SMEM), vmem, vmem],
        out_specs=[vmem] * 4,
        compiler_params=params(),
        cost_estimate=pl.CostEstimate(flops=0, bytes_accessed=10_000_000, transcendentals=0),
        name="core_sum",
    )(place, keep, recv)


def mirror_kernel(place_ref, near_ref, recv_ref, *refs):
    *earlier_refs, back_ref = refs
    core = place_ref[0]
    lags, rows, _ = near_ref.shape
    task = len(earlier_refs)
    for index, earlier_ref in enumerate(earlier_refs):
        back_ref[:, index] = earlier_ref[:, index]
    for back in range(lags - 1):
        lag = lags - 1 - back
        turned = (near_ref[lag] + recv_ref[lag - 1].astype(f32)).T
        low, high = turned[: rows // 2], turned[rows // 2 :]
        back_ref[back, task] = jnp.where(core == 0, low, high).astype(bf16)
        back_ref[lags - 1 + back, task] = jnp.where(core == 0, high, low).astype(bf16)


def mirror(place, near, recv, earlier):
    lags, rows, cols = near.shape
    vmem = pl.BlockSpec(memory_space=pltpu.VMEM)
    return pl.pallas_call(
        mirror_kernel,
        out_shape=jax.ShapeDtypeStruct((2 * (lags - 1), len(earlier) + 1, cols // 2, rows), bf16),
        in_specs=[pl.BlockSpec(memory_space=pltpu.SMEM), vmem, vmem] + [vmem] * len(earlier),
        out_specs=vmem,
        compiler_params=params(),
        cost_estimate=pl.CostEstimate(flops=0, bytes_accessed=8_000_000, transcendentals=0),
        name="mirror",
    )(place, near, recv, *earlier)


def own_rows_kernel(flip_ref, place_ref, near_ref, far_ref, turn_ref, rest_ref, *refs):
    out_ref = refs[-1]
    chip = place_ref[1]
    lags, step, half = far_ref.shape
    near = near_ref[:lags]
    first = near[:1] + rest_ref[lags:].astype(f32)
    near = jnp.concatenate([first, near[1:] + turn_ref[: lags - 1].astype(f32)], 0)
    far = far_ref[...] + rest_ref[:lags].astype(f32)
    out_ref[:, 0, :, :half] = jnp.swapaxes(jnp.where(chip == 0, near, far), 0, 1)
    out_ref[:, 0, :, half:] = jnp.swapaxes(jnp.where(chip == 0, far, near), 0, 1)


def own_rows(place, flip, task, near, far, turn, rest, out):
    lags, rows, half = far.shape
    step = 16
    count = rows // step
    smem = pl.BlockSpec(memory_space=pltpu.SMEM)

    def piece(array):
        return pl.BlockSpec((array.shape[0], step, half), lambda s, flip, place: (0, s, 0))

    def half_piece(array):
        return pl.BlockSpec(
            (array.shape[0], step, half), lambda s, flip, place: (0, place[1] * count + s, 0)
        )

    extra = [] if out is None else [out]
    return pl.pallas_call(
        own_rows_kernel,
        out_shape=jax.ShapeDtypeStruct((rows, ROUNDS, lags, 2 * half), f32),
        grid_spec=pltpu.PrefetchScalarGridSpec(
            num_scalar_prefetch=2,
            grid=(count,),
            in_specs=[half_piece(near), piece(far), half_piece(turn), piece(rest)]
            + [pl.BlockSpec(memory_space=pl.ANY)] * len(extra),
            out_specs=pl.BlockSpec(
                (step, 1, lags, 2 * half),
                lambda s, flip, place: (s, 2 * task + flip[task, place[2]], 0, 0),
            ),
        ),
        input_output_aliases={6: 0} if extra else {},
        compiler_params=params(),
        cost_estimate=pl.CostEstimate(flops=0, bytes_accessed=5_000_000, transcendentals=0),
        name="own_rows",
    )(flip, place, near, far, turn, rest, *extra)


def gather_back_kernel(index_ref, source_ref, out_ref, sems):
    places, tasks = out_ref.shape[:2]
    copies = []
    for place in range(places):
        for task in range(tasks):
            copy = pltpu.make_async_copy(
                source_ref.at[index_ref[task, place], task],
                out_ref.at[place, task],
                sems.at[task, place],
            )
            copy.start()
            copies.append(copy)
    for copy in copies:
        copy.wait()


def gather_back(source, index):
    return pl.pallas_call(
        gather_back_kernel,
        out_shape=jax.ShapeDtypeStruct(source.shape, source.dtype),
        in_specs=[
            pl.BlockSpec(memory_space=pltpu.SMEM),
            pl.BlockSpec(memory_space=pltpu.VMEM),
        ],
        out_specs=pl.BlockSpec(memory_space=pl.ANY),
        scratch_shapes=[pltpu.SemaphoreType.DMA(index.shape)],
        compiler_params=params(),
        name="gather_back",
    )(index, source)


def mirrored_rows_kernel(flip_ref, place_ref, near_ref, far_ref, in_ref, out_ref):
    core = place_ref[0]
    near = near_ref[:, 0].astype(f32)
    far = far_ref[:, 0].astype(f32)
    first = jnp.where(core == 0, near, far)
    second = jnp.where(core == 0, far, near)
    lanes = first.shape[2]
    lane = lax.broadcasted_iota(jnp.int32, first.shape, 2)
    quarter = lanes // 2
    low = jnp.where(lane < quarter, first, pltpu.roll(second, quarter, 2))
    high = jnp.where(lane < quarter, pltpu.roll(first, quarter, 2), second)
    out_ref[:, 0, :, :lanes] = jnp.swapaxes(low, 0, 1)
    out_ref[:, 0, :, lanes:] = jnp.swapaxes(high, 0, 1)


def mirrored_rows(place, flip, near, far, out):
    rows, _, lags, cols = out.shape
    tasks = near.shape[1]
    step = 16
    back = pl.BlockSpec((lags, 1, step, near.shape[3]), lambda t, s, flip, place: (0, t, s, 0))
    return pl.pallas_call(
        mirrored_rows_kernel,
        out_shape=jax.ShapeDtypeStruct(out.shape, f32),
        grid_spec=pltpu.PrefetchScalarGridSpec(
            num_scalar_prefetch=2,
            grid=(tasks, rows // step),
            in_specs=[back, back, pl.BlockSpec(memory_space=pl.ANY)],
            out_specs=pl.BlockSpec(
                (step, 1, lags, cols),
                lambda t, s, flip, place: (s, 2 * t + 1 - flip[t, place[2]], 0, 0),
            ),
        ),
        input_output_aliases={4: 0},
        compiler_params=params(),
        name="mirrored_rows",
    )(flip, place, near, far, out)


def exchange(array):
    return lax.all_to_all(array, "pair", split_axis=0, concat_axis=0, tiled=True)


def after(array, *others):
    return lax.optimization_barrier((array,) + others)[0]


def local(spectra, channel_order, partners):
    num_bins, _, num_windows, cols = spectra.shape
    win_count = lax.axis_size("win")
    win = lax.axis_index("win")
    place = jnp.stack([win % 2, win // 2, lax.axis_index("pair")]).astype(jnp.int32)
    other_core = [(i, i ^ 1) for i in range(win_count)]
    other_chip = [(i, i ^ 2) for i in range(win_count)]
    norm = 1.0 / math.sqrt(num_windows * win_count * num_bins)
    tasks = ROUNDS // 2

    own = whiten(spectra, channel_order).reshape(num_bins, 2 * num_windows, cols)
    own_turned = turn(own)
    mate_of, back_of, flip = plan(partners)
    shares = exchange(own)
    arranged = list(gather(shares, mate_of))
    first = after(arranged[0], own_turned)
    mates = [exchange(first)] + [exchange(block) for block in arranged[1:]]
    parts, back, moved = [], [], []
    for task in range(tasks):
        keep, send = correlate(own_turned, mates[task], place, norm, LAGS + 1)
        recv = lax.ppermute(after(send, *moved), "win", other_core)
        near, far, turn_send, rest_send = core_sum(place, keep, recv)
        turn_recv = lax.ppermute(turn_send, "win", other_chip)
        if task + 1 < tasks:
            mates[task + 1] = after(mates[task + 1], turn_send)
            rest_recv = lax.ppermute(rest_send, "win", other_chip)
            moved = [turn_recv, rest_recv]
            back = [mirror(place, near, turn_recv, back)]
            out = own_rows(place, flip, task, near, far, turn_recv, rest_recv, None)
        else:
            turn_recv, out = lax.optimization_barrier((turn_recv, out))
            back = [mirror(place, near, turn_recv, back)]
            rest_recv = lax.ppermute(after(rest_send, turn_recv), "win", other_chip)
    spread = after(exchange(back[0]), rest_recv)
    out = own_rows(place, flip, tasks - 1, near, far, turn_recv, rest_recv, out)
    returned = after(exchange(gather_back(spread, back_of)), out)
    far = lax.ppermute(returned[LAGS:], "win", other_core)
    return mirrored_rows(place, flip, returned, far, out)[None]


def solution(mesh):
    return jax.shard_map(
        local,
        mesh=mesh,
        in_specs=(P(None, None, "win", "pair"), P("pair", None), P()),
        out_specs=P("pair", "win", None, None, None),
        check_vma=False,
    )
```

```python
import functools
import math

import jax
import jax.numpy as jnp
from jax import lax
from jax.experimental import pallas as pl
from jax.experimental.pallas import tpu as pltpu
from jax.sharding import PartitionSpec as P

LAGS = 16
ROUNDS = 4
VMEM_BYTES = 62 * 1024 * 1024
QUARTER_ORDER = (0, 2, 1, 3)
bf16 = jnp.bfloat16
f32 = jnp.float32


def params(**more):
    return pltpu.CompilerParams(vmem_limit_bytes=VMEM_BYTES, **more)


def whiten_kernel(order_ref, spectra_ref, out_ref):
    num_bins, _, rows, cols = spectra_ref.shape
    slots = lax.broadcasted_iota(jnp.int32, (cols, cols), 0)
    pick = (slots == order_ref[...]).astype(f32).astype(bf16)
    values = spectra_ref[...].astype(f32)
    power = values[:, 0] * values[:, 0] + values[:, 1] * values[:, 1]
    parts = []
    for f in range(num_bins):
        lo, hi = max(f - 2, 0), min(f + 2, num_bins - 1)
        total = power[lo]
        for g in range(lo + 1, hi + 1):
            total = total + power[g]
        inv_scale = jnp.minimum(lax.rsqrt(total * (1.0 / (hi - lo + 1))), 2.0)
        parts.append((values[f] * inv_scale[None]).astype(bf16).reshape(2 * rows, cols))
    flat = jnp.concatenate(parts, 0)
    ordered = jnp.dot(flat, pick, preferred_element_type=f32).astype(bf16)
    out_ref[...] = ordered.reshape(num_bins, 2, rows, cols)


def whiten(spectra, channel_order):
    num_bins, _, num_windows, cols = spectra.shape
    rows = 32
    return pl.pallas_call(
        whiten_kernel,
        grid=(num_windows // rows,),
        out_shape=jax.ShapeDtypeStruct(spectra.shape, bf16),
        in_specs=[
            pl.BlockSpec((1, cols), lambda s: (0, 0)),
            pl.BlockSpec((num_bins, 2, rows, cols), lambda s: (0, 0, s, 0)),
        ],
        out_specs=pl.BlockSpec((num_bins, 2, rows, cols), lambda s: (0, 0, s, 0)),
        compiler_params=params(),
        name="whiten",
    )(channel_order, spectra)


def turn_kernel(own_ref, out_ref):
    bins, _, cols = own_ref.shape
    quarter = cols // 4
    for f in range(bins):
        turned = own_ref[f].astype(f32).T.astype(bf16)
        for place, source in enumerate(QUARTER_ORDER):
            out_ref[f, place * quarter : (place + 1) * quarter, :] = turned[
                source * quarter : (source + 1) * quarter
            ]


def turn(own_rows):
    num_bins, depth, cols = own_rows.shape
    bins = 8
    return pl.pallas_call(
        turn_kernel,
        grid=(num_bins // bins,),
        out_shape=jax.ShapeDtypeStruct((num_bins, cols, depth), bf16),
        in_specs=[pl.BlockSpec((bins, depth, cols), lambda s: (s, 0, 0))],
        out_specs=pl.BlockSpec((bins, cols, depth), lambda s: (s, 0, 0)),
        compiler_params=params(),
        cost_estimate=pl.CostEstimate(flops=0, bytes_accessed=12_000_000, transcendentals=0),
        name="turn",
    )(own_rows)


def gather_kernel(index_ref, source_ref, *refs):
    *out_refs, sems = refs
    copies = []
    for group, out_ref in enumerate(out_refs):
        for place in range(out_ref.shape[0]):
            copy = pltpu.make_async_copy(
                source_ref.at[index_ref[group, place]], out_ref.at[place], sems.at[group, place]
            )
            copy.start()
            copies.append(copy)
    for copy in copies:
        copy.wait()


def gather(source, index):
    groups, places = index.shape
    return pl.pallas_call(
        gather_kernel,
        out_shape=[jax.ShapeDtypeStruct((places,) + source.shape[1:], source.dtype)] * groups,
        in_specs=[
            pl.BlockSpec(memory_space=pltpu.SMEM),
            pl.BlockSpec(memory_space=pltpu.VMEM),
        ],
        out_specs=[pl.BlockSpec(memory_space=pl.ANY)] * groups,
        scratch_shapes=[pltpu.SemaphoreType.DMA(index.shape)],
        compiler_params=params(),
        name="gather",
    )(index, source)


def weighted(terms):
    total = None
    for weight, value in terms:
        if abs(weight) < 1e-12:
            continue
        term = value * weight
        total = term if total is None else total + term
    return total


def lag_sums(real, imag, norm):
    cosine = lambda f, t: math.cos(math.pi * f * t / 32) * norm
    sine = lambda f, t: -math.sin(math.pi * f * t / 32) * norm
    even, odd = {}, {}
    low = {0: real(0), 16: real(16)}
    diff = {0: low[0]}
    for f in range(1, 16):
        a, b = real(f), real(32 - f)
        low[f], diff[f] = a + b, a - b
    for t in (1, 3, 5, 7):
        even[t] = weighted([(cosine(f, t), diff[f]) for f in range(16)])
    minus = {f: low[f] - low[16 - f] for f in range(8)}
    for t in (2, 6):
        even[t] = weighted([(cosine(f, t), minus[f]) for f in range(8)])
    plus = {f: low[f] + low[16 - f] for f in range(8)}
    plus[8] = low[8]
    even[4] = weighted([(cosine(f, 4), plus[f] - plus[8 - f]) for f in range(4)])
    sums = {f: plus[f] + plus[8 - f] for f in range(4)}
    sums[4] = plus[4]
    even[8] = weighted([(cosine(f, 8), sums[f]) for f in range(5)])
    total = sums[0]
    for f in range(1, 5):
        total = total + sums[f]
    even[0] = total * norm

    add = {16: imag(16)}
    sub = {}
    for f in range(1, 16):
        a, b = imag(f), imag(32 - f)
        add[f], sub[f] = a + b, a - b
    for t in (1, 3, 5, 7):
        odd[t] = weighted([(sine(f, t), add[f]) for f in range(1, 17)])
    sums = {f: sub[f] + sub[16 - f] for f in range(1, 8)}
    sums[8] = sub[8]
    for t in (2, 6):
        odd[t] = weighted([(sine(f, t), sums[f]) for f in range(1, 9)])
    minus = {f: sub[f] - sub[16 - f] for f in range(1, 8)}
    odd[4] = weighted(
        [(sine(f, 4), minus[f] + minus[8 - f]) for f in range(1, 4)] + [(sine(4, 4), minus[4])]
    )
    odd[8] = weighted([(sine(f, 8), minus[f] - minus[8 - f]) for f in range(1, 4)])
    return even, odd


def correlate_kernel(
    norm, place_ref, own_ref, mate_ref, keep_ref, send_ref, own, mate, cross, own_sems, mate_sems
):
    num_bins, slots, _ = own.shape
    chunks = own_sems.shape[0]
    bins = num_bins // chunks
    copies = []
    for chunk in range(chunks):
        where = pl.ds(chunk * bins, bins)
        pair = (
            pltpu.make_async_copy(own_ref.at[where], own.at[where], own_sems.at[chunk]),
            pltpu.make_async_copy(mate_ref.at[where], mate.at[where], mate_sems.at[chunk]),
        )
        for copy in pair:
            copy.start()
        copies.append(pair)
    for chunk in range(chunks):
        for copy in copies[chunk]:
            copy.wait()
        for f in range(chunk * bins, (chunk + 1) * bins):
            left, right = own[f], mate[f]
            half = right.shape[0] // 2
            turned = jnp.concatenate([right[half:], -right[:half]], 0)
            cross[f, :slots] = jnp.dot(left, right, preferred_element_type=f32)
            cross[f, slots:] = jnp.dot(left, turned, preferred_element_type=f32)

    lags, half, cols = keep_ref.shape
    core = place_ref[0]
    rows, lanes = 16, 128

    def part(out_ref, base):
        def body(chunk, carry):
            row = pl.multiple_of(chunk * rows, rows)
            where = pl.ds(pl.multiple_of(base + row, rows), rows)
            turned = pl.ds(pl.multiple_of(slots + base + row, rows), rows)
            for lane in range(0, cols, lanes):
                even, odd = lag_sums(
                    lambda f: cross[f, where, lane : lane + lanes],
                    lambda f: cross[f, turned, lane : lane + lanes],
                    norm,
                )
                for lag in range(lags):
                    t = lag - LAGS // 2
                    if t == 0:
                        value = even[0]
                    elif t > 0:
                        value = even[t] + odd[t]
                    else:
                        value = even[-t] - odd[-t]
                    out_ref[lag, pl.ds(row, rows), lane : lane + lanes] = value.astype(
                        out_ref.dtype
                    )
            return carry

        lax.fori_loop(0, half // rows, body, 0)

    part(keep_ref, core * half)
    part(send_ref, (1 - core) * half)


def correlate(own, mate, place, norm, lags):
    num_bins, slots, depth = own.shape
    cols = mate.shape[2]
    chunks = 8
    anywhere = pl.BlockSpec(memory_space=pl.ANY)
    vmem = pl.BlockSpec(memory_space=pltpu.VMEM)
    return pl.pallas_call(
        functools.partial(correlate_kernel, norm),
        out_shape=[
            jax.ShapeDtypeStruct((lags, slots // 2, cols), f32),
            jax.ShapeDtypeStruct((lags, slots // 2, cols), bf16),
        ],
        in_specs=[pl.BlockSpec(memory_space=pltpu.SMEM), anywhere, anywhere],
        out_specs=[vmem, vmem],
        scratch_shapes=[
            pltpu.VMEM(own.shape, bf16),
            pltpu.VMEM(mate.shape, bf16),
            pltpu.VMEM((num_bins, 2 * slots, cols), f32),
            pltpu.SemaphoreType.DMA((chunks,)),
            pltpu.SemaphoreType.DMA((chunks,)),
        ],
        compiler_params=params(),
        cost_estimate=pl.CostEstimate(
            flops=4 * num_bins * slots * depth * cols, bytes_accessed=20_000_000, transcendentals=0
        ),
        name="correlate",
    )(place, own, mate)


def plan_kernel(partners_ref, mate_ref, back_ref, flip_ref):
    rounds, blocks = partners_ref.shape
    for task in range(rounds // 2):
        first, second = 2 * task, 2 * task + 1

        def clear(block, carry):
            flip_ref[task, block] = -1
            return carry

        def walk(block):
            partner = partners_ref[first, block]
            flip_ref[task, block] = 0
            flip_ref[task, partner] = 1
            mate_ref[task, block] = partner
            back_ref[task, partner] = block
            following = partners_ref[second, partner]
            mate_ref[task, partner] = following
            back_ref[task, following] = partner
            return following

        def start(block, carry):
            lax.while_loop(lambda block: flip_ref[task, block] < 0, walk, block)
            return carry

        lax.fori_loop(0, blocks, clear, 0)
        lax.fori_loop(0, blocks, start, 0)


def plan(partners):
    rounds, blocks = partners.shape
    smem = pl.BlockSpec(memory_space=pltpu.SMEM)
    table = jax.ShapeDtypeStruct((rounds // 2, blocks), jnp.int32)
    return pl.pallas_call(
        plan_kernel,
        out_shape=[table] * 3,
        in_specs=[smem],
        out_specs=[smem] * 3,
        compiler_params=params(),
        name="plan",
    )(partners)


def core_sum_kernel(place_ref, keep_ref, recv_ref, *refs):
    own_ref, send_ref, piece_ref = refs[-3:]
    core, chip = place_ref[0], place_ref[1]
    lags, rows, cols = own_ref.shape
    own_rows = pl.ds(pl.multiple_of(chip * rows, rows), rows)
    other_rows = pl.ds(pl.multiple_of((1 - chip) * rows, rows), rows)
    for lag in range(lags + 1):
        if lag < lags:
            own_ref[lag] = keep_ref[lag, own_rows, :] + recv_ref[lag, own_rows, :].astype(f32)
            send_ref[lag] = (
                keep_ref[lag, other_rows, :] + recv_ref[lag, other_rows, :].astype(f32)
            ).astype(bf16)
        if lag > 0:
            back = lags - lag
            turned = (keep_ref[lag] + recv_ref[lag].astype(f32)).T
            for half in range(2):
                low = turned[2 * half * rows : (2 * half + 1) * rows]
                high = turned[(2 * half + 1) * rows : (2 * half + 2) * rows]
                base = 2 * half * lags + back
                piece_ref[base, 0] = jnp.where(core == 0, low, high).astype(bf16)
                piece_ref[base + lags, 0] = jnp.where(core == 0, high, low).astype(bf16)


def core_sum(place, keep, recv, task, tasks, pieces):
    lags, rows, cols = keep.shape
    vmem = pl.BlockSpec(memory_space=pltpu.VMEM)
    count = 4 * (lags - 1)
    shape = (count, tasks, cols // 4, rows)
    whole = pl.BlockSpec((lags - 1, rows // 2, cols), lambda s: (0, 0, 0))
    given = pl.BlockSpec((lags, rows, cols), lambda s: (0, 0, 0))
    extra = [] if pieces is None else [pieces]
    return pl.pallas_call(
        core_sum_kernel,
        grid=(1,),
        out_shape=[
            jax.ShapeDtypeStruct((lags - 1, rows // 2, cols), f32),
            jax.ShapeDtypeStruct((lags - 1, rows // 2, cols), bf16),
            jax.ShapeDtypeStruct(shape, bf16),
        ],
        in_specs=[pl.BlockSpec(memory_space=pltpu.SMEM), given, given]
        + [pl.BlockSpec(memory_space=pl.ANY)] * len(extra),
        out_specs=[
            whole,
            whole,
            pl.BlockSpec((count, 1) + shape[2:], lambda s: (0, task, 0, 0)),
        ],
        input_output_aliases={3: 2} if extra else {},
        compiler_params=params(),
        cost_estimate=pl.CostEstimate(flops=0, bytes_accessed=12_000_000, transcendentals=0),
        name="core_sum",
    )(place, keep, recv, *extra)


def gather_sum_kernel(index_ref, spread_ref, out_ref):
    places, tasks = out_ref.shape[:2]

    def body(place, carry):
        for task in range(tasks):
            source = index_ref[task, place]
            out_ref[place, task] = (
                spread_ref[source, task].astype(f32)
                + spread_ref[places + source, task].astype(f32)
            ).astype(bf16)
        return carry

    lax.fori_loop(0, places, body, 0, unroll=4)


def gather_sum(index, spread):
    places = index.shape[1]
    vmem = pl.BlockSpec(memory_space=pltpu.VMEM)
    return pl.pallas_call(
        gather_sum_kernel,
        out_shape=jax.ShapeDtypeStruct((places,) + spread.shape[1:], bf16),
        in_specs=[pl.BlockSpec(memory_space=pltpu.SMEM), vmem],
        out_specs=vmem,
        compiler_params=params(),
        name="gather_sum",
    )(index, spread)


def own_rows_kernel(flip_ref, place_ref, own_ref, recv_ref, *refs):
    out_ref = refs[-1]
    out_ref[:, 0] = jnp.swapaxes(own_ref[...] + recv_ref[...].astype(f32), 0, 1)


def own_rows(place, flip, task, own, recv, out):
    lags, rows, cols = own.shape
    step = 16
    extra = [] if out is None else [out]
    piece = pl.BlockSpec((lags, step, cols), lambda s, flip, place: (0, s, 0))
    return pl.pallas_call(
        own_rows_kernel,
        out_shape=jax.ShapeDtypeStruct((rows, ROUNDS, lags, cols), f32),
        grid_spec=pltpu.PrefetchScalarGridSpec(
            num_scalar_prefetch=2,
            grid=(rows // step,),
            in_specs=[piece, piece] + [pl.BlockSpec(memory_space=pl.ANY)] * len(extra),
            out_specs=pl.BlockSpec(
                (step, 1, lags, cols),
                lambda s, flip, place: (s, 2 * task + flip[task, place[2]], 0, 0),
            ),
        ),
        input_output_aliases={4: 0} if extra else {},
        compiler_params=params(),
        cost_estimate=pl.CostEstimate(flops=0, bytes_accessed=5_000_000, transcendentals=0),
        name="own_rows",
    )(flip, place, own, recv, *extra)


def mirrored_rows_kernel(flip_ref, place_ref, near_ref, far_ref, in_ref, out_ref):
    core = place_ref[0]
    near = near_ref[:, 0].astype(f32)
    far = far_ref[:, 0].astype(f32)
    first = jnp.where(core == 0, near, far)
    second = jnp.where(core == 0, far, near)
    lanes = first.shape[2]
    lane = lax.broadcasted_iota(jnp.int32, first.shape, 2)
    quarter = lanes // 2
    low = jnp.where(lane < quarter, first, pltpu.roll(second, quarter, 2))
    high = jnp.where(lane < quarter, pltpu.roll(first, quarter, 2), second)
    out_ref[:, 0, :, :lanes] = jnp.swapaxes(low, 0, 1)
    out_ref[:, 0, :, lanes:] = jnp.swapaxes(high, 0, 1)


def mirrored_rows(place, flip, near, far, out):
    rows, _, lags, cols = out.shape
    tasks = near.shape[1]
    step = 32
    back = pl.BlockSpec((lags, 1, step, near.shape[3]), lambda t, s, flip, place: (0, t, s, 0))
    return pl.pallas_call(
        mirrored_rows_kernel,
        out_shape=jax.ShapeDtypeStruct(out.shape, f32),
        grid_spec=pltpu.PrefetchScalarGridSpec(
            num_scalar_prefetch=2,
            grid=(tasks, rows // step),
            in_specs=[back, back, pl.BlockSpec(memory_space=pl.ANY)],
            out_specs=pl.BlockSpec(
                (step, 1, lags, cols),
                lambda t, s, flip, place: (s, 2 * t + 1 - flip[t, place[2]], 0, 0),
            ),
        ),
        input_output_aliases={4: 0},
        compiler_params=params(),
        name="mirrored_rows",
    )(flip, place, near, far, out)


def exchange(array):
    return lax.all_to_all(array, "pair", split_axis=0, concat_axis=0, tiled=True)


def after(array, *others):
    return lax.optimization_barrier((array,) + others)[0]


def local(spectra, channel_order, partners):
    num_bins, _, num_windows, cols = spectra.shape
    win_count = lax.axis_size("win")
    win = lax.axis_index("win")
    place = jnp.stack([win % 2, win // 2, lax.axis_index("pair")]).astype(jnp.int32)
    other_core = [(i, i ^ 1) for i in range(win_count)]
    other_chip = [(i, i ^ 2) for i in range(win_count)]
    norm = 1.0 / math.sqrt(num_windows * win_count * num_bins)
    tasks = ROUNDS // 2
    num_blocks = lax.axis_size("pair")

    own = whiten(spectra, channel_order).reshape(num_bins, 2 * num_windows, cols)
    own_turned = turn(own)
    mate_of, back_of, flip = plan(partners)
    shares = exchange(own)
    arranged = gather(shares, mate_of)
    mates = [exchange(after(arranged[0], own_turned)), exchange(arranged[1])]
    groups = [
        [(block * 2 + chip_index) * 2 + core_index for chip_index in range(2) for block in range(num_blocks)]
        for core_index in range(2)
    ]
    rows, moved, pieces = [], [], None
    for task in range(tasks):
        keep, send = correlate(own_turned, mates[task], place, norm, LAGS + 1)
        recv = lax.ppermute(after(send, *moved), "win", other_core)
        own_sum, row_send, pieces = core_sum(place, keep, recv, task, tasks, pieces)
        if task + 1 < tasks:
            mates[task + 1] = after(mates[task + 1], row_send)
        if task + 1 < tasks:
            rows.append((own_sum, lax.ppermute(row_send, "win", other_chip)))
            moved = [rows[task][1]]
    out = own_rows(place, flip, 0, *rows[0], None)
    spread = lax.all_to_all(
        after(pieces, out), ("pair", "win"), 0, 0, tiled=True, axis_index_groups=groups
    )
    row_recv = lax.ppermute(row_send, "win", other_chip)
    returned = exchange(after(gather_sum(back_of, spread), row_recv))
    out = own_rows(place, flip, 1, own_sum, row_recv, out)
    returned = after(returned, out)
    far = lax.ppermute(returned[LAGS:], "win", other_core)
    return mirrored_rows(place, flip, returned, far, out)[None]


def solution(mesh):
    return jax.shard_map(
        local,
        mesh=mesh,
        in_specs=(P(None, None, "win", "pair"), P("pair", None), P()),
        out_specs=P("pair", "win", None, None, None),
        check_vma=False,
    )
```

```python
import functools
import math

import jax
import jax.numpy as jnp
from jax import lax
from jax.experimental import pallas as pl
from jax.experimental.pallas import tpu as pltpu
from jax.sharding import PartitionSpec as P

LAGS = 16
ROUNDS = 4
VMEM_BYTES = 62 * 1024 * 1024
QUARTER_ORDER = (0, 2, 1, 3)
bf16 = jnp.bfloat16
f32 = jnp.float32


def params(**more):
    return pltpu.CompilerParams(vmem_limit_bytes=VMEM_BYTES, **more)


def whiten_kernel(order_ref, spectra_ref, out_ref):
    num_bins, _, rows, cols = spectra_ref.shape
    slots = lax.broadcasted_iota(jnp.int32, (cols, cols), 0)
    pick = (slots == order_ref[...]).astype(f32).astype(bf16)
    values = spectra_ref[...].astype(f32)
    power = values[:, 0] * values[:, 0] + values[:, 1] * values[:, 1]
    parts = []
    for f in range(num_bins):
        lo, hi = max(f - 2, 0), min(f + 2, num_bins - 1)
        total = power[lo]
        for g in range(lo + 1, hi + 1):
            total = total + power[g]
        inv_scale = jnp.minimum(lax.rsqrt(total * (1.0 / (hi - lo + 1))), 2.0)
        parts.append((values[f] * inv_scale[None]).astype(bf16).reshape(2 * rows, cols))
    flat = jnp.concatenate(parts, 0)
    ordered = jnp.dot(flat, pick, preferred_element_type=f32).astype(bf16)
    out_ref[...] = ordered.reshape(num_bins, 2, rows, cols)


def whiten(spectra, channel_order):
    num_bins, _, num_windows, cols = spectra.shape
    rows = 48
    return pl.pallas_call(
        whiten_kernel,
        grid=(num_windows // rows,),
        out_shape=jax.ShapeDtypeStruct(spectra.shape, bf16),
        in_specs=[
            pl.BlockSpec((1, cols), lambda s: (0, 0)),
            pl.BlockSpec((num_bins, 2, rows, cols), lambda s: (0, 0, s, 0)),
        ],
        out_specs=pl.BlockSpec((num_bins, 2, rows, cols), lambda s: (0, 0, s, 0)),
        compiler_params=params(),
        name="whiten",
    )(channel_order, spectra)


def turn_kernel(own_ref, out_ref):
    bins, _, cols = own_ref.shape
    quarter = cols // 4
    for f in range(bins):
        turned = own_ref[f].astype(f32).T.astype(bf16)
        for place, source in enumerate(QUARTER_ORDER):
            out_ref[f, place * quarter : (place + 1) * quarter, :] = turned[
                source * quarter : (source + 1) * quarter
            ]


def turn(own_rows):
    num_bins, depth, cols = own_rows.shape
    bins = 8
    return pl.pallas_call(
        turn_kernel,
        grid=(num_bins // bins,),
        out_shape=jax.ShapeDtypeStruct((num_bins, cols, depth), bf16),
        in_specs=[pl.BlockSpec((bins, depth, cols), lambda s: (s, 0, 0))],
        out_specs=pl.BlockSpec((bins, cols, depth), lambda s: (s, 0, 0)),
        compiler_params=params(),
        cost_estimate=pl.CostEstimate(flops=0, bytes_accessed=12_000_000, transcendentals=0),
        name="turn",
    )(own_rows)


def gather_kernel(index_ref, source_ref, *refs):
    *out_refs, arranged, sems = refs
    places = source_ref.shape[0]
    chunks = sems.shape[1]
    step = places // chunks
    copies = []
    for group, out_ref in enumerate(out_refs):
        for chunk in range(chunks):

            def body(place, carry):
                arranged[group, place] = source_ref[index_ref[group, place]]
                return carry

            lax.fori_loop(chunk * step, (chunk + 1) * step, body, 0)
            where = pl.ds(chunk * step, step)
            copy = pltpu.make_async_copy(
                arranged.at[group, where], out_ref.at[where], sems.at[group, chunk]
            )
            copy.start()
            copies.append(copy)
    for copy in copies:
        copy.wait()


def gather(source, index):
    groups = index.shape[0]
    anywhere = pl.BlockSpec(memory_space=pl.ANY)
    return pl.pallas_call(
        gather_kernel,
        out_shape=[jax.ShapeDtypeStruct(source.shape, source.dtype)] * groups,
        in_specs=[
            pl.BlockSpec(memory_space=pltpu.SMEM),
            pl.BlockSpec(memory_space=pltpu.VMEM),
        ],
        out_specs=[anywhere] * groups,
        scratch_shapes=[
            pltpu.VMEM((groups,) + source.shape, source.dtype),
            pltpu.SemaphoreType.DMA((groups, 4)),
        ],
        compiler_params=params(),
        name="gather",
    )(index, source)


def weighted(terms):
    total = None
    for weight, value in terms:
        if abs(weight) < 1e-12:
            continue
        term = value * weight
        total = term if total is None else total + term
    return total


def lag_sums(real, imag, norm):
    cosine = lambda f, t: math.cos(math.pi * f * t / 32) * norm
    sine = lambda f, t: -math.sin(math.pi * f * t / 32) * norm
    even, odd = {}, {}
    low = {0: real(0), 16: real(16)}
    diff = {0: low[0]}
    for f in range(1, 16):
        a, b = real(f), real(32 - f)
        low[f], diff[f] = a + b, a - b
    for t in (1, 3, 5, 7):
        even[t] = weighted([(cosine(f, t), diff[f]) for f in range(16)])
    minus = {f: low[f] - low[16 - f] for f in range(8)}
    for t in (2, 6):
        even[t] = weighted([(cosine(f, t), minus[f]) for f in range(8)])
    plus = {f: low[f] + low[16 - f] for f in range(8)}
    plus[8] = low[8]
    even[4] = weighted([(cosine(f, 4), plus[f] - plus[8 - f]) for f in range(4)])
    sums = {f: plus[f] + plus[8 - f] for f in range(4)}
    sums[4] = plus[4]
    even[8] = weighted([(cosine(f, 8), sums[f]) for f in range(5)])
    total = sums[0]
    for f in range(1, 5):
        total = total + sums[f]
    even[0] = total * norm

    add = {16: imag(16)}
    sub = {}
    for f in range(1, 16):
        a, b = imag(f), imag(32 - f)
        add[f], sub[f] = a + b, a - b
    for t in (1, 3, 5, 7):
        odd[t] = weighted([(sine(f, t), add[f]) for f in range(1, 17)])
    sums = {f: sub[f] + sub[16 - f] for f in range(1, 8)}
    sums[8] = sub[8]
    for t in (2, 6):
        odd[t] = weighted([(sine(f, t), sums[f]) for f in range(1, 9)])
    minus = {f: sub[f] - sub[16 - f] for f in range(1, 8)}
    odd[4] = weighted(
        [(sine(f, 4), minus[f] + minus[8 - f]) for f in range(1, 4)] + [(sine(4, 4), minus[4])]
    )
    odd[8] = weighted([(sine(f, 8), minus[f] - minus[8 - f]) for f in range(1, 4)])
    return even, odd


def correlate_kernel(
    norm, place_ref, own_ref, mate_ref, keep_ref, send_ref, own, mate, cross, own_sems, mate_sems
):
    num_bins, slots, _ = own.shape
    chunks = own_sems.shape[0]
    bins = num_bins // chunks
    copies = []
    for chunk in range(chunks):
        where = pl.ds(chunk * bins, bins)
        pair = (
            pltpu.make_async_copy(own_ref.at[where], own.at[where], own_sems.at[chunk]),
            pltpu.make_async_copy(mate_ref.at[where], mate.at[where], mate_sems.at[chunk]),
        )
        for copy in pair:
            copy.start()
        copies.append(pair)
    for chunk in range(chunks):
        for copy in copies[chunk]:
            copy.wait()
        for f in range(chunk * bins, (chunk + 1) * bins):
            left, right = own[f], mate[f]
            half = right.shape[0] // 2
            turned = jnp.concatenate([right[half:], -right[:half]], 0)
            cross[f, :slots] = jnp.dot(left, right, preferred_element_type=f32)
            cross[f, slots:] = jnp.dot(left, turned, preferred_element_type=f32)

    lags, half, cols = keep_ref.shape
    core = place_ref[0]
    rows, lanes = 16, 128

    def part(out_ref, base):
        def body(chunk, carry):
            row = pl.multiple_of(chunk * rows, rows)
            where = pl.ds(pl.multiple_of(base + row, rows), rows)
            turned = pl.ds(pl.multiple_of(slots + base + row, rows), rows)
            for lane in range(0, cols, lanes):
                even, odd = lag_sums(
                    lambda f: cross[f, where, lane : lane + lanes],
                    lambda f: cross[f, turned, lane : lane + lanes],
                    norm,
                )
                for lag in range(lags):
                    t = lag - LAGS // 2
                    if t == 0:
                        value = even[0]
                    elif t > 0:
                        value = even[t] + odd[t]
                    else:
                        value = even[-t] - odd[-t]
                    out_ref[lag, pl.ds(row, rows), lane : lane + lanes] = value.astype(
                        out_ref.dtype
                    )
            return carry

        lax.fori_loop(0, half // rows, body, 0)

    part(keep_ref, core * half)
    part(send_ref, (1 - core) * half)


def correlate(own, mate, place, norm, lags):
    num_bins, slots, depth = own.shape
    cols = mate.shape[2]
    chunks = 8
    anywhere = pl.BlockSpec(memory_space=pl.ANY)
    vmem = pl.BlockSpec(memory_space=pltpu.VMEM)
    return pl.pallas_call(
        functools.partial(correlate_kernel, norm),
        out_shape=[
            jax.ShapeDtypeStruct((lags, slots // 2, cols), f32),
            jax.ShapeDtypeStruct((lags, slots // 2, cols), bf16),
        ],
        in_specs=[pl.BlockSpec(memory_space=pltpu.SMEM), anywhere, anywhere],
        out_specs=[vmem, vmem],
        scratch_shapes=[
            pltpu.VMEM(own.shape, bf16),
            pltpu.VMEM(mate.shape, bf16),
            pltpu.VMEM((num_bins, 2 * slots, cols), f32),
            pltpu.SemaphoreType.DMA((chunks,)),
            pltpu.SemaphoreType.DMA((chunks,)),
        ],
        compiler_params=params(),
        cost_estimate=pl.CostEstimate(
            flops=4 * num_bins * slots * depth * cols, bytes_accessed=20_000_000, transcendentals=0
        ),
        name="correlate",
    )(place, own, mate)


def plan_kernel(partners_ref, mate_ref, back_ref, flip_ref):
    rounds, blocks = partners_ref.shape
    for task in range(rounds // 2):
        first, second = 2 * task, 2 * task + 1

        def clear(block, carry):
            flip_ref[task, block] = -1
            return carry

        def walk(block):
            partner = partners_ref[first, block]
            flip_ref[task, block] = 0
            flip_ref[task, partner] = 1
            mate_ref[task, block] = partner
            back_ref[task, partner] = block
            following = partners_ref[second, partner]
            mate_ref[task, partner] = following
            back_ref[task, following] = partner
            return following

        def start(block, carry):
            lax.while_loop(lambda block: flip_ref[task, block] < 0, walk, block)
            return carry

        lax.fori_loop(0, blocks, clear, 0)
        lax.fori_loop(0, blocks, start, 0)


def plan(partners):
    rounds, blocks = partners.shape
    smem = pl.BlockSpec(memory_space=pltpu.SMEM)
    table = jax.ShapeDtypeStruct((rounds // 2, blocks), jnp.int32)
    return pl.pallas_call(
        plan_kernel,
        out_shape=[table] * 3,
        in_specs=[smem],
        out_specs=[smem] * 3,
        compiler_params=params(),
        name="plan",
    )(partners)


def core_sum_kernel(task, place_ref, keep_ref, recv_ref, *refs):
    own_ref, send_ref, piece_ref, keep, recv, own, send, piece, in_sems, out_sems, piece_sems = refs[-11:]
    core, chip = place_ref[0], place_ref[1]
    lags, rows, cols = own.shape
    own_rows = pl.ds(pl.multiple_of(chip * rows, rows), rows)
    other_rows = pl.ds(pl.multiple_of((1 - chip) * rows, rows), rows)
    chunks = in_sems.shape[1]
    step = lags // chunks
    bounds = [0] + [chunk * step + 1 for chunk in range(1, chunks)] + [lags + 1]
    arrivals, departures = [], []
    for chunk in range(chunks):
        where = pl.ds(bounds[chunk], bounds[chunk + 1] - bounds[chunk])
        pair = (
            pltpu.make_async_copy(keep_ref.at[where], keep.at[where], in_sems.at[0, chunk]),
            pltpu.make_async_copy(recv_ref.at[where], recv.at[where], in_sems.at[1, chunk]),
        )
        for copy in pair:
            copy.start()
        arrivals.append(pair)

    def leave(source, target, sem):
        copy = pltpu.make_async_copy(source, target, sem)
        copy.start()
        departures.append(copy)

    for chunk in range(chunks):
        for copy in arrivals[chunk]:
            copy.wait()
        first, last = bounds[chunk], bounds[chunk + 1]
        for lag in range(first, min(last, lags)):
            own[lag] = keep[lag, own_rows, :] + recv[lag, own_rows, :].astype(f32)
            send[lag] = (keep[lag, other_rows, :] + recv[lag, other_rows, :].astype(f32)).astype(
                bf16
            )
        for lag in range(max(first, 1), last):
            back = lags - lag
            turned = (keep[lag] + recv[lag].astype(f32)).T
            for half in range(2):
                low = turned[2 * half * rows : (2 * half + 1) * rows]
                high = turned[(2 * half + 1) * rows : (2 * half + 2) * rows]
                base = 2 * half * lags + back
                piece[base] = jnp.where(core == 0, low, high).astype(bf16)
                piece[base + lags] = jnp.where(core == 0, high, low).astype(bf16)
        where = pl.ds(first, min(last, lags) - first)
        leave(own.at[where], own_ref.at[where], out_sems.at[0, chunk])
        leave(send.at[where], send_ref.at[where], out_sems.at[1, chunk])
        for group in range(4):
            where = pl.ds(group * lags + lags - last + 1, step)
            leave(piece.at[where], piece_ref.at[where, task], piece_sems.at[group, chunk])
    for copy in departures:
        copy.wait()


def core_sum(place, keep, recv, task, tasks, pieces):
    lags, rows, cols = keep.shape
    anywhere = pl.BlockSpec(memory_space=pl.ANY)
    count = 4 * (lags - 1)
    part = (lags - 1, rows // 2, cols)
    piece = (cols // 4, rows)
    extra = [] if pieces is None else [pieces]
    return pl.pallas_call(
        functools.partial(core_sum_kernel, task),
        out_shape=[
            jax.ShapeDtypeStruct(part, f32),
            jax.ShapeDtypeStruct(part, bf16),
            jax.ShapeDtypeStruct((count, tasks) + piece, bf16),
        ],
        in_specs=[pl.BlockSpec(memory_space=pltpu.SMEM)] + [anywhere] * (2 + len(extra)),
        out_specs=[anywhere] * 3,
        scratch_shapes=[
            pltpu.VMEM(keep.shape, f32),
            pltpu.VMEM(keep.shape, bf16),
            pltpu.VMEM(part, f32),
            pltpu.VMEM(part, bf16),
            pltpu.VMEM((count,) + piece, bf16),
            pltpu.SemaphoreType.DMA((2, 4)),
            pltpu.SemaphoreType.DMA((2, 4)),
            pltpu.SemaphoreType.DMA((4, 4)),
        ],
        input_output_aliases={3: 2} if extra else {},
        compiler_params=params(),
        cost_estimate=pl.CostEstimate(flops=0, bytes_accessed=12_000_000, transcendentals=0),
        name="core_sum",
    )(place, keep, recv, *extra)


def gather_sum_kernel(index_ref, spread_ref, out_ref):
    places, tasks = out_ref.shape[:2]

    def body(place, carry):
        for task in range(tasks):
            source = index_ref[task, place]
            out_ref[place, task] = (
                spread_ref[source, task].astype(f32)
                + spread_ref[places + source, task].astype(f32)
            ).astype(bf16)
        return carry

    lax.fori_loop(0, places, body, 0, unroll=4)


def gather_sum(index, spread):
    places = index.shape[1]
    vmem = pl.BlockSpec(memory_space=pltpu.VMEM)
    return pl.pallas_call(
        gather_sum_kernel,
        out_shape=jax.ShapeDtypeStruct((places,) + spread.shape[1:], bf16),
        in_specs=[pl.BlockSpec(memory_space=pltpu.SMEM), vmem],
        out_specs=vmem,
        compiler_params=params(),
        name="gather_sum",
    )(index, spread)


def own_rows_kernel(flip_ref, place_ref, own_ref, recv_ref, *refs):
    out_ref = refs[-1]
    out_ref[:, 0] = jnp.swapaxes(own_ref[...] + recv_ref[...].astype(f32), 0, 1)


def own_rows(place, flip, task, own, recv, out):
    lags, rows, cols = own.shape
    step = 64
    extra = [] if out is None else [out]
    piece = pl.BlockSpec((lags, step, cols), lambda s, flip, place: (0, s, 0))
    return pl.pallas_call(
        own_rows_kernel,
        out_shape=jax.ShapeDtypeStruct((rows, ROUNDS, lags, cols), f32),
        grid_spec=pltpu.PrefetchScalarGridSpec(
            num_scalar_prefetch=2,
            grid=(rows // step,),
            in_specs=[piece, piece] + [pl.BlockSpec(memory_space=pl.ANY)] * len(extra),
            out_specs=pl.BlockSpec(
                (step, 1, lags, cols),
                lambda s, flip, place: (s, 2 * task + flip[task, place[2]], 0, 0),
            ),
        ),
        input_output_aliases={4: 0} if extra else {},
        compiler_params=params(),
        cost_estimate=pl.CostEstimate(flops=0, bytes_accessed=5_000_000, transcendentals=0),
        name="own_rows",
    )(flip, place, own, recv, *extra)


def mirrored_rows_kernel(flip_ref, place_ref, near_ref, far_ref, in_ref, out_ref):
    core = place_ref[0]
    near = near_ref[:, 0].astype(f32)
    far = far_ref[:, 0].astype(f32)
    first = jnp.where(core == 0, near, far)
    second = jnp.where(core == 0, far, near)
    lanes = first.shape[2]
    lane = lax.broadcasted_iota(jnp.int32, first.shape, 2)
    quarter = lanes // 2
    low = jnp.where(lane < quarter, first, pltpu.roll(second, quarter, 2))
    high = jnp.where(lane < quarter, pltpu.roll(first, quarter, 2), second)
    out_ref[:, 0, :, :lanes] = jnp.swapaxes(low, 0, 1)
    out_ref[:, 0, :, lanes:] = jnp.swapaxes(high, 0, 1)


def mirrored_rows(place, flip, near, far, out):
    rows, _, lags, cols = out.shape
    tasks = near.shape[1]
    step = 64
    back = pl.BlockSpec((lags, 1, step, near.shape[3]), lambda t, s, flip, place: (0, t, s, 0))
    return pl.pallas_call(
        mirrored_rows_kernel,
        out_shape=jax.ShapeDtypeStruct(out.shape, f32),
        grid_spec=pltpu.PrefetchScalarGridSpec(
            num_scalar_prefetch=2,
            grid=(tasks, rows // step),
            in_specs=[back, back, pl.BlockSpec(memory_space=pl.ANY)],
            out_specs=pl.BlockSpec(
                (step, 1, lags, cols),
                lambda t, s, flip, place: (s, 2 * t + 1 - flip[t, place[2]], 0, 0),
            ),
        ),
        input_output_aliases={4: 0},
        compiler_params=params(),
        name="mirrored_rows",
    )(flip, place, near, far, out)


def exchange(array):
    return lax.all_to_all(array, "pair", split_axis=0, concat_axis=0, tiled=True)


def after(array, *others):
    return lax.optimization_barrier((array,) + others)[0]


def local(spectra, channel_order, partners):
    num_bins, _, num_windows, cols = spectra.shape
    win_count = lax.axis_size("win")
    win = lax.axis_index("win")
    place = jnp.stack([win % 2, win // 2, lax.axis_index("pair")]).astype(jnp.int32)
    other_core = [(i, i ^ 1) for i in range(win_count)]
    other_chip = [(i, i ^ 2) for i in range(win_count)]
    norm = 1.0 / math.sqrt(num_windows * win_count * num_bins)
    tasks = ROUNDS // 2
    num_blocks = lax.axis_size("pair")

    own = whiten(spectra, channel_order).reshape(num_bins, 2 * num_windows, cols)
    own_turned = turn(own)
    mate_of, back_of, flip = plan(partners)
    shares = exchange(own)
    arranged = gather(shares, mate_of)
    mates = [exchange(after(arranged[0], own_turned)), exchange(arranged[1])]
    groups = [
        [(block * 2 + chip_index) * 2 + core_index for chip_index in range(2) for block in range(num_blocks)]
        for core_index in range(2)
    ]
    rows, moved, pieces = [], [], None
    for task in range(tasks):
        keep, send = correlate(own_turned, mates[task], place, norm, LAGS + 1)
        recv = lax.ppermute(after(send, *moved), "win", other_core)
        own_sum, row_send, pieces = core_sum(place, keep, recv, task, tasks, pieces)
        if task + 1 < tasks:
            mates[task + 1] = after(mates[task + 1], row_send)
        if task + 1 < tasks:
            rows.append((own_sum, lax.ppermute(row_send, "win", other_chip)))
            moved = [rows[task][1]]
    out = own_rows(place, flip, 0, *rows[0], None)
    spread = lax.all_to_all(
        pieces, ("pair", "win"), 0, 0, tiled=True, axis_index_groups=groups
    )
    spread = after(spread, out)
    row_recv = lax.ppermute(row_send, "win", other_chip)
    returned = exchange(gather_sum(back_of, spread))
    out = own_rows(place, flip, 1, own_sum, row_recv, out)
    far = lax.ppermute(returned[LAGS:], "win", other_core)
    return mirrored_rows(place, flip, returned, far, out)[None]


def solution(mesh):
    return jax.shard_map(
        local,
        mesh=mesh,
        in_specs=(P(None, None, "win", "pair"), P("pair", None), P()),
        out_specs=P("pair", "win", None, None, None),
        check_vma=False,
    )
```

```python
import functools
import math

import jax
import jax.numpy as jnp
from jax import lax
from jax.experimental import pallas as pl
from jax.experimental.pallas import tpu as pltpu
from jax.sharding import PartitionSpec as P

LAGS = 16
ROUNDS = 4
VMEM_BYTES = 63 * 1024 * 1024
QUARTER_ORDER = (0, 2, 1, 3)
bf16 = jnp.bfloat16
f32 = jnp.float32


def params(**more):
    return pltpu.CompilerParams(vmem_limit_bytes=VMEM_BYTES, **more)


def whiten_kernel(order_ref, spectra_ref, out_ref):
    num_bins, _, rows, cols = spectra_ref.shape
    slots = lax.broadcasted_iota(jnp.int32, (cols, cols), 0)
    pick = (slots == order_ref[...]).astype(f32).astype(bf16)
    values = spectra_ref[...].astype(f32)
    power = values[:, 0] * values[:, 0] + values[:, 1] * values[:, 1]
    parts = []
    for f in range(num_bins):
        lo, hi = max(f - 2, 0), min(f + 2, num_bins - 1)
        total = power[lo]
        for g in range(lo + 1, hi + 1):
            total = total + power[g]
        inv_scale = jnp.minimum(lax.rsqrt(total * (1.0 / (hi - lo + 1))), 2.0)
        parts.append((values[f] * inv_scale[None]).astype(bf16).reshape(2 * rows, cols))
    flat = jnp.concatenate(parts, 0)
    ordered = jnp.dot(flat, pick, preferred_element_type=f32).astype(bf16)
    out_ref[...] = ordered.reshape(num_bins, 2, rows, cols)


def whiten(spectra, channel_order):
    num_bins, _, num_windows, cols = spectra.shape
    rows = 48
    return pl.pallas_call(
        whiten_kernel,
        grid=(num_windows // rows,),
        out_shape=jax.ShapeDtypeStruct(spectra.shape, bf16),
        in_specs=[
            pl.BlockSpec((1, cols), lambda s: (0, 0)),
            pl.BlockSpec((num_bins, 2, rows, cols), lambda s: (0, 0, s, 0)),
        ],
        out_specs=pl.BlockSpec((num_bins, 2, rows, cols), lambda s: (0, 0, s, 0)),
        compiler_params=params(),
        name="whiten",
    )(channel_order, spectra)


def turn_kernel(own_ref, out_ref):
    bins, _, cols = own_ref.shape
    quarter = cols // 4
    for f in range(bins):
        turned = own_ref[f].astype(f32).T.astype(bf16)
        for place, source in enumerate(QUARTER_ORDER):
            out_ref[f, place * quarter : (place + 1) * quarter, :] = turned[
                source * quarter : (source + 1) * quarter
            ]


def turn(own_rows):
    num_bins, depth, cols = own_rows.shape
    bins = 8
    return pl.pallas_call(
        turn_kernel,
        grid=(num_bins // bins,),
        out_shape=jax.ShapeDtypeStruct((num_bins, cols, depth), bf16),
        in_specs=[pl.BlockSpec((bins, depth, cols), lambda s: (s, 0, 0))],
        out_specs=pl.BlockSpec((bins, cols, depth), lambda s: (s, 0, 0)),
        compiler_params=params(),
        cost_estimate=pl.CostEstimate(flops=0, bytes_accessed=12_000_000, transcendentals=0),
        name="turn",
    )(own_rows)


def plan_task(task, partners_ref, mate_ref, back_ref, flip_ref):
    blocks = partners_ref.shape[1]
    first, second = 2 * task, 2 * task + 1
    for block in range(blocks):
        flip_ref[task, block] = -1

    def walk(block):
        partner = partners_ref[first, block]
        following = partners_ref[second, partner]
        flip_ref[task, block] = 0
        flip_ref[task, partner] = 1
        mate_ref[task, block] = partner
        back_ref[task, partner] = block
        mate_ref[task, partner] = following
        back_ref[task, following] = partner
        return following

    def start(block, carry):
        lax.while_loop(lambda block: flip_ref[task, block] < 0, walk, block)
        return carry

    lax.fori_loop(0, blocks, start, 0)


def gather_kernel(partners_ref, source_ref, *refs):
    *out_refs, mate_ref, back_ref, flip_ref, source, arranged, in_sem, sems = refs
    arrival = pltpu.make_async_copy(source_ref, source, in_sem.at[0])
    arrival.start()
    places = source.shape[0]
    chunks = sems.shape[1]
    step = places // chunks
    copies = []
    for task, out_ref in enumerate(out_refs):
        plan_task(task, partners_ref, mate_ref, back_ref, flip_ref)
        if task == 0:
            arrival.wait()
        for chunk in range(chunks):

            def body(place, carry):
                arranged[task, place] = source[mate_ref[task, place]]
                return carry

            lax.fori_loop(chunk * step, (chunk + 1) * step, body, 0)
            where = pl.ds(chunk * step, step)
            copy = pltpu.make_async_copy(
                arranged.at[task, where], out_ref.at[where], sems.at[task, chunk]
            )
            copy.start()
            copies.append(copy)
    for copy in copies:
        copy.wait()


def gather(source, partners):
    rounds, blocks = partners.shape
    tasks = rounds // 2
    anywhere = pl.BlockSpec(memory_space=pl.ANY)
    smem = pl.BlockSpec(memory_space=pltpu.SMEM)
    table = jax.ShapeDtypeStruct((tasks, blocks), jnp.int32)
    results = pl.pallas_call(
        gather_kernel,
        out_shape=[jax.ShapeDtypeStruct(source.shape, source.dtype)] * tasks + [table] * 3,
        in_specs=[smem, anywhere],
        out_specs=[anywhere] * tasks + [smem] * 3,
        scratch_shapes=[
            pltpu.VMEM(source.shape, source.dtype),
            pltpu.VMEM((tasks,) + source.shape, source.dtype),
            pltpu.SemaphoreType.DMA((1,)),
            pltpu.SemaphoreType.DMA((tasks, 4)),
        ],
        compiler_params=params(),
        name="gather",
    )(partners, source)
    return results[:tasks], results[tasks + 1], results[tasks + 2]


def weighted(terms):
    total = None
    for weight, value in terms:
        if abs(weight) < 1e-12:
            continue
        term = value * weight
        total = term if total is None else total + term
    return total


def odd_multiples(base, sign):
    twice = lambda f, k: 2 * math.cos(math.pi * f * k / 16)
    plus = {f: base[f] + base[16 - f] for f in range(1, 8)}
    minus = {f: base[f] - base[16 - f] for f in range(1, 8)}
    end = base[16] if base[0] is None else base[0]
    flip = -1 if base[0] is None else 1
    doubled = end + end
    first = end + base[8]
    for f in range(1, 8):
        first = first + plus[f]
    sums = [first]
    for k in (1, 2, 3):
        if k == 2:
            total = weighted([(twice(f, k), plus[f] - plus[8 - f]) for f in range(1, 4)])
            total = total + doubled - (base[8] + base[8])
        else:
            total = weighted([(twice(f, k), minus[f]) for f in range(1, 8)])
            total = total + doubled if flip > 0 else total - doubled
        sums.append(total + sums[-1] if sign > 0 else total - sums[-1])
    return sums


def lag_sums(real, imag, norm):
    cosine = lambda f, t: math.cos(math.pi * f * t / 32) * norm
    sine = lambda f, t: -math.sin(math.pi * f * t / 32) * norm
    even, odd = {}, {}
    low = {0: real(0), 16: real(16)}
    diff = {0: low[0]}
    for f in range(1, 16):
        a, b = real(f), real(32 - f)
        low[f], diff[f] = a + b, a - b
    base = {f: diff[f] * cosine(f, 1) for f in range(16)}
    base[16] = None
    even[1], even[3], even[5], even[7] = odd_multiples(base, -1)
    minus = {f: low[f] - low[16 - f] for f in range(8)}
    for t in (2, 6):
        even[t] = weighted([(cosine(f, t), minus[f]) for f in range(8)])
    plus = {f: low[f] + low[16 - f] for f in range(8)}
    plus[8] = low[8]
    even[4] = weighted([(cosine(f, 4), plus[f] - plus[8 - f]) for f in range(4)])
    sums = {f: plus[f] + plus[8 - f] for f in range(4)}
    sums[4] = plus[4]
    even[8] = weighted([(cosine(f, 8), sums[f]) for f in range(5)])
    total = sums[0]
    for f in range(1, 5):
        total = total + sums[f]
    even[0] = total * norm

    add = {16: imag(16)}
    sub = {}
    for f in range(1, 16):
        a, b = imag(f), imag(32 - f)
        add[f], sub[f] = a + b, a - b
    base = {f: add[f] * sine(f, 1) for f in range(1, 17)}
    base[0] = None
    odd[1], odd[3], odd[5], odd[7] = odd_multiples(base, 1)
    sums = {f: sub[f] + sub[16 - f] for f in range(1, 8)}
    sums[8] = sub[8]
    for t in (2, 6):
        odd[t] = weighted([(sine(f, t), sums[f]) for f in range(1, 9)])
    minus = {f: sub[f] - sub[16 - f] for f in range(1, 8)}
    odd[4] = weighted(
        [(sine(f, 4), minus[f] + minus[8 - f]) for f in range(1, 4)] + [(sine(4, 4), minus[4])]
    )
    odd[8] = weighted([(sine(f, 8), minus[f] - minus[8 - f]) for f in range(1, 4)])
    return even, odd


def correlate_kernel(
    norm, place_ref, own_ref, mate_ref, keep_ref, send_ref, own, mate, cross, own_sems, mate_sems
):
    num_bins, slots, _ = own.shape
    chunks = own_sems.shape[0]
    bins = num_bins // chunks
    copies = []
    for chunk in range(chunks):
        where = pl.ds(chunk * bins, bins)
        pair = (
            pltpu.make_async_copy(own_ref.at[where], own.at[where], own_sems.at[chunk]),
            pltpu.make_async_copy(mate_ref.at[where], mate.at[where], mate_sems.at[chunk]),
        )
        for copy in pair:
            copy.start()
        copies.append(pair)
    for chunk in range(chunks):
        for copy in copies[chunk]:
            copy.wait()
        for f in range(chunk * bins, (chunk + 1) * bins):
            left, right = own[f], mate[f]
            half = right.shape[0] // 2
            turned = jnp.concatenate([right[half:], -right[:half]], 0)
            cross[f, :slots] = jnp.dot(left, right, preferred_element_type=f32)
            cross[f, slots:] = jnp.dot(left, turned, preferred_element_type=f32)

    lags, half, cols = keep_ref.shape
    core = place_ref[0]
    rows, lanes = 16, 128

    def part(out_ref, base):
        def body(chunk, carry):
            row = pl.multiple_of(chunk * rows, rows)
            where = pl.ds(pl.multiple_of(base + row, rows), rows)
            turned = pl.ds(pl.multiple_of(slots + base + row, rows), rows)
            for lane in range(0, cols, lanes):
                even, odd = lag_sums(
                    lambda f: cross[f, where, lane : lane + lanes],
                    lambda f: cross[f, turned, lane : lane + lanes],
                    norm,
                )
                for lag in range(lags):
                    t = lag - LAGS // 2
                    if t == 0:
                        value = even[0]
                    elif t > 0:
                        value = even[t] + odd[t]
                    else:
                        value = even[-t] - odd[-t]
                    out_ref[lag, pl.ds(row, rows), lane : lane + lanes] = value.astype(
                        out_ref.dtype
                    )
            return carry

        lax.fori_loop(0, half // rows, body, 0)

    part(keep_ref, core * half)
    part(send_ref, (1 - core) * half)


def correlate(own, mate, place, norm, lags):
    num_bins, slots, depth = own.shape
    cols = mate.shape[2]
    chunks = 8
    anywhere = pl.BlockSpec(memory_space=pl.ANY)
    vmem = pl.BlockSpec(memory_space=pltpu.VMEM)
    return pl.pallas_call(
        functools.partial(correlate_kernel, norm),
        out_shape=[
            jax.ShapeDtypeStruct((lags, slots // 2, cols), f32),
            jax.ShapeDtypeStruct((lags, slots // 2, cols), bf16),
        ],
        in_specs=[pl.BlockSpec(memory_space=pltpu.SMEM), anywhere, anywhere],
        out_specs=[vmem, vmem],
        scratch_shapes=[
            pltpu.VMEM(own.shape, bf16),
            pltpu.VMEM(mate.shape, bf16),
            pltpu.VMEM((num_bins, 2 * slots, cols), f32),
            pltpu.SemaphoreType.DMA((chunks,)),
            pltpu.SemaphoreType.DMA((chunks,)),
        ],
        compiler_params=params(),
        cost_estimate=pl.CostEstimate(
            flops=4 * num_bins * slots * depth * cols, bytes_accessed=20_000_000, transcendentals=0
        ),
        name="correlate",
    )(place, own, mate)


def core_sum_kernel(task, place_ref, keep_ref, recv_ref, *refs):
    own_ref, send_ref, piece_ref, keep, recv, own, send, piece, in_sems, out_sems, piece_sems = refs[-11:]
    core, chip = place_ref[0], place_ref[1]
    lags, rows, cols = own.shape
    own_rows = pl.ds(pl.multiple_of(chip * rows, rows), rows)
    other_rows = pl.ds(pl.multiple_of((1 - chip) * rows, rows), rows)
    chunks = in_sems.shape[1]
    step = lags // chunks
    bounds = [0] + [chunk * step + 1 for chunk in range(1, chunks)] + [lags + 1]
    arrivals, departures = [], []
    for chunk in range(chunks):
        where = pl.ds(bounds[chunk], bounds[chunk + 1] - bounds[chunk])
        pair = (
            pltpu.make_async_copy(keep_ref.at[where], keep.at[where], in_sems.at[0, chunk]),
            pltpu.make_async_copy(recv_ref.at[where], recv.at[where], in_sems.at[1, chunk]),
        )
        for copy in pair:
            copy.start()
        arrivals.append(pair)

    def leave(source, target, sem):
        copy = pltpu.make_async_copy(source, target, sem)
        copy.start()
        departures.append(copy)

    for chunk in range(chunks):
        for copy in arrivals[chunk]:
            copy.wait()
        first, last = bounds[chunk], bounds[chunk + 1]
        for lag in range(first, min(last, lags)):
            own[lag] = keep[lag, own_rows, :] + recv[lag, own_rows, :].astype(f32)
            send[lag] = (keep[lag, other_rows, :] + recv[lag, other_rows, :].astype(f32)).astype(
                bf16
            )
        for lag in range(max(first, 1), last):
            back = lags - lag
            turned = (keep[lag] + recv[lag].astype(f32)).T
            for half in range(2):
                low = turned[2 * half * rows : (2 * half + 1) * rows]
                high = turned[(2 * half + 1) * rows : (2 * half + 2) * rows]
                base = 2 * half * lags + back
                piece[base] = jnp.where(core == 0, low, high).astype(bf16)
                piece[base + lags] = jnp.where(core == 0, high, low).astype(bf16)
        where = pl.ds(first, min(last, lags) - first)
        leave(own.at[where], own_ref.at[where], out_sems.at[0, chunk])
        leave(send.at[where], send_ref.at[where], out_sems.at[1, chunk])
        for group in range(4):
            where = pl.ds(group * lags + lags - last + 1, step)
            leave(piece.at[where], piece_ref.at[where, task], piece_sems.at[group, chunk])
    for copy in departures:
        copy.wait()


def core_sum(place, keep, recv, task, tasks, pieces):
    lags, rows, cols = keep.shape
    anywhere = pl.BlockSpec(memory_space=pl.ANY)
    count = 4 * (lags - 1)
    part = (lags - 1, rows // 2, cols)
    piece = (cols // 4, rows)
    extra = [] if pieces is None else [pieces]
    return pl.pallas_call(
        functools.partial(core_sum_kernel, task),
        out_shape=[
            jax.ShapeDtypeStruct(part, f32),
            jax.ShapeDtypeStruct(part, bf16),
            jax.ShapeDtypeStruct((count, tasks) + piece, bf16),
        ],
        in_specs=[pl.BlockSpec(memory_space=pltpu.SMEM)] + [anywhere] * (2 + len(extra)),
        out_specs=[anywhere] * 3,
        scratch_shapes=[
            pltpu.VMEM(keep.shape, f32),
            pltpu.VMEM(keep.shape, bf16),
            pltpu.VMEM(part, f32),
            pltpu.VMEM(part, bf16),
            pltpu.VMEM((count,) + piece, bf16),
            pltpu.SemaphoreType.DMA((2, 4)),
            pltpu.SemaphoreType.DMA((2, 4)),
            pltpu.SemaphoreType.DMA((4, 4)),
        ],
        input_output_aliases={3: 2} if extra else {},
        compiler_params=params(),
        cost_estimate=pl.CostEstimate(flops=0, bytes_accessed=12_000_000, transcendentals=0),
        name="core_sum",
    )(place, keep, recv, *extra)


def gather_sum_kernel(index_ref, spread_ref, out_ref):
    places, tasks = out_ref.shape[:2]

    def body(place, carry):
        for task in range(tasks):
            source = index_ref[task, place]
            out_ref[place, task] = (
                spread_ref[source, task].astype(f32)
                + spread_ref[places + source, task].astype(f32)
            ).astype(bf16)
        return carry

    lax.fori_loop(0, places, body, 0, unroll=4)


def gather_sum(index, spread):
    places = index.shape[1]
    vmem = pl.BlockSpec(memory_space=pltpu.VMEM)
    return pl.pallas_call(
        gather_sum_kernel,
        out_shape=jax.ShapeDtypeStruct((places,) + spread.shape[1:], bf16),
        in_specs=[pl.BlockSpec(memory_space=pltpu.SMEM), vmem],
        out_specs=vmem,
        compiler_params=params(),
        name="gather_sum",
    )(index, spread)


def own_rows_kernel(flip_ref, place_ref, own_ref, recv_ref, *refs):
    out_ref = refs[-1]
    out_ref[:, 0] = jnp.swapaxes(own_ref[...] + recv_ref[...].astype(f32), 0, 1)


def own_rows(place, flip, task, own, recv, out):
    lags, rows, cols = own.shape
    step = 64
    extra = [] if out is None else [out]
    piece = pl.BlockSpec((lags, step, cols), lambda s, flip, place: (0, s, 0))
    return pl.pallas_call(
        own_rows_kernel,
        out_shape=jax.ShapeDtypeStruct((rows, ROUNDS, lags, cols), f32),
        grid_spec=pltpu.PrefetchScalarGridSpec(
            num_scalar_prefetch=2,
            grid=(rows // step,),
            in_specs=[piece, piece] + [pl.BlockSpec(memory_space=pl.ANY)] * len(extra),
            out_specs=pl.BlockSpec(
                (step, 1, lags, cols),
                lambda s, flip, place: (s, 2 * task + flip[task, place[2]], 0, 0),
            ),
        ),
        input_output_aliases={4: 0} if extra else {},
        compiler_params=params(),
        cost_estimate=pl.CostEstimate(flops=0, bytes_accessed=5_000_000, transcendentals=0),
        name="own_rows",
    )(flip, place, own, recv, *extra)


def mirrored_rows_kernel(flip_ref, place_ref, near_ref, far_ref, in_ref, out_ref):
    core = place_ref[0]
    near = near_ref[:, 0].astype(f32)
    far = far_ref[:, 0].astype(f32)
    first = jnp.where(core == 0, near, far)
    second = jnp.where(core == 0, far, near)
    lanes = first.shape[2]
    lane = lax.broadcasted_iota(jnp.int32, first.shape, 2)
    quarter = lanes // 2
    low = jnp.where(lane < quarter, first, pltpu.roll(second, quarter, 2))
    high = jnp.where(lane < quarter, pltpu.roll(first, quarter, 2), second)
    out_ref[:, 0, :, :lanes] = jnp.swapaxes(low, 0, 1)
    out_ref[:, 0, :, lanes:] = jnp.swapaxes(high, 0, 1)


def mirrored_rows(place, flip, near, far, out):
    rows, _, lags, cols = out.shape
    tasks = near.shape[1]
    step = 64
    back = pl.BlockSpec((lags, 1, step, near.shape[3]), lambda t, s, flip, place: (0, t, s, 0))
    return pl.pallas_call(
        mirrored_rows_kernel,
        out_shape=jax.ShapeDtypeStruct(out.shape, f32),
        grid_spec=pltpu.PrefetchScalarGridSpec(
            num_scalar_prefetch=2,
            grid=(tasks, rows // step),
            in_specs=[back, back, pl.BlockSpec(memory_space=pl.ANY)],
            out_specs=pl.BlockSpec(
                (step, 1, lags, cols),
                lambda t, s, flip, place: (s, 2 * t + 1 - flip[t, place[2]], 0, 0),
            ),
        ),
        input_output_aliases={4: 0},
        compiler_params=params(),
        name="mirrored_rows",
    )(flip, place, near, far, out)


def exchange(array):
    return lax.all_to_all(array, "pair", split_axis=0, concat_axis=0, tiled=True)


def after(array, *others):
    return lax.optimization_barrier((array,) + others)[0]


def local(spectra, channel_order, partners):
    num_bins, _, num_windows, cols = spectra.shape
    win_count = lax.axis_size("win")
    win = lax.axis_index("win")
    place = jnp.stack([win % 2, win // 2, lax.axis_index("pair")]).astype(jnp.int32)
    other_core = [(i, i ^ 1) for i in range(win_count)]
    other_chip = [(i, i ^ 2) for i in range(win_count)]
    norm = 1.0 / math.sqrt(num_windows * win_count * num_bins)
    tasks = ROUNDS // 2
    num_blocks = lax.axis_size("pair")

    own = whiten(spectra, channel_order).reshape(num_bins, 2 * num_windows, cols)
    shares = exchange(own)
    arranged, back_of, flip = gather(shares, partners)
    mates = [exchange(block) for block in arranged]
    own_turned = turn(after(own, mates[0]))
    groups = [
        [(block * 2 + chip_index) * 2 + core_index for chip_index in range(2) for block in range(num_blocks)]
        for core_index in range(2)
    ]
    rows, moved, pieces = [], [], None
    for task in range(tasks):
        keep, send = correlate(own_turned, mates[task], place, norm, LAGS + 1)
        recv = lax.ppermute(after(send, *moved), "win", other_core)
        own_sum, row_send, pieces = core_sum(place, keep, recv, task, tasks, pieces)
        if task + 1 < tasks:
            mates[task + 1] = after(mates[task + 1], row_send)
        if task + 1 < tasks:
            rows.append((own_sum, lax.ppermute(row_send, "win", other_chip)))
            moved = [rows[task][1]]
    out = own_rows(place, flip, 0, *rows[0], None)
    spread = lax.all_to_all(
        after(pieces, out), ("pair", "win"), 0, 0, tiled=True, axis_index_groups=groups
    )
    row_recv = lax.ppermute(row_send, "win", other_chip)
    returned = exchange(gather_sum(back_of, spread))
    out = own_rows(place, flip, 1, own_sum, row_recv, out)
    far = lax.ppermute(returned[LAGS:], "win", other_core)
    return mirrored_rows(place, flip, returned, far, out)[None]


def solution(mesh):
    return jax.shard_map(
        local,
        mesh=mesh,
        in_specs=(P(None, None, "win", "pair"), P("pair", None), P()),
        out_specs=P("pair", "win", None, None, None),
        check_vma=False,
    )
```

```python
import functools
import math

import jax
import jax.numpy as jnp
from jax import lax
from jax.experimental import pallas as pl
from jax.experimental.pallas import tpu as pltpu
from jax.sharding import PartitionSpec as P

LAGS = 16
ROUNDS = 4
VMEM_BYTES = 63 * 1024 * 1024
QUARTER_ORDER = (0, 2, 1, 3)
bf16 = jnp.bfloat16
f32 = jnp.float32


def params(**more):
    return pltpu.CompilerParams(vmem_limit_bytes=VMEM_BYTES, **more)


def whiten_kernel(order_ref, spectra_ref, out_ref):
    num_bins, _, rows, cols = spectra_ref.shape
    slots = lax.broadcasted_iota(jnp.int32, (cols, cols), 0)
    pick = (slots == order_ref[...]).astype(f32).astype(bf16)
    values = spectra_ref[...].astype(f32)
    power = values[:, 0] * values[:, 0] + values[:, 1] * values[:, 1]
    parts = []
    for f in range(num_bins):
        lo, hi = max(f - 2, 0), min(f + 2, num_bins - 1)
        total = power[lo]
        for g in range(lo + 1, hi + 1):
            total = total + power[g]
        inv_scale = jnp.minimum(lax.rsqrt(total * (1.0 / (hi - lo + 1))), 2.0)
        parts.append((values[f] * inv_scale[None]).astype(bf16).reshape(2 * rows, cols))
    flat = jnp.concatenate(parts, 0)
    ordered = jnp.dot(flat, pick, preferred_element_type=f32).astype(bf16)
    out_ref[...] = ordered.reshape(num_bins, 2, rows, cols)


def whiten(spectra, channel_order):
    num_bins, _, num_windows, cols = spectra.shape
    rows = 48
    return pl.pallas_call(
        whiten_kernel,
        grid=(num_windows // rows,),
        out_shape=jax.ShapeDtypeStruct(spectra.shape, bf16),
        in_specs=[
            pl.BlockSpec((1, cols), lambda s: (0, 0)),
            pl.BlockSpec((num_bins, 2, rows, cols), lambda s: (0, 0, s, 0)),
        ],
        out_specs=pl.BlockSpec((num_bins, 2, rows, cols), lambda s: (0, 0, s, 0)),
        compiler_params=params(),
        name="whiten",
    )(channel_order, spectra)


def turn_kernel(own_ref, out_ref):
    bins, _, cols = own_ref.shape
    quarter = cols // 4
    for f in range(bins):
        turned = own_ref[f].astype(f32).T.astype(bf16)
        for place, source in enumerate(QUARTER_ORDER):
            out_ref[f, place * quarter : (place + 1) * quarter, :] = turned[
                source * quarter : (source + 1) * quarter
            ]


def turn(own_rows):
    num_bins, depth, cols = own_rows.shape
    bins = 8
    return pl.pallas_call(
        turn_kernel,
        grid=(num_bins // bins,),
        out_shape=jax.ShapeDtypeStruct((num_bins, cols, depth), bf16),
        in_specs=[pl.BlockSpec((bins, depth, cols), lambda s: (s, 0, 0))],
        out_specs=pl.BlockSpec((bins, cols, depth), lambda s: (s, 0, 0)),
        compiler_params=params(),
        cost_estimate=pl.CostEstimate(flops=0, bytes_accessed=12_000_000, transcendentals=0),
        name="turn",
    )(own_rows)


def plan_task(task, partners_ref, mate_ref, back_ref, flip_ref):
    blocks = partners_ref.shape[1]
    first, second = 2 * task, 2 * task + 1
    for block in range(blocks):
        flip_ref[task, block] = -1

    def walk(block):
        partner = partners_ref[first, block]
        following = partners_ref[second, partner]
        flip_ref[task, block] = 0
        flip_ref[task, partner] = 1
        mate_ref[task, block] = partner
        back_ref[task, partner] = block
        mate_ref[task, partner] = following
        back_ref[task, following] = partner
        return following

    def start(block, carry):
        lax.while_loop(lambda block: flip_ref[task, block] < 0, walk, block)
        return carry

    lax.fori_loop(0, blocks, start, 0)


def gather_kernel(partners_ref, source_ref, *refs):
    *out_refs, mate_ref, back_ref, flip_ref, source, arranged, in_sem, sems = refs
    arrival = pltpu.make_async_copy(source_ref, source, in_sem.at[0])
    arrival.start()
    places = source.shape[0]
    chunks = sems.shape[1]
    step = places // chunks
    copies = []
    for task, out_ref in enumerate(out_refs):
        plan_task(task, partners_ref, mate_ref, back_ref, flip_ref)
        if task == 0:
            arrival.wait()
        for chunk in range(chunks):

            def body(place, carry):
                arranged[task, place] = source[mate_ref[task, place]]
                return carry

            lax.fori_loop(chunk * step, (chunk + 1) * step, body, 0)
            where = pl.ds(chunk * step, step)
            copy = pltpu.make_async_copy(
                arranged.at[task, where], out_ref.at[where], sems.at[task, chunk]
            )
            copy.start()
            copies.append(copy)
    for copy in copies:
        copy.wait()


def gather(source, partners):
    rounds, blocks = partners.shape
    tasks = rounds // 2
    anywhere = pl.BlockSpec(memory_space=pl.ANY)
    smem = pl.BlockSpec(memory_space=pltpu.SMEM)
    table = jax.ShapeDtypeStruct((tasks, blocks), jnp.int32)
    results = pl.pallas_call(
        gather_kernel,
        out_shape=[jax.ShapeDtypeStruct(source.shape, source.dtype)] * tasks + [table] * 3,
        in_specs=[smem, anywhere],
        out_specs=[anywhere] * tasks + [smem] * 3,
        scratch_shapes=[
            pltpu.VMEM(source.shape, source.dtype),
            pltpu.VMEM((tasks,) + source.shape, source.dtype),
            pltpu.SemaphoreType.DMA((1,)),
            pltpu.SemaphoreType.DMA((tasks, 4)),
        ],
        compiler_params=params(),
        name="gather",
    )(partners, source)
    return results[:tasks], results[tasks + 1], results[tasks + 2]


def weighted(terms):
    total = None
    for weight, value in terms:
        if abs(weight) < 1e-12:
            continue
        term = value * weight
        total = term if total is None else total + term
    return total


def odd_multiples(base, sign):
    twice = lambda f, k: 2 * math.cos(math.pi * f * k / 16)
    plus = {f: base[f] + base[16 - f] for f in range(1, 8)}
    minus = {f: base[f] - base[16 - f] for f in range(1, 8)}
    end = base[16] if base[0] is None else base[0]
    flip = -1 if base[0] is None else 1
    doubled = end + end
    first = end + base[8]
    for f in range(1, 8):
        first = first + plus[f]
    sums = [first]
    for k in (1, 2, 3):
        if k == 2:
            total = weighted([(twice(f, k), plus[f] - plus[8 - f]) for f in range(1, 4)])
            total = total + doubled - (base[8] + base[8])
        else:
            total = weighted([(twice(f, k), minus[f]) for f in range(1, 8)])
            total = total + doubled if flip > 0 else total - doubled
        sums.append(total + sums[-1] if sign > 0 else total - sums[-1])
    return sums


def lag_sums(real, imag, norm):
    cosine = lambda f, t: math.cos(math.pi * f * t / 32) * norm
    sine = lambda f, t: -math.sin(math.pi * f * t / 32) * norm
    even, odd = {}, {}
    low = {0: real(0), 16: real(16)}
    diff = {0: low[0]}
    for f in range(1, 16):
        a, b = real(f), real(32 - f)
        low[f], diff[f] = a + b, a - b
    base = {f: diff[f] * cosine(f, 1) for f in range(16)}
    base[16] = None
    even[1], even[3], even[5], even[7] = odd_multiples(base, -1)
    minus = {f: low[f] - low[16 - f] for f in range(8)}
    for t in (2, 6):
        even[t] = weighted([(cosine(f, t), minus[f]) for f in range(8)])
    plus = {f: low[f] + low[16 - f] for f in range(8)}
    plus[8] = low[8]
    even[4] = weighted([(cosine(f, 4), plus[f] - plus[8 - f]) for f in range(4)])
    sums = {f: plus[f] + plus[8 - f] for f in range(4)}
    sums[4] = plus[4]
    even[8] = weighted([(cosine(f, 8), sums[f]) for f in range(5)])
    total = sums[0]
    for f in range(1, 5):
        total = total + sums[f]
    even[0] = total * norm

    add = {16: imag(16)}
    sub = {}
    for f in range(1, 16):
        a, b = imag(f), imag(32 - f)
        add[f], sub[f] = a + b, a - b
    base = {f: add[f] * sine(f, 1) for f in range(1, 17)}
    base[0] = None
    odd[1], odd[3], odd[5], odd[7] = odd_multiples(base, 1)
    sums = {f: sub[f] + sub[16 - f] for f in range(1, 8)}
    sums[8] = sub[8]
    for t in (2, 6):
        odd[t] = weighted([(sine(f, t), sums[f]) for f in range(1, 9)])
    minus = {f: sub[f] - sub[16 - f] for f in range(1, 8)}
    odd[4] = weighted(
        [(sine(f, 4), minus[f] + minus[8 - f]) for f in range(1, 4)] + [(sine(4, 4), minus[4])]
    )
    odd[8] = weighted([(sine(f, 8), minus[f] - minus[8 - f]) for f in range(1, 4)])
    return even, odd


def correlate_kernel(
    norm, place_ref, own_ref, mate_ref, keep_ref, send_ref, own, mate, cross, own_sems, mate_sems
):
    num_bins, slots, _ = own.shape
    chunks = own_sems.shape[0]
    bins = num_bins // chunks
    copies = []
    for chunk in range(chunks):
        where = pl.ds(chunk * bins, bins)
        pair = (
            pltpu.make_async_copy(own_ref.at[where], own.at[where], own_sems.at[chunk]),
            pltpu.make_async_copy(mate_ref.at[where], mate.at[where], mate_sems.at[chunk]),
        )
        for copy in pair:
            copy.start()
        copies.append(pair)
    for chunk in range(chunks):
        for copy in copies[chunk]:
            copy.wait()
        for f in range(chunk * bins, (chunk + 1) * bins):
            left, right = own[f], mate[f]
            half = right.shape[0] // 2
            turned = jnp.concatenate([right[half:], -right[:half]], 0)
            cross[f, :slots] = jnp.dot(left, right, preferred_element_type=f32)
            cross[f, slots:] = jnp.dot(left, turned, preferred_element_type=f32)

    lags, half, cols = keep_ref.shape
    core = place_ref[0]
    rows, lanes = 16, 128

    def part(out_ref, base):
        def body(chunk, carry):
            row = pl.multiple_of(chunk * rows, rows)
            where = pl.ds(pl.multiple_of(base + row, rows), rows)
            turned = pl.ds(pl.multiple_of(slots + base + row, rows), rows)
            for lane in range(0, cols, lanes):
                even, odd = lag_sums(
                    lambda f: cross[f, where, lane : lane + lanes],
                    lambda f: cross[f, turned, lane : lane + lanes],
                    norm,
                )
                for lag in range(lags):
                    t = lag - LAGS // 2
                    if t == 0:
                        value = even[0]
                    elif t > 0:
                        value = even[t] + odd[t]
                    else:
                        value = even[-t] - odd[-t]
                    out_ref[lag, pl.ds(row, rows), lane : lane + lanes] = value.astype(
                        out_ref.dtype
                    )
            return carry

        lax.fori_loop(0, half // rows, body, 0)

    part(keep_ref, core * half)
    part(send_ref, (1 - core) * half)


def correlate(own, mate, place, norm, lags):
    num_bins, slots, depth = own.shape
    cols = mate.shape[2]
    chunks = 8
    anywhere = pl.BlockSpec(memory_space=pl.ANY)
    vmem = pl.BlockSpec(memory_space=pltpu.VMEM)
    return pl.pallas_call(
        functools.partial(correlate_kernel, norm),
        out_shape=[
            jax.ShapeDtypeStruct((lags, slots // 2, cols), f32),
            jax.ShapeDtypeStruct((lags, slots // 2, cols), bf16),
        ],
        in_specs=[pl.BlockSpec(memory_space=pltpu.SMEM), anywhere, anywhere],
        out_specs=[vmem, vmem],
        scratch_shapes=[
            pltpu.VMEM(own.shape, bf16),
            pltpu.VMEM(mate.shape, bf16),
            pltpu.VMEM((num_bins, 2 * slots, cols), f32),
            pltpu.SemaphoreType.DMA((chunks,)),
            pltpu.SemaphoreType.DMA((chunks,)),
        ],
        compiler_params=params(),
        cost_estimate=pl.CostEstimate(
            flops=4 * num_bins * slots * depth * cols, bytes_accessed=20_000_000, transcendentals=0
        ),
        name="correlate",
    )(place, own, mate)


def core_sum_kernel(task, place_ref, keep_ref, recv_ref, *refs):
    own_ref, send_ref, piece_ref, keep, recv, own, send, piece, in_sems, out_sems, piece_sems = refs[-11:]
    core, chip = place_ref[0], place_ref[1]
    lags, rows, cols = own.shape
    own_rows = pl.ds(pl.multiple_of(chip * rows, rows), rows)
    other_rows = pl.ds(pl.multiple_of((1 - chip) * rows, rows), rows)
    chunks = in_sems.shape[1]
    step = lags // chunks
    bounds = [0] + [chunk * step + 1 for chunk in range(1, chunks)] + [lags + 1]
    arrivals, departures = [], []
    for chunk in range(chunks):
        where = pl.ds(bounds[chunk], bounds[chunk + 1] - bounds[chunk])
        pair = (
            pltpu.make_async_copy(keep_ref.at[where], keep.at[where], in_sems.at[0, chunk]),
            pltpu.make_async_copy(recv_ref.at[where], recv.at[where], in_sems.at[1, chunk]),
        )
        for copy in pair:
            copy.start()
        arrivals.append(pair)

    def leave(source, target, sem):
        copy = pltpu.make_async_copy(source, target, sem)
        copy.start()
        departures.append(copy)

    for chunk in range(chunks):
        for copy in arrivals[chunk]:
            copy.wait()
        first, last = bounds[chunk], bounds[chunk + 1]
        for lag in range(first, min(last, lags)):
            own[lag] = keep[lag, own_rows, :] + recv[lag, own_rows, :].astype(f32)
            send[lag] = (keep[lag, other_rows, :] + recv[lag, other_rows, :].astype(f32)).astype(
                bf16
            )
        for lag in range(max(first, 1), last):
            back = lags - lag
            turned = (keep[lag] + recv[lag].astype(f32)).T
            for half in range(2):
                low = turned[2 * half * rows : (2 * half + 1) * rows]
                high = turned[(2 * half + 1) * rows : (2 * half + 2) * rows]
                base = 2 * half * lags + back
                piece[base] = jnp.where(core == 0, low, high).astype(bf16)
                piece[base + lags] = jnp.where(core == 0, high, low).astype(bf16)
        where = pl.ds(first, min(last, lags) - first)
        leave(own.at[where], own_ref.at[where], out_sems.at[0, chunk])
        leave(send.at[where], send_ref.at[where], out_sems.at[1, chunk])
        for group in range(4):
            where = pl.ds(group * lags + lags - last + 1, step)
            leave(piece.at[where], piece_ref.at[where, task], piece_sems.at[group, chunk])
    for copy in departures:
        copy.wait()


def core_sum(place, keep, recv, task, tasks, pieces):
    lags, rows, cols = keep.shape
    anywhere = pl.BlockSpec(memory_space=pl.ANY)
    count = 4 * (lags - 1)
    part = (lags - 1, rows // 2, cols)
    piece = (cols // 4, rows)
    extra = [] if pieces is None else [pieces]
    return pl.pallas_call(
        functools.partial(core_sum_kernel, task),
        out_shape=[
            jax.ShapeDtypeStruct(part, f32),
            jax.ShapeDtypeStruct(part, bf16),
            jax.ShapeDtypeStruct((count, tasks) + piece, bf16),
        ],
        in_specs=[pl.BlockSpec(memory_space=pltpu.SMEM)] + [anywhere] * (2 + len(extra)),
        out_specs=[anywhere] * 3,
        scratch_shapes=[
            pltpu.VMEM(keep.shape, f32),
            pltpu.VMEM(keep.shape, bf16),
            pltpu.VMEM(part, f32),
            pltpu.VMEM(part, bf16),
            pltpu.VMEM((count,) + piece, bf16),
            pltpu.SemaphoreType.DMA((2, 4)),
            pltpu.SemaphoreType.DMA((2, 4)),
            pltpu.SemaphoreType.DMA((4, 4)),
        ],
        input_output_aliases={3: 2} if extra else {},
        compiler_params=params(),
        cost_estimate=pl.CostEstimate(flops=0, bytes_accessed=12_000_000, transcendentals=0),
        name="core_sum",
    )(place, keep, recv, *extra)


def gather_sum_kernel(index_ref, spread_ref, out_ref):
    places = out_ref.shape[0]
    task = pl.program_id(0)

    def body(place, carry):
        source = index_ref[task, place]
        out_ref[place, 0] = (
            spread_ref[source, 0].astype(f32) + spread_ref[places + source, 0].astype(f32)
        ).astype(bf16)
        return carry

    lax.fori_loop(0, places, body, 0, unroll=8)


def gather_sum(index, spread):
    tasks, places = index.shape
    pieces, piece = spread.shape[0], spread.shape[2:]
    return pl.pallas_call(
        gather_sum_kernel,
        grid=(tasks,),
        out_shape=jax.ShapeDtypeStruct((places, tasks) + piece, bf16),
        in_specs=[
            pl.BlockSpec(memory_space=pltpu.SMEM),
            pl.BlockSpec((pieces, 1) + piece, lambda t: (0, t, 0, 0)),
        ],
        out_specs=pl.BlockSpec((places, 1) + piece, lambda t: (0, t, 0, 0)),
        compiler_params=params(),
        name="gather_sum",
    )(index, spread)


def own_rows_kernel(flip_ref, place_ref, own_ref, recv_ref, *refs):
    out_ref = refs[-1]
    out_ref[:, 0] = jnp.swapaxes(own_ref[...] + recv_ref[...].astype(f32), 0, 1)


def own_rows(place, flip, task, own, recv, out):
    lags, rows, cols = own.shape
    step = 64
    extra = [] if out is None else [out]
    piece = pl.BlockSpec((lags, step, cols), lambda s, flip, place: (0, s, 0))
    return pl.pallas_call(
        own_rows_kernel,
        out_shape=jax.ShapeDtypeStruct((rows, ROUNDS, lags, cols), f32),
        grid_spec=pltpu.PrefetchScalarGridSpec(
            num_scalar_prefetch=2,
            grid=(rows // step,),
            in_specs=[piece, piece] + [pl.BlockSpec(memory_space=pl.ANY)] * len(extra),
            out_specs=pl.BlockSpec(
                (step, 1, lags, cols),
                lambda s, flip, place: (s, 2 * task + flip[task, place[2]], 0, 0),
            ),
        ),
        input_output_aliases={4: 0} if extra else {},
        compiler_params=params(),
        cost_estimate=pl.CostEstimate(flops=0, bytes_accessed=5_000_000, transcendentals=0),
        name="own_rows",
    )(flip, place, own, recv, *extra)


def last_rows_kernel(flip_ref, place_ref, own_ref, recv_ref, near_ref, far_ref, in_ref, out_ref):
    step = pl.program_id(0)

    @pl.when(step == 0)
    def _():
        out_ref[:, 0] = jnp.swapaxes(own_ref[...] + recv_ref[...].astype(f32), 0, 1)

    @pl.when(step > 0)
    def _():
        core = place_ref[0]
        near = near_ref[:, 0].astype(f32)
        far = far_ref[:, 0].astype(f32)
        first = jnp.where(core == 0, near, far)
        second = jnp.where(core == 0, far, near)
        lanes = first.shape[2]
        lane = lax.broadcasted_iota(jnp.int32, first.shape, 2)
        quarter = lanes // 2
        low = jnp.where(lane < quarter, first, pltpu.roll(second, quarter, 2))
        high = jnp.where(lane < quarter, pltpu.roll(first, quarter, 2), second)
        out_ref[:, 0, :, :lanes] = jnp.swapaxes(low, 0, 1)
        out_ref[:, 0, :, lanes:] = jnp.swapaxes(high, 0, 1)


def last_rows(place, flip, own, recv, near, far, out):
    rows, _, lags, cols = out.shape
    tasks = near.shape[1]
    whole = pl.BlockSpec((lags, rows, cols), lambda s, flip, place: (0, 0, 0))
    back = pl.BlockSpec(
        (lags, 1, rows, near.shape[3]),
        lambda s, flip, place: (0, jnp.maximum(s - 1, 0), 0, 0),
    )

    def target(s, flip, place):
        task = jnp.maximum(s - 1, 0)
        block = place[2]
        mirrored = 2 * task + 1 - flip[task, block]
        return (0, jnp.where(s == 0, 2 * (tasks - 1) + flip[tasks - 1, block], mirrored), 0, 0)

    return pl.pallas_call(
        last_rows_kernel,
        out_shape=jax.ShapeDtypeStruct(out.shape, f32),
        grid_spec=pltpu.PrefetchScalarGridSpec(
            num_scalar_prefetch=2,
            grid=(tasks + 1,),
            in_specs=[whole, whole, back, back, pl.BlockSpec(memory_space=pl.ANY)],
            out_specs=pl.BlockSpec((rows, 1, lags, cols), target),
        ),
        input_output_aliases={6: 0},
        compiler_params=params(),
        name="last_rows",
    )(flip, place, own, recv, near, far, out)


def exchange(array):
    return lax.all_to_all(array, "pair", split_axis=0, concat_axis=0, tiled=True)


def after(array, *others):
    return lax.optimization_barrier((array,) + others)[0]


def local(spectra, channel_order, partners):
    num_bins, _, num_windows, cols = spectra.shape
    win_count = lax.axis_size("win")
    win = lax.axis_index("win")
    place = jnp.stack([win % 2, win // 2, lax.axis_index("pair")]).astype(jnp.int32)
    other_core = [(i, i ^ 1) for i in range(win_count)]
    other_chip = [(i, i ^ 2) for i in range(win_count)]
    norm = 1.0 / math.sqrt(num_windows * win_count * num_bins)
    tasks = ROUNDS // 2
    num_blocks = lax.axis_size("pair")

    own = whiten(spectra, channel_order).reshape(num_bins, 2 * num_windows, cols)
    shares = exchange(own)
    arranged, back_of, flip = gather(shares, partners)
    mates = [exchange(block) for block in arranged]
    own_turned = turn(after(own, mates[0]))
    groups = [
        [(block * 2 + chip_index) * 2 + core_index for chip_index in range(2) for block in range(num_blocks)]
        for core_index in range(2)
    ]
    rows, moved, pieces = [], [], None
    for task in range(tasks):
        keep, send = correlate(own_turned, mates[task], place, norm, LAGS + 1)
        recv = lax.ppermute(after(send, *moved), "win", other_core)
        own_sum, row_send, pieces = core_sum(place, keep, recv, task, tasks, pieces)
        if task + 1 < tasks:
            mates[task + 1] = after(mates[task + 1], row_send)
        if task + 1 < tasks:
            rows.append((own_sum, lax.ppermute(row_send, "win", other_chip)))
            moved = [rows[task][1]]
    out = own_rows(place, flip, 0, *rows[0], None)
    spread = lax.all_to_all(
        after(pieces, out), ("pair", "win"), 0, 0, tiled=True, axis_index_groups=groups
    )
    row_recv = lax.ppermute(row_send, "win", other_chip)
    returned = exchange(gather_sum(back_of, spread))
    far = lax.ppermute(returned[LAGS:], "win", other_core)
    return last_rows(place, flip, own_sum, row_recv, returned, far, out)[None]


def solution(mesh):
    return jax.shard_map(
        local,
        mesh=mesh,
        in_specs=(P(None, None, "win", "pair"), P("pair", None), P()),
        out_specs=P("pair", "win", None, None, None),
        check_vma=False,
    )
```

```python
import functools
import math

import jax
import jax.numpy as jnp
from jax import lax
from jax.experimental import pallas as pl
from jax.experimental.pallas import tpu as pltpu
from jax.sharding import PartitionSpec as P

LAGS = 16
ROUNDS = 4
VMEM_BYTES = 63 * 1024 * 1024
QUARTER_ORDER = (0, 2, 1, 3)
bf16 = jnp.bfloat16
f32 = jnp.float32


def params(**more):
    return pltpu.CompilerParams(vmem_limit_bytes=VMEM_BYTES, **more)


def whiten_kernel(order_ref, spectra_ref, out_ref):
    num_bins, _, rows, cols = spectra_ref.shape
    slots = lax.broadcasted_iota(jnp.int32, (cols, cols), 0)
    pick = (slots == order_ref[...]).astype(f32).astype(bf16)
    values = spectra_ref[...].astype(f32)
    power = values[:, 0] * values[:, 0] + values[:, 1] * values[:, 1]
    parts = []
    for f in range(num_bins):
        lo, hi = max(f - 2, 0), min(f + 2, num_bins - 1)
        total = power[lo]
        for g in range(lo + 1, hi + 1):
            total = total + power[g]
        inv_scale = jnp.minimum(lax.rsqrt(total * (1.0 / (hi - lo + 1))), 2.0)
        parts.append((values[f] * inv_scale[None]).astype(bf16).reshape(2 * rows, cols))
    flat = jnp.concatenate(parts, 0)
    ordered = jnp.dot(flat, pick, preferred_element_type=f32).astype(bf16)
    out_ref[...] = ordered.reshape(num_bins, 2, rows, cols)


def whiten(spectra, channel_order):
    num_bins, _, num_windows, cols = spectra.shape
    rows = 48
    return pl.pallas_call(
        whiten_kernel,
        grid=(num_windows // rows,),
        out_shape=jax.ShapeDtypeStruct(spectra.shape, bf16),
        in_specs=[
            pl.BlockSpec((1, cols), lambda s: (0, 0)),
            pl.BlockSpec((num_bins, 2, rows, cols), lambda s: (0, 0, s, 0)),
        ],
        out_specs=pl.BlockSpec((num_bins, 2, rows, cols), lambda s: (0, 0, s, 0)),
        compiler_params=params(),
        name="whiten",
    )(channel_order, spectra)


def turn_kernel(own_ref, out_ref):
    bins, _, cols = own_ref.shape
    quarter = cols // 4
    for f in range(bins):
        turned = own_ref[f].astype(f32).T.astype(bf16)
        for place, source in enumerate(QUARTER_ORDER):
            out_ref[f, place * quarter : (place + 1) * quarter, :] = turned[
                source * quarter : (source + 1) * quarter
            ]


def turn(own_rows):
    num_bins, depth, cols = own_rows.shape
    bins = 8
    return pl.pallas_call(
        turn_kernel,
        grid=(num_bins // bins,),
        out_shape=jax.ShapeDtypeStruct((num_bins, cols, depth), bf16),
        in_specs=[pl.BlockSpec((bins, depth, cols), lambda s: (s, 0, 0))],
        out_specs=pl.BlockSpec((bins, cols, depth), lambda s: (s, 0, 0)),
        compiler_params=params(),
        cost_estimate=pl.CostEstimate(flops=0, bytes_accessed=12_000_000, transcendentals=0),
        name="turn",
    )(own_rows)


def plan_task(task, partners_ref, mate_ref, back_ref, flip_ref):
    blocks = partners_ref.shape[1]
    first, second = 2 * task, 2 * task + 1
    for block in range(blocks):
        flip_ref[task, block] = -1

    def walk(block):
        partner = partners_ref[first, block]
        following = partners_ref[second, partner]
        flip_ref[task, block] = 0
        flip_ref[task, partner] = 1
        mate_ref[task, block] = partner
        back_ref[task, partner] = block
        mate_ref[task, partner] = following
        back_ref[task, following] = partner
        return following

    def start(block, carry):
        lax.while_loop(lambda block: flip_ref[task, block] < 0, walk, block)
        return carry

    lax.fori_loop(0, blocks, start, 0)


def gather_kernel(partners_ref, source_ref, *refs):
    *out_refs, mate_ref, back_ref, flip_ref, source, arranged, in_sem, sems = refs
    arrival = pltpu.make_async_copy(source_ref, source, in_sem.at[0])
    arrival.start()
    places = source.shape[0]
    chunks = sems.shape[1]
    step = places // chunks
    copies = []
    for task, out_ref in enumerate(out_refs):
        plan_task(task, partners_ref, mate_ref, back_ref, flip_ref)
        if task == 0:
            arrival.wait()
        for chunk in range(chunks):

            def body(place, carry):
                arranged[task, place] = source[mate_ref[task, place]]
                return carry

            lax.fori_loop(chunk * step, (chunk + 1) * step, body, 0)
            where = pl.ds(chunk * step, step)
            copy = pltpu.make_async_copy(
                arranged.at[task, where], out_ref.at[where], sems.at[task, chunk]
            )
            copy.start()
            copies.append(copy)
    for copy in copies:
        copy.wait()


def gather(source, partners):
    rounds, blocks = partners.shape
    tasks = rounds // 2
    anywhere = pl.BlockSpec(memory_space=pl.ANY)
    smem = pl.BlockSpec(memory_space=pltpu.SMEM)
    table = jax.ShapeDtypeStruct((tasks, blocks), jnp.int32)
    results = pl.pallas_call(
        gather_kernel,
        out_shape=[jax.ShapeDtypeStruct(source.shape, source.dtype)] * tasks + [table] * 3,
        in_specs=[smem, anywhere],
        out_specs=[anywhere] * tasks + [smem] * 3,
        scratch_shapes=[
            pltpu.VMEM(source.shape, source.dtype),
            pltpu.VMEM((tasks,) + source.shape, source.dtype),
            pltpu.SemaphoreType.DMA((1,)),
            pltpu.SemaphoreType.DMA((tasks, 4)),
        ],
        compiler_params=params(),
        name="gather",
    )(partners, source)
    return results[:tasks], results[tasks + 1], results[tasks + 2]


def weighted(terms):
    total = None
    for weight, value in terms:
        if abs(weight) < 1e-12:
            continue
        term = value * weight
        total = term if total is None else total + term
    return total


def odd_multiples(base, sign):
    twice = lambda f, k: 2 * math.cos(math.pi * f * k / 16)
    plus = {f: base[f] + base[16 - f] for f in range(1, 8)}
    minus = {f: base[f] - base[16 - f] for f in range(1, 8)}
    end = base[16] if base[0] is None else base[0]
    flip = -1 if base[0] is None else 1
    doubled = end + end
    first = end + base[8]
    for f in range(1, 8):
        first = first + plus[f]
    sums = [first]
    for k in (1, 2, 3):
        if k == 2:
            total = weighted([(twice(f, k), plus[f] - plus[8 - f]) for f in range(1, 4)])
            total = total + doubled - (base[8] + base[8])
        else:
            total = weighted([(twice(f, k), minus[f]) for f in range(1, 8)])
            total = total + doubled if flip > 0 else total - doubled
        sums.append(total + sums[-1] if sign > 0 else total - sums[-1])
    return sums


def lag_sums(real, imag, norm):
    cosine = lambda f, t: math.cos(math.pi * f * t / 32) * norm
    sine = lambda f, t: -math.sin(math.pi * f * t / 32) * norm
    even, odd = {}, {}
    low = {0: real(0), 16: real(16)}
    diff = {0: low[0]}
    for f in range(1, 16):
        a, b = real(f), real(32 - f)
        low[f], diff[f] = a + b, a - b
    base = {f: diff[f] * cosine(f, 1) for f in range(16)}
    base[16] = None
    even[1], even[3], even[5], even[7] = odd_multiples(base, -1)
    minus = {f: low[f] - low[16 - f] for f in range(8)}
    for t in (2, 6):
        even[t] = weighted([(cosine(f, t), minus[f]) for f in range(8)])
    plus = {f: low[f] + low[16 - f] for f in range(8)}
    plus[8] = low[8]
    even[4] = weighted([(cosine(f, 4), plus[f] - plus[8 - f]) for f in range(4)])
    sums = {f: plus[f] + plus[8 - f] for f in range(4)}
    sums[4] = plus[4]
    even[8] = weighted([(cosine(f, 8), sums[f]) for f in range(5)])
    total = sums[0]
    for f in range(1, 5):
        total = total + sums[f]
    even[0] = total * norm

    add = {16: imag(16)}
    sub = {}
    for f in range(1, 16):
        a, b = imag(f), imag(32 - f)
        add[f], sub[f] = a + b, a - b
    base = {f: add[f] * sine(f, 1) for f in range(1, 17)}
    base[0] = None
    odd[1], odd[3], odd[5], odd[7] = odd_multiples(base, 1)
    sums = {f: sub[f] + sub[16 - f] for f in range(1, 8)}
    sums[8] = sub[8]
    for t in (2, 6):
        odd[t] = weighted([(sine(f, t), sums[f]) for f in range(1, 9)])
    minus = {f: sub[f] - sub[16 - f] for f in range(1, 8)}
    odd[4] = weighted(
        [(sine(f, 4), minus[f] + minus[8 - f]) for f in range(1, 4)] + [(sine(4, 4), minus[4])]
    )
    odd[8] = weighted([(sine(f, 8), minus[f] - minus[8 - f]) for f in range(1, 4)])
    return even, odd


def correlate_kernel(
    norm, place_ref, own_ref, mate_ref, keep_ref, send_ref, own, mate, cross, own_sems, mate_sems
):
    num_bins, slots, _ = own.shape
    chunks = own_sems.shape[0]
    bins = num_bins // chunks
    copies = []
    for chunk in range(chunks):
        where = pl.ds(chunk * bins, bins)
        pair = (
            pltpu.make_async_copy(own_ref.at[where], own.at[where], own_sems.at[chunk]),
            pltpu.make_async_copy(mate_ref.at[where], mate.at[where], mate_sems.at[chunk]),
        )
        for copy in pair:
            copy.start()
        copies.append(pair)
    for chunk in range(chunks):
        for copy in copies[chunk]:
            copy.wait()
        for f in range(chunk * bins, (chunk + 1) * bins):
            left, right = own[f], mate[f]
            half = right.shape[0] // 2
            turned = jnp.concatenate([right[half:], -right[:half]], 0)
            cross[f, :slots] = jnp.dot(left, right, preferred_element_type=f32)
            cross[f, slots:] = jnp.dot(left, turned, preferred_element_type=f32)

    lags, half, cols = keep_ref.shape
    core = place_ref[0]
    rows, lanes = 16, 128

    def part(out_ref, base):
        def body(chunk, carry):
            row = pl.multiple_of(chunk * rows, rows)
            where = pl.ds(pl.multiple_of(base + row, rows), rows)
            turned = pl.ds(pl.multiple_of(slots + base + row, rows), rows)
            for lane in range(0, cols, lanes):
                even, odd = lag_sums(
                    lambda f: cross[f, where, lane : lane + lanes],
                    lambda f: cross[f, turned, lane : lane + lanes],
                    norm,
                )
                for lag in range(lags):
                    t = lag - LAGS // 2
                    if t == 0:
                        value = even[0]
                    elif t > 0:
                        value = even[t] + odd[t]
                    else:
                        value = even[-t] - odd[-t]
                    out_ref[lag, pl.ds(row, rows), lane : lane + lanes] = value.astype(
                        out_ref.dtype
                    )
            return carry

        lax.fori_loop(0, half // rows, body, 0)

    part(keep_ref, core * half)
    part(send_ref, (1 - core) * half)


def correlate(own, mate, place, norm, lags):
    num_bins, slots, depth = own.shape
    cols = mate.shape[2]
    chunks = 16
    anywhere = pl.BlockSpec(memory_space=pl.ANY)
    vmem = pl.BlockSpec(memory_space=pltpu.VMEM)
    return pl.pallas_call(
        functools.partial(correlate_kernel, norm),
        out_shape=[
            jax.ShapeDtypeStruct((lags, slots // 2, cols), f32),
            jax.ShapeDtypeStruct((lags, slots // 2, cols), bf16),
        ],
        in_specs=[pl.BlockSpec(memory_space=pltpu.SMEM), anywhere, anywhere],
        out_specs=[vmem, vmem],
        scratch_shapes=[
            pltpu.VMEM(own.shape, bf16),
            pltpu.VMEM(mate.shape, bf16),
            pltpu.VMEM((num_bins, 2 * slots, cols), f32),
            pltpu.SemaphoreType.DMA((chunks,)),
            pltpu.SemaphoreType.DMA((chunks,)),
        ],
        compiler_params=params(),
        cost_estimate=pl.CostEstimate(
            flops=4 * num_bins * slots * depth * cols, bytes_accessed=20_000_000, transcendentals=0
        ),
        name="correlate",
    )(place, own, mate)


def core_sum_kernel(task, place_ref, keep_ref, recv_ref, *refs):
    own_ref, send_ref, piece_ref, keep, recv, own, send, piece, in_sems, out_sems, piece_sems = refs[-11:]
    core, chip = place_ref[0], place_ref[1]
    lags, rows, cols = own.shape
    own_rows = pl.ds(pl.multiple_of(chip * rows, rows), rows)
    other_rows = pl.ds(pl.multiple_of((1 - chip) * rows, rows), rows)
    chunks = in_sems.shape[1]
    step = lags // chunks
    bounds = [0] + [chunk * step + 1 for chunk in range(1, chunks)] + [lags + 1]
    arrivals, departures = [], []
    for chunk in range(chunks):
        where = pl.ds(bounds[chunk], bounds[chunk + 1] - bounds[chunk])
        pair = (
            pltpu.make_async_copy(keep_ref.at[where], keep.at[where], in_sems.at[0, chunk]),
            pltpu.make_async_copy(recv_ref.at[where], recv.at[where], in_sems.at[1, chunk]),
        )
        for copy in pair:
            copy.start()
        arrivals.append(pair)

    def leave(source, target, sem):
        copy = pltpu.make_async_copy(source, target, sem)
        copy.start()
        departures.append(copy)

    for chunk in range(chunks):
        for copy in arrivals[chunk]:
            copy.wait()
        first, last = bounds[chunk], bounds[chunk + 1]
        for lag in range(first, min(last, lags)):
            own[lag] = keep[lag, own_rows, :] + recv[lag, own_rows, :].astype(f32)
            send[lag] = (keep[lag, other_rows, :] + recv[lag, other_rows, :].astype(f32)).astype(
                bf16
            )
        for lag in range(max(first, 1), last):
            back = lags - lag
            turned = (keep[lag] + recv[lag].astype(f32)).T
            for half in range(2):
                low = turned[2 * half * rows : (2 * half + 1) * rows]
                high = turned[(2 * half + 1) * rows : (2 * half + 2) * rows]
                base = 2 * half * lags + back
                piece[base] = jnp.where(core == 0, low, high).astype(bf16)
                piece[base + lags] = jnp.where(core == 0, high, low).astype(bf16)
        where = pl.ds(first, min(last, lags) - first)
        leave(own.at[where], own_ref.at[where], out_sems.at[0, chunk])
        leave(send.at[where], send_ref.at[where], out_sems.at[1, chunk])
        for group in range(4):
            where = pl.ds(group * lags + lags - last + 1, step)
            leave(piece.at[where], piece_ref.at[where, task], piece_sems.at[group, chunk])
    for copy in departures:
        copy.wait()


def core_sum(place, keep, recv, task, tasks, pieces):
    lags, rows, cols = keep.shape
    anywhere = pl.BlockSpec(memory_space=pl.ANY)
    count = 4 * (lags - 1)
    part = (lags - 1, rows // 2, cols)
    piece = (cols // 4, rows)
    extra = [] if pieces is None else [pieces]
    return pl.pallas_call(
        functools.partial(core_sum_kernel, task),
        out_shape=[
            jax.ShapeDtypeStruct(part, f32),
            jax.ShapeDtypeStruct(part, bf16),
            jax.ShapeDtypeStruct((count, tasks) + piece, bf16),
        ],
        in_specs=[pl.BlockSpec(memory_space=pltpu.SMEM)] + [anywhere] * (2 + len(extra)),
        out_specs=[anywhere] * 3,
        scratch_shapes=[
            pltpu.VMEM(keep.shape, f32),
            pltpu.VMEM(keep.shape, bf16),
            pltpu.VMEM(part, f32),
            pltpu.VMEM(part, bf16),
            pltpu.VMEM((count,) + piece, bf16),
            pltpu.SemaphoreType.DMA((2, 4)),
            pltpu.SemaphoreType.DMA((2, 4)),
            pltpu.SemaphoreType.DMA((4, 4)),
        ],
        input_output_aliases={3: 2} if extra else {},
        compiler_params=params(),
        cost_estimate=pl.CostEstimate(flops=0, bytes_accessed=12_000_000, transcendentals=0),
        name="core_sum",
    )(place, keep, recv, *extra)


def gather_sum_kernel(index_ref, spread_ref, out_ref):
    places = out_ref.shape[0]
    task = pl.program_id(0)

    def body(place, carry):
        source = index_ref[task, place]
        out_ref[place, 0] = (
            spread_ref[source, 0].astype(f32) + spread_ref[places + source, 0].astype(f32)
        ).astype(bf16)
        return carry

    lax.fori_loop(0, places, body, 0, unroll=8)


def gather_sum(index, spread):
    tasks, places = index.shape
    pieces, piece = spread.shape[0], spread.shape[2:]
    return pl.pallas_call(
        gather_sum_kernel,
        grid=(tasks,),
        out_shape=jax.ShapeDtypeStruct((places, tasks) + piece, bf16),
        in_specs=[
            pl.BlockSpec(memory_space=pltpu.SMEM),
            pl.BlockSpec((pieces, 1) + piece, lambda t: (0, t, 0, 0)),
        ],
        out_specs=pl.BlockSpec((places, 1) + piece, lambda t: (0, t, 0, 0)),
        compiler_params=params(),
        name="gather_sum",
    )(index, spread)


def own_rows_kernel(flip_ref, place_ref, own_ref, recv_ref, *refs):
    out_ref = refs[-1]
    out_ref[:, 0] = jnp.swapaxes(own_ref[...] + recv_ref[...].astype(f32), 0, 1)


def own_rows(place, flip, task, own, recv, out):
    lags, rows, cols = own.shape
    step = 64
    extra = [] if out is None else [out]
    piece = pl.BlockSpec((lags, step, cols), lambda s, flip, place: (0, s, 0))
    return pl.pallas_call(
        own_rows_kernel,
        out_shape=jax.ShapeDtypeStruct((rows, ROUNDS, lags, cols), f32),
        grid_spec=pltpu.PrefetchScalarGridSpec(
            num_scalar_prefetch=2,
            grid=(rows // step,),
            in_specs=[piece, piece] + [pl.BlockSpec(memory_space=pl.ANY)] * len(extra),
            out_specs=pl.BlockSpec(
                (step, 1, lags, cols),
                lambda s, flip, place: (s, 2 * task + flip[task, place[2]], 0, 0),
            ),
        ),
        input_output_aliases={4: 0} if extra else {},
        compiler_params=params(),
        cost_estimate=pl.CostEstimate(flops=0, bytes_accessed=5_000_000, transcendentals=0),
        name="own_rows",
    )(flip, place, own, recv, *extra)


def last_rows_kernel(flip_ref, place_ref, own_ref, recv_ref, near_ref, far_ref, in_ref, out_ref):
    step = pl.program_id(0)

    @pl.when(step == 0)
    def _():
        out_ref[:, 0] = jnp.swapaxes(own_ref[...] + recv_ref[...].astype(f32), 0, 1)

    @pl.when(step > 0)
    def _():
        core = place_ref[0]
        near = near_ref[:, 0].astype(f32)
        far = far_ref[:, 0].astype(f32)
        first = jnp.where(core == 0, near, far)
        second = jnp.where(core == 0, far, near)
        lanes = first.shape[2]
        lane = lax.broadcasted_iota(jnp.int32, first.shape, 2)
        quarter = lanes // 2
        low = jnp.where(lane < quarter, first, pltpu.roll(second, quarter, 2))
        high = jnp.where(lane < quarter, pltpu.roll(first, quarter, 2), second)
        out_ref[:, 0, :, :lanes] = jnp.swapaxes(low, 0, 1)
        out_ref[:, 0, :, lanes:] = jnp.swapaxes(high, 0, 1)


def last_rows(place, flip, own, recv, near, far, out):
    rows, _, lags, cols = out.shape
    tasks = near.shape[1]
    whole = pl.BlockSpec((lags, rows, cols), lambda s, flip, place: (0, 0, 0))
    back = pl.BlockSpec(
        (lags, 1, rows, near.shape[3]),
        lambda s, flip, place: (0, jnp.maximum(s - 1, 0), 0, 0),
    )

    def target(s, flip, place):
        task = jnp.maximum(s - 1, 0)
        block = place[2]
        mirrored = 2 * task + 1 - flip[task, block]
        return (0, jnp.where(s == 0, 2 * (tasks - 1) + flip[tasks - 1, block], mirrored), 0, 0)

    return pl.pallas_call(
        last_rows_kernel,
        out_shape=jax.ShapeDtypeStruct(out.shape, f32),
        grid_spec=pltpu.PrefetchScalarGridSpec(
            num_scalar_prefetch=2,
            grid=(tasks + 1,),
            in_specs=[whole, whole, back, back, pl.BlockSpec(memory_space=pl.ANY)],
            out_specs=pl.BlockSpec((rows, 1, lags, cols), target),
        ),
        input_output_aliases={6: 0},
        compiler_params=params(),
        name="last_rows",
    )(flip, place, own, recv, near, far, out)


def exchange(array):
    return lax.all_to_all(array, "pair", split_axis=0, concat_axis=0, tiled=True)


def after(array, *others):
    return lax.optimization_barrier((array,) + others)[0]


def local(spectra, channel_order, partners):
    num_bins, _, num_windows, cols = spectra.shape
    win_count = lax.axis_size("win")
    win = lax.axis_index("win")
    place = jnp.stack([win % 2, win // 2, lax.axis_index("pair")]).astype(jnp.int32)
    other_core = [(i, i ^ 1) for i in range(win_count)]
    other_chip = [(i, i ^ 2) for i in range(win_count)]
    norm = 1.0 / math.sqrt(num_windows * win_count * num_bins)
    tasks = ROUNDS // 2
    num_blocks = lax.axis_size("pair")

    own = whiten(spectra, channel_order).reshape(num_bins, 2 * num_windows, cols)
    shares = exchange(own)
    arranged, back_of, flip = gather(shares, partners)
    mates = [exchange(block) for block in arranged]
    own_turned = turn(after(own, mates[0]))
    groups = [
        [(block * 2 + chip_index) * 2 + core_index for chip_index in range(2) for block in range(num_blocks)]
        for core_index in range(2)
    ]
    rows, moved, pieces = [], [], None
    for task in range(tasks):
        keep, send = correlate(own_turned, mates[task], place, norm, LAGS + 1)
        recv = lax.ppermute(after(send, *moved), "win", other_core)
        own_sum, row_send, pieces = core_sum(place, keep, recv, task, tasks, pieces)
        if task + 1 < tasks:
            mates[task + 1] = after(mates[task + 1], row_send)
        if task + 1 < tasks:
            rows.append((own_sum, lax.ppermute(row_send, "win", other_chip)))
            moved = [rows[task][1]]
    out = own_rows(place, flip, 0, *rows[0], None)
    spread = lax.all_to_all(
        pieces, ("pair", "win"), 0, 0, tiled=True, axis_index_groups=groups
    )
    row_recv = lax.ppermute(row_send, "win", other_chip)
    returned = exchange(gather_sum(back_of, spread))
    far = lax.ppermute(after(returned[LAGS:], out), "win", other_core)
    return last_rows(place, flip, own_sum, row_recv, returned, far, out)[None]


def solution(mesh):
    return jax.shard_map(
        local,
        mesh=mesh,
        in_specs=(P(None, None, "win", "pair"), P("pair", None), P()),
        out_specs=P("pair", "win", None, None, None),
        check_vma=False,
    )
```

```python
import functools
import math

import jax
import jax.numpy as jnp
from jax import lax
from jax.experimental import pallas as pl
from jax.experimental.pallas import tpu as pltpu
from jax.sharding import PartitionSpec as P

LAGS = 16
ROUNDS = 4
VMEM_BYTES = 63 * 1024 * 1024
QUARTER_ORDER = (0, 2, 1, 3)
bf16 = jnp.bfloat16
f32 = jnp.float32


def params(**more):
    return pltpu.CompilerParams(vmem_limit_bytes=VMEM_BYTES, **more)


def whiten_kernel(order_ref, spectra_ref, out_ref):
    num_bins, _, rows, cols = spectra_ref.shape
    slots = lax.broadcasted_iota(jnp.int32, (cols, cols), 0)
    pick = (slots == order_ref[...]).astype(f32).astype(bf16)
    values = spectra_ref[...].astype(f32)
    power = values[:, 0] * values[:, 0] + values[:, 1] * values[:, 1]
    parts = []
    for f in range(num_bins):
        lo, hi = max(f - 2, 0), min(f + 2, num_bins - 1)
        total = power[lo]
        for g in range(lo + 1, hi + 1):
            total = total + power[g]
        inv_scale = jnp.minimum(lax.rsqrt(total * (1.0 / (hi - lo + 1))), 2.0)
        parts.append((values[f] * inv_scale[None]).astype(bf16).reshape(2 * rows, cols))
    flat = jnp.concatenate(parts, 0)
    ordered = jnp.dot(flat, pick, preferred_element_type=f32).astype(bf16)
    out_ref[...] = ordered.reshape(num_bins, 2, rows, cols)


def whiten(spectra, channel_order):
    num_bins, _, num_windows, cols = spectra.shape
    rows = 48
    return pl.pallas_call(
        whiten_kernel,
        grid=(num_windows // rows,),
        out_shape=jax.ShapeDtypeStruct(spectra.shape, bf16),
        in_specs=[
            pl.BlockSpec((1, cols), lambda s: (0, 0)),
            pl.BlockSpec((num_bins, 2, rows, cols), lambda s: (0, 0, s, 0)),
        ],
        out_specs=pl.BlockSpec((num_bins, 2, rows, cols), lambda s: (0, 0, s, 0)),
        compiler_params=params(),
        name="whiten",
    )(channel_order, spectra)


def turn_kernel(own_ref, out_ref):
    bins, _, cols = own_ref.shape
    quarter = cols // 4
    for f in range(bins):
        turned = own_ref[f].astype(f32).T.astype(bf16)
        for place, source in enumerate(QUARTER_ORDER):
            out_ref[f, place * quarter : (place + 1) * quarter, :] = turned[
                source * quarter : (source + 1) * quarter
            ]


def turn(own_rows):
    num_bins, depth, cols = own_rows.shape
    bins = 8
    return pl.pallas_call(
        turn_kernel,
        grid=(num_bins // bins,),
        out_shape=jax.ShapeDtypeStruct((num_bins, cols, depth), bf16),
        in_specs=[pl.BlockSpec((bins, depth, cols), lambda s: (s, 0, 0))],
        out_specs=pl.BlockSpec((bins, cols, depth), lambda s: (s, 0, 0)),
        compiler_params=params(),
        cost_estimate=pl.CostEstimate(flops=0, bytes_accessed=12_000_000, transcendentals=0),
        name="turn",
    )(own_rows)


def plan_task(task, partners_ref, mate_ref, back_ref, flip_ref):
    blocks = partners_ref.shape[1]
    first, second = 2 * task, 2 * task + 1
    for block in range(blocks):
        flip_ref[task, block] = -1

    def walk(block):
        partner = partners_ref[first, block]
        following = partners_ref[second, partner]
        flip_ref[task, block] = 0
        flip_ref[task, partner] = 1
        mate_ref[task, block] = partner
        back_ref[task, partner] = block
        mate_ref[task, partner] = following
        back_ref[task, following] = partner
        return following

    def start(block, carry):
        lax.while_loop(lambda block: flip_ref[task, block] < 0, walk, block)
        return carry

    lax.fori_loop(0, blocks, start, 0)


def gather_kernel(partners_ref, source_ref, *refs):
    *out_refs, mate_ref, back_ref, flip_ref, source, arranged, in_sem, sems = refs
    arrival = pltpu.make_async_copy(source_ref, source, in_sem.at[0])
    arrival.start()
    places = source.shape[0]
    chunks = sems.shape[1]
    step = places // chunks
    copies = []
    for task, out_ref in enumerate(out_refs):
        plan_task(task, partners_ref, mate_ref, back_ref, flip_ref)
        if task == 0:
            arrival.wait()
        for chunk in range(chunks):

            def body(place, carry):
                arranged[task, place] = source[mate_ref[task, place]]
                return carry

            lax.fori_loop(chunk * step, (chunk + 1) * step, body, 0)
            where = pl.ds(chunk * step, step)
            copy = pltpu.make_async_copy(
                arranged.at[task, where], out_ref.at[where], sems.at[task, chunk]
            )
            copy.start()
            copies.append(copy)
    for copy in copies:
        copy.wait()


def gather(source, partners):
    rounds, blocks = partners.shape
    tasks = rounds // 2
    anywhere = pl.BlockSpec(memory_space=pl.ANY)
    smem = pl.BlockSpec(memory_space=pltpu.SMEM)
    table = jax.ShapeDtypeStruct((tasks, blocks), jnp.int32)
    results = pl.pallas_call(
        gather_kernel,
        out_shape=[jax.ShapeDtypeStruct(source.shape, source.dtype)] * tasks + [table] * 3,
        in_specs=[smem, anywhere],
        out_specs=[anywhere] * tasks + [smem] * 3,
        scratch_shapes=[
            pltpu.VMEM(source.shape, source.dtype),
            pltpu.VMEM((tasks,) + source.shape, source.dtype),
            pltpu.SemaphoreType.DMA((1,)),
            pltpu.SemaphoreType.DMA((tasks, 2)),
        ],
        compiler_params=params(),
        name="gather",
    )(partners, source)
    return results[:tasks], results[tasks + 1], results[tasks + 2]


def weighted(terms):
    total = None
    for weight, value in terms:
        if abs(weight) < 1e-12:
            continue
        term = value * weight
        total = term if total is None else total + term
    return total


def odd_multiples(base, sign):
    twice = lambda f, k: 2 * math.cos(math.pi * f * k / 16)
    plus = {f: base[f] + base[16 - f] for f in range(1, 8)}
    minus = {f: base[f] - base[16 - f] for f in range(1, 8)}
    end = base[16] if base[0] is None else base[0]
    flip = -1 if base[0] is None else 1
    doubled = end + end
    first = end + base[8]
    for f in range(1, 8):
        first = first + plus[f]
    sums = [first]
    for k in (1, 2, 3):
        if k == 2:
            total = weighted([(twice(f, k), plus[f] - plus[8 - f]) for f in range(1, 4)])
            total = total + doubled - (base[8] + base[8])
        else:
            total = weighted([(twice(f, k), minus[f]) for f in range(1, 8)])
            total = total + doubled if flip > 0 else total - doubled
        sums.append(total + sums[-1] if sign > 0 else total - sums[-1])
    return sums


def lag_sums(real, imag, norm):
    cosine = lambda f, t: math.cos(math.pi * f * t / 32) * norm
    sine = lambda f, t: -math.sin(math.pi * f * t / 32) * norm
    even, odd = {}, {}
    low = {0: real(0), 16: real(16)}
    diff = {0: low[0]}
    for f in range(1, 16):
        a, b = real(f), real(32 - f)
        low[f], diff[f] = a + b, a - b
    base = {f: diff[f] * cosine(f, 1) for f in range(16)}
    base[16] = None
    even[1], even[3], even[5], even[7] = odd_multiples(base, -1)
    minus = {f: low[f] - low[16 - f] for f in range(8)}
    for t in (2, 6):
        even[t] = weighted([(cosine(f, t), minus[f]) for f in range(8)])
    plus = {f: low[f] + low[16 - f] for f in range(8)}
    plus[8] = low[8]
    even[4] = weighted([(cosine(f, 4), plus[f] - plus[8 - f]) for f in range(4)])
    sums = {f: plus[f] + plus[8 - f] for f in range(4)}
    sums[4] = plus[4]
    even[8] = weighted([(cosine(f, 8), sums[f]) for f in range(5)])
    total = sums[0]
    for f in range(1, 5):
        total = total + sums[f]
    even[0] = total * norm

    add = {16: imag(16)}
    sub = {}
    for f in range(1, 16):
        a, b = imag(f), imag(32 - f)
        add[f], sub[f] = a + b, a - b
    base = {f: add[f] * sine(f, 1) for f in range(1, 17)}
    base[0] = None
    odd[1], odd[3], odd[5], odd[7] = odd_multiples(base, 1)
    sums = {f: sub[f] + sub[16 - f] for f in range(1, 8)}
    sums[8] = sub[8]
    for t in (2, 6):
        odd[t] = weighted([(sine(f, t), sums[f]) for f in range(1, 9)])
    minus = {f: sub[f] - sub[16 - f] for f in range(1, 8)}
    odd[4] = weighted(
        [(sine(f, 4), minus[f] + minus[8 - f]) for f in range(1, 4)] + [(sine(4, 4), minus[4])]
    )
    odd[8] = weighted([(sine(f, 8), minus[f] - minus[8 - f]) for f in range(1, 4)])
    return even, odd


def correlate_kernel(
    norm, place_ref, own_ref, mate_ref, keep_ref, send_ref, own, mate, cross, own_sems, mate_sems
):
    num_bins, slots, _ = own.shape
    chunks = own_sems.shape[0]
    bins = num_bins // chunks
    copies = []
    for chunk in range(chunks):
        where = pl.ds(chunk * bins, bins)
        pair = (
            pltpu.make_async_copy(own_ref.at[where], own.at[where], own_sems.at[chunk]),
            pltpu.make_async_copy(mate_ref.at[where], mate.at[where], mate_sems.at[chunk]),
        )
        for copy in pair:
            copy.start()
        copies.append(pair)
    for chunk in range(chunks):
        for copy in copies[chunk]:
            copy.wait()
        for f in range(chunk * bins, (chunk + 1) * bins):
            left, right = own[f], mate[f]
            half = right.shape[0] // 2
            turned = jnp.concatenate([right[half:], -right[:half]], 0)
            cross[f, :slots] = jnp.dot(left, right, preferred_element_type=f32)
            cross[f, slots:] = jnp.dot(left, turned, preferred_element_type=f32)

    lags, half, cols = keep_ref.shape
    core = place_ref[0]
    rows, lanes = 16, 128

    def part(out_ref, base):
        def body(chunk, carry):
            row = pl.multiple_of(chunk * rows, rows)
            where = pl.ds(pl.multiple_of(base + row, rows), rows)
            turned = pl.ds(pl.multiple_of(slots + base + row, rows), rows)
            for lane in range(0, cols, lanes):
                even, odd = lag_sums(
                    lambda f: cross[f, where, lane : lane + lanes],
                    lambda f: cross[f, turned, lane : lane + lanes],
                    norm,
                )
                for lag in range(lags):
                    t = lag - LAGS // 2
                    if t == 0:
                        value = even[0]
                    elif t > 0:
                        value = even[t] + odd[t]
                    else:
                        value = even[-t] - odd[-t]
                    out_ref[lag, pl.ds(row, rows), lane : lane + lanes] = value.astype(
                        out_ref.dtype
                    )
            return carry

        lax.fori_loop(0, half // rows, body, 0)

    part(keep_ref, core * half)
    part(send_ref, (1 - core) * half)


def correlate(own, mate, place, norm, lags):
    num_bins, slots, depth = own.shape
    cols = mate.shape[2]
    chunks = 8
    anywhere = pl.BlockSpec(memory_space=pl.ANY)
    vmem = pl.BlockSpec(memory_space=pltpu.VMEM)
    return pl.pallas_call(
        functools.partial(correlate_kernel, norm),
        out_shape=[
            jax.ShapeDtypeStruct((lags, slots // 2, cols), f32),
            jax.ShapeDtypeStruct((lags, slots // 2, cols), bf16),
        ],
        in_specs=[pl.BlockSpec(memory_space=pltpu.SMEM), anywhere, anywhere],
        out_specs=[vmem, vmem],
        scratch_shapes=[
            pltpu.VMEM(own.shape, bf16),
            pltpu.VMEM(mate.shape, bf16),
            pltpu.VMEM((num_bins, 2 * slots, cols), f32),
            pltpu.SemaphoreType.DMA((chunks,)),
            pltpu.SemaphoreType.DMA((chunks,)),
        ],
        compiler_params=params(),
        cost_estimate=pl.CostEstimate(
            flops=4 * num_bins * slots * depth * cols, bytes_accessed=20_000_000, transcendentals=0
        ),
        name="correlate",
    )(place, own, mate)


def core_sum_kernel(task, place_ref, keep_ref, recv_ref, *refs):
    own_ref, send_ref, piece_ref, keep, recv, own, send, piece, in_sems, out_sems, piece_sems = refs[-11:]
    core, chip = place_ref[0], place_ref[1]
    lags, rows, cols = own.shape
    own_rows = pl.ds(pl.multiple_of(chip * rows, rows), rows)
    other_rows = pl.ds(pl.multiple_of((1 - chip) * rows, rows), rows)
    chunks = in_sems.shape[1]
    step = lags // chunks
    bounds = [0] + [chunk * step + 1 for chunk in range(1, chunks)] + [lags + 1]
    arrivals, departures = [], []
    for chunk in range(chunks):
        where = pl.ds(bounds[chunk], bounds[chunk + 1] - bounds[chunk])
        pair = (
            pltpu.make_async_copy(keep_ref.at[where], keep.at[where], in_sems.at[0, chunk]),
            pltpu.make_async_copy(recv_ref.at[where], recv.at[where], in_sems.at[1, chunk]),
        )
        for copy in pair:
            copy.start()
        arrivals.append(pair)

    def leave(source, target, sem):
        copy = pltpu.make_async_copy(source, target, sem)
        copy.start()
        departures.append(copy)

    for chunk in range(chunks):
        for copy in arrivals[chunk]:
            copy.wait()
        first, last = bounds[chunk], bounds[chunk + 1]
        for lag in range(first, min(last, lags)):
            own[lag] = keep[lag, own_rows, :] + recv[lag, own_rows, :].astype(f32)
            send[lag] = (keep[lag, other_rows, :] + recv[lag, other_rows, :].astype(f32)).astype(
                bf16
            )
        for lag in range(max(first, 1), last):
            back = lags - lag
            turned = (keep[lag] + recv[lag].astype(f32)).T
            for half in range(2):
                low = turned[2 * half * rows : (2 * half + 1) * rows]
                high = turned[(2 * half + 1) * rows : (2 * half + 2) * rows]
                base = 2 * half * lags + back
                piece[base] = jnp.where(core == 0, low, high).astype(bf16)
                piece[base + lags] = jnp.where(core == 0, high, low).astype(bf16)
        where = pl.ds(first, min(last, lags) - first)
        leave(own.at[where], own_ref.at[where], out_sems.at[0, chunk])
        leave(send.at[where], send_ref.at[where], out_sems.at[1, chunk])
        for group in range(4):
            where = pl.ds(group * lags + lags - last + 1, step)
            leave(piece.at[where], piece_ref.at[where, task], piece_sems.at[group, chunk])
    for copy in departures:
        copy.wait()


def core_sum(place, keep, recv, task, tasks, pieces):
    lags, rows, cols = keep.shape
    anywhere = pl.BlockSpec(memory_space=pl.ANY)
    count = 4 * (lags - 1)
    part = (lags - 1, rows // 2, cols)
    piece = (cols // 4, rows)
    extra = [] if pieces is None else [pieces]
    return pl.pallas_call(
        functools.partial(core_sum_kernel, task),
        out_shape=[
            jax.ShapeDtypeStruct(part, f32),
            jax.ShapeDtypeStruct(part, bf16),
            jax.ShapeDtypeStruct((count, tasks) + piece, bf16),
        ],
        in_specs=[pl.BlockSpec(memory_space=pltpu.SMEM)] + [anywhere] * (2 + len(extra)),
        out_specs=[anywhere] * 3,
        scratch_shapes=[
            pltpu.VMEM(keep.shape, f32),
            pltpu.VMEM(keep.shape, bf16),
            pltpu.VMEM(part, f32),
            pltpu.VMEM(part, bf16),
            pltpu.VMEM((count,) + piece, bf16),
            pltpu.SemaphoreType.DMA((2, 2)),
            pltpu.SemaphoreType.DMA((2, 2)),
            pltpu.SemaphoreType.DMA((4, 2)),
        ],
        input_output_aliases={3: 2} if extra else {},
        compiler_params=params(),
        cost_estimate=pl.CostEstimate(flops=0, bytes_accessed=12_000_000, transcendentals=0),
        name="core_sum",
    )(place, keep, recv, *extra)


def gather_sum_kernel(index_ref, spread_ref, out_ref):
    places = out_ref.shape[0]
    task = pl.program_id(0)

    def body(place, carry):
        source = index_ref[task, place]
        out_ref[place, 0] = (
            spread_ref[source, 0].astype(f32) + spread_ref[places + source, 0].astype(f32)
        ).astype(bf16)
        return carry

    lax.fori_loop(0, places, body, 0, unroll=8)


def gather_sum(index, spread):
    tasks, places = index.shape
    pieces, piece = spread.shape[0], spread.shape[2:]
    return pl.pallas_call(
        gather_sum_kernel,
        grid=(tasks,),
        out_shape=jax.ShapeDtypeStruct((places, tasks) + piece, bf16),
        in_specs=[
            pl.BlockSpec(memory_space=pltpu.SMEM),
            pl.BlockSpec((pieces, 1) + piece, lambda t: (0, t, 0, 0)),
        ],
        out_specs=pl.BlockSpec((places, 1) + piece, lambda t: (0, t, 0, 0)),
        compiler_params=params(),
        name="gather_sum",
    )(index, spread)


def own_rows_kernel(flip_ref, place_ref, own_ref, recv_ref, *refs):
    out_ref = refs[-1]
    out_ref[:, 0] = jnp.swapaxes(own_ref[...] + recv_ref[...].astype(f32), 0, 1)


def own_rows(place, flip, task, own, recv, out):
    lags, rows, cols = own.shape
    step = 64
    extra = [] if out is None else [out]
    piece = pl.BlockSpec((lags, step, cols), lambda s, flip, place: (0, s, 0))
    return pl.pallas_call(
        own_rows_kernel,
        out_shape=jax.ShapeDtypeStruct((rows, ROUNDS, lags, cols), f32),
        grid_spec=pltpu.PrefetchScalarGridSpec(
            num_scalar_prefetch=2,
            grid=(rows // step,),
            in_specs=[piece, piece] + [pl.BlockSpec(memory_space=pl.ANY)] * len(extra),
            out_specs=pl.BlockSpec(
                (step, 1, lags, cols),
                lambda s, flip, place: (s, 2 * task + flip[task, place[2]], 0, 0),
            ),
        ),
        input_output_aliases={4: 0} if extra else {},
        compiler_params=params(),
        cost_estimate=pl.CostEstimate(flops=0, bytes_accessed=5_000_000, transcendentals=0),
        name="own_rows",
    )(flip, place, own, recv, *extra)


def last_rows_kernel(flip_ref, place_ref, own_ref, recv_ref, near_ref, far_ref, in_ref, out_ref):
    step = pl.program_id(0)

    @pl.when(step == 0)
    def _():
        out_ref[:, 0] = jnp.swapaxes(own_ref[...] + recv_ref[...].astype(f32), 0, 1)

    @pl.when(step > 0)
    def _():
        core = place_ref[0]
        near = near_ref[:, 0].astype(f32)
        far = far_ref[:, 0].astype(f32)
        first = jnp.where(core == 0, near, far)
        second = jnp.where(core == 0, far, near)
        lanes = first.shape[2]
        lane = lax.broadcasted_iota(jnp.int32, first.shape, 2)
        quarter = lanes // 2
        low = jnp.where(lane < quarter, first, pltpu.roll(second, quarter, 2))
        high = jnp.where(lane < quarter, pltpu.roll(first, quarter, 2), second)
        out_ref[:, 0, :, :lanes] = jnp.swapaxes(low, 0, 1)
        out_ref[:, 0, :, lanes:] = jnp.swapaxes(high, 0, 1)


def last_rows(place, flip, own, recv, near, far, out):
    rows, _, lags, cols = out.shape
    tasks = near.shape[1]
    whole = pl.BlockSpec((lags, rows, cols), lambda s, flip, place: (0, 0, 0))
    back = pl.BlockSpec(
        (lags, 1, rows, near.shape[3]),
        lambda s, flip, place: (0, jnp.maximum(s - 1, 0), 0, 0),
    )

    def target(s, flip, place):
        task = jnp.maximum(s - 1, 0)
        block = place[2]
        mirrored = 2 * task + 1 - flip[task, block]
        return (0, jnp.where(s == 0, 2 * (tasks - 1) + flip[tasks - 1, block], mirrored), 0, 0)

    return pl.pallas_call(
        last_rows_kernel,
        out_shape=jax.ShapeDtypeStruct(out.shape, f32),
        grid_spec=pltpu.PrefetchScalarGridSpec(
            num_scalar_prefetch=2,
            grid=(tasks + 1,),
            in_specs=[whole, whole, back, back, pl.BlockSpec(memory_space=pl.ANY)],
            out_specs=pl.BlockSpec((rows, 1, lags, cols), target),
        ),
        input_output_aliases={6: 0},
        compiler_params=params(),
        name="last_rows",
    )(flip, place, own, recv, near, far, out)


def exchange(array):
    return lax.all_to_all(array, "pair", split_axis=0, concat_axis=0, tiled=True)


def after(array, *others):
    return lax.optimization_barrier((array,) + others)[0]


def local(spectra, channel_order, partners):
    num_bins, _, num_windows, cols = spectra.shape
    win_count = lax.axis_size("win")
    win = lax.axis_index("win")
    place = jnp.stack([win % 2, win // 2, lax.axis_index("pair")]).astype(jnp.int32)
    other_core = [(i, i ^ 1) for i in range(win_count)]
    other_chip = [(i, i ^ 2) for i in range(win_count)]
    norm = 1.0 / math.sqrt(num_windows * win_count * num_bins)
    tasks = ROUNDS // 2
    num_blocks = lax.axis_size("pair")

    own = whiten(spectra, channel_order).reshape(num_bins, 2 * num_windows, cols)
    shares = exchange(own)
    arranged, back_of, flip = gather(shares, partners)
    mates = [exchange(block) for block in arranged]
    own_turned = turn(after(own, mates[0]))
    groups = [
        [(block * 2 + chip_index) * 2 + core_index for chip_index in range(2) for block in range(num_blocks)]
        for core_index in range(2)
    ]
    rows, moved, pieces = [], [], None
    for task in range(tasks):
        keep, send = correlate(own_turned, mates[task], place, norm, LAGS + 1)
        recv = lax.ppermute(after(send, *moved), "win", other_core)
        own_sum, row_send, pieces = core_sum(place, keep, recv, task, tasks, pieces)
        if task + 1 < tasks:
            mates[task + 1] = after(mates[task + 1], row_send)
        if task + 1 < tasks:
            rows.append((own_sum, lax.ppermute(row_send, "win", other_chip)))
            moved = [rows[task][1]]
    out = own_rows(place, flip, 0, *rows[0], None)
    spread = lax.all_to_all(
        after(pieces, out), ("pair", "win"), 0, 0, tiled=True, axis_index_groups=groups
    )
    row_recv = lax.ppermute(row_send, "win", other_chip)
    returned = exchange(gather_sum(back_of, spread))
    far = lax.ppermute(returned[LAGS:], "win", other_core)
    return last_rows(place, flip, own_sum, row_recv, returned, far, out)[None]


def solution(mesh):
    return jax.shard_map(
        local,
        mesh=mesh,
        in_specs=(P(None, None, "win", "pair"), P("pair", None), P()),
        out_specs=P("pair", "win", None, None, None),
        check_vma=False,
    )
```
